256 devices in a mesh: section: 4 (over y), tile: 64 (over z, x, core).
Axes of the slice: x: 4, y: 4, z: 8, core: 2. Of those that a mesh axis runs over, the one named last changes fastest.
Arguments:
- acts: bfloat16 [4, 320, 192, 128], P('section', 'tile'), may hold values from -6 to 6
- cot_top: bfloat16 [320, 192, 128], P('tile'), may hold values from -6 to 6
- land: int32 [320], P('tile'), may hold values from 0 to 1, as said below
- owners: int32 [192], P('tile'), may hold values from 0 to 319, as said below
- dw_kernel: float32 [4, 49, 192], P('section'), may hold values from -0.875 to 0.875
- ln_gain: float32 [4, 192], P('section'), may hold values from 0.5 to 1.5
- w_up: bfloat16 [4, 192, 768], P('section'), may hold values from -0.4375 to 0.4375
- b_up: float32 [4, 768], P('section'), may hold values from -1 to 1
- w_down: bfloat16 [4, 192, 768], P('section'), may hold values from -0.21875 to 0.21875
- layer_scale: float32 [4, 192], P('section'), may hold values from 0.5 to 1.5
Outputs:
- d_input: bfloat16 [4, 192, 192, 128], P('section', 'tile')
- grad_kernel: float32 [4, 49, 192], P('section')
- grad_gain: float32 [4, 192], P('section')
- grad_up: float32 [4, 192, 768], P('section')
- grad_bias: float32 [4, 768], P('section')
- grad_down: float32 [4, 192, 768], P('section')
- grad_scale: float32 [4, 192], P('section')
The draws below stay inside these ranges and needn't reach their ends.
Inputs may be any that keep to these rules, and one draw needn't show every extreme that they name: `land`: 192 of the 320 tiles are wet; each device's 5 tiles hold between 1 and 5 wet ones. `owners`: the wet tiles in ascending order, 3 to a device; each is listed on its own device or on the next one along tile; at most 2 tiles of one device are listed on the next, and some device hands exactly 2.
All inputs are finite; a program needn't handle non-finite values.
Results may differ from the reference program's by a relative error of at most 0.02.
Values may be sent and summed in bfloat16 or wider, within the bound.
No kernel may reach another device: no remote copies, remote signals or barrier semaphores. Data moves between devices by JAX's collectives and lax.ppermute only.
A program may use at most 128 MiB of HBM per device.

```python
import math
import jax
import jax.numpy as jnp
from jax import lax

C = 192
F = 768
KS = 7
TPD = 5
K = 3
CAP = 2
TH = 1
W = 128
NTILES = 320
SLOTS = 192
ROWS = 320
CELLS = 40960
N_SECTION = 4


def wet_layout(key):
    devices = NTILES // TPD
    key_carry, key_pick, key_place = jax.random.split(key, 3)
    carried = jax.random.randint(key_carry, (devices + 1,), 0, CAP + 1)
    place = jnp.arange(devices + 1)
    picked = jax.random.randint(key_pick, (), 1, devices)
    carried = jnp.where(place == picked, CAP, carried)
    carried = jnp.where((place == 0) | (place == devices), 0, carried)
    counts = K + carried[1:] - carried[:-1]
    scores = jax.random.randint(key_place, (devices, TPD), 0, 1048576) * TPD + jnp.arange(TPD)[None, :]
    ranks = jnp.argsort(jnp.argsort(scores, axis=1), axis=1)
    wetness = (ranks < counts[:, None]).astype(jnp.int32).reshape(-1)
    ordering = jnp.argsort(1 - wetness, stable=True)
    return (wetness, ordering[:SLOTS].astype(jnp.int32))


def draw_land(key, part):
    wetness, listing = wet_layout(key)
    return wetness


def draw_owners(key, part):
    wetness, listing = wet_layout(key)
    return listing


def block_scale(rng, shape, pieces, low, high):
    level = 1.0
    for position, blocks in pieces:
        draws = jax.random.uniform(jax.random.fold_in(jax.random.fold_in(rng, 6), position), (blocks,), jnp.float32, low / len(pieces), high / len(pieces))
        level = level * jnp.repeat(jnp.exp(draws), shape[position] // blocks).reshape((-1,) + (1,) * (len(shape) - 1 - position))
    return level


def noise(own_key, shape, scale, limit, shards=(), held_as=jnp.bfloat16):
    level = block_scale(own_key, shape, shards, -0.22, 0.18) if shards else 1.0
    values = jax.random.normal(own_key, shape, jnp.float32) * scale * level
    return jnp.minimum(jnp.maximum(values, -limit), limit).astype(held_as)


def setup_inputs(seed: int = 0) -> dict:
    splits = jax.random.split(jax.random.key(seed), 11)
    return {
        "acts": noise(splits[0], (N_SECTION, ROWS, C, W), 1.0, 6.0, ((0, 4), (1, 64))),
        "cot_top": noise(splits[1], (ROWS, C, W), 1.0, 6.0, ((0, 64),)),
        "land": draw_land(jax.random.fold_in(splits[10], 71), 0),
        "owners": draw_owners(jax.random.fold_in(splits[10], 71), 0),
        "dw_kernel": noise(splits[4], (N_SECTION, KS * KS, C), (KS * KS) ** -0.5, 0.875, ((0, 4),), jnp.float32),
        "ln_gain": jnp.clip(0.5 + 1.0 * jax.random.uniform(splits[5], (N_SECTION, C), jnp.float32) ** block_scale(splits[5], (N_SECTION, C), ((0, 4),), -0.2, 0.2), 0.5, 1.5),
        "w_up": noise(splits[6], (N_SECTION, C, F), C ** -0.5, 0.4375, ((0, 4),)),
        "b_up": jnp.clip(jax.random.uniform(splits[7], (N_SECTION, F), jnp.float32, -1.0, 1.0) * block_scale(splits[7], (N_SECTION, F), ((0, 4),), -0.4, 0.0), -1.0, 1.0),
        "w_down": noise(splits[8], (N_SECTION, C, F), F ** -0.5, 0.21875, ((0, 4),)),
        "layer_scale": jnp.clip(0.5 + 1.0 * jax.random.uniform(splits[9], (N_SECTION, C), jnp.float32) ** block_scale(splits[9], (N_SECTION, C), ((0, 4),), -0.2, 0.2), 0.5, 1.5),
    }


norm_eps = 1e-06
tanh_root = math.sqrt(2.0 / math.pi)
cubic_coef = 0.044715

def extend_cols(source, margin):
    return jnp.concatenate([source[..., -margin:], source, source[..., :margin]], axis=-1)

def depthwise(padded, kernel, row_count, col_count):
    running = jnp.zeros((row_count, padded.shape[1], col_count), jnp.float32)
    for tap_row in range(KS):
        for tap_col in range(KS):
            weight_col = kernel[tap_row * KS + tap_col][:, None]
            running = running + weight_col * padded[tap_row:tap_row + row_count, :, tap_col:tap_col + col_count].astype(jnp.float32)
    return running

def transpose_conv(padded, kernel, row_count, col_count):
    running = jnp.zeros((row_count, padded.shape[1], col_count), jnp.float32)
    for tap_row in range(KS):
        for tap_col in range(KS):
            weight_col = kernel[tap_row * KS + tap_col][:, None]
            first_row = KS - 1 - tap_row
            first_col = KS - 1 - tap_col
            running = running + weight_col * padded[first_row:first_row + row_count, :, first_col:first_col + col_count].astype(jnp.float32)
    return running

def kernel_taps(fieldlow, padded, row_count, col_count):
    grads = []
    source = fieldlow.astype(jnp.float32)
    for tap_row in range(KS):
        for tap_col in range(KS):
            window = padded[tap_row:tap_row + row_count, :, tap_col:tap_col + col_count].astype(jnp.float32)
            grads.append(lax.optimization_barrier(jnp.sum(source * window, axis=(0, 2))))
    return jnp.stack(grads)

def normalize(source):
    center = source - lax.optimization_barrier(jnp.mean(source, axis=1, keepdims=True))
    inverse = lax_rsqrt(lax.optimization_barrier(jnp.mean(center * center, axis=1, keepdims=True)) + norm_eps)
    return (center * inverse, inverse)

def lax_rsqrt(source):
    return 1.0 / jnp.sqrt(source)

def gelu_parts(preact):
    inner = tanh_root * (preact + cubic_coef * preact * preact * preact)
    hyper = jnp.tanh(inner)
    value = 0.5 * preact * (1.0 + hyper)
    slope = 0.5 * (1.0 + hyper) + 0.5 * preact * (1.0 - hyper * hyper) * tanh_root * (1.0 + 3.0 * cubic_coef * preact * preact)
    return (value, slope)

def reference(acts, cot_top, land, owners, dw_kernel, ln_gain, w_up, b_up, w_down, layer_scale):
    row_count = acts.shape[1]
    chan_count = acts.shape[2]
    col_count = acts.shape[3]
    wet = jnp.repeat(land.astype(jnp.float32), TH)[:, None, None]
    scale = 1.0 / math.sqrt(CELLS)
    cotangent = cot_top
    results = {}
    for section in range(N_SECTION - 1, -1, -1):
        kernel = dw_kernel[section]
        gain = ln_gain[section][:, None]
        up_f = w_up[section].astype(jnp.float32)
        down_f = w_down[section].astype(jnp.float32)
        padded = extend_cols(jnp.pad(acts[section], ((3, 3), (0, 0), (0, 0))), 3)
        field = depthwise(padded, kernel, row_count, col_count)
        nhat, inverse = normalize(field)
        normed = (nhat * gain).astype(jnp.bfloat16)
        preact = jnp.einsum('rcw,cf->rfw', normed.astype(jnp.float32), up_f) + b_up[section][:, None]
        value, slope = gelu_parts(preact)
        hidden = value.astype(jnp.bfloat16)
        branch = jnp.einsum('rfw,cf->rcw', hidden.astype(jnp.float32), down_f)
        cot_f = cotangent.astype(jnp.float32)
        outgrad = (cot_f * layer_scale[section][:, None] * wet).astype(jnp.bfloat16)
        pregrad = jnp.einsum('rcw,cf->rfw', outgrad.astype(jnp.float32), down_f) * slope
        lowgrad = pregrad.astype(jnp.bfloat16)
        featgrad = jnp.einsum('rfw,cf->rcw', lowgrad.astype(jnp.float32), up_f)
        scaled = featgrad * gain
        fieldgrad = inverse * (scaled - lax.optimization_barrier(jnp.mean(scaled, axis=1, keepdims=True)) - nhat * lax.optimization_barrier(jnp.mean(scaled * nhat, axis=1, keepdims=True)))
        fieldlow = fieldgrad.astype(jnp.bfloat16)
        grad_pad = extend_cols(jnp.pad(fieldlow, ((3, 3), (0, 0), (0, 0))), 3)
        inputgrad = (cot_f + transpose_conv(grad_pad, kernel, row_count, col_count)).astype(jnp.bfloat16)
        tiles = inputgrad.reshape(NTILES, TH, chan_count, col_count)
        slotted = jnp.take(tiles, owners, axis=0).reshape(SLOTS * TH, chan_count, col_count)
        results[section] = (slotted, scale * kernel_taps(fieldlow, padded, row_count, col_count), scale * lax.optimization_barrier(jnp.sum(featgrad * nhat, axis=(0, 2))), scale * jnp.einsum('rcw,rfw->cf', normed.astype(jnp.float32), lowgrad.astype(jnp.float32)), scale * lax.optimization_barrier(jnp.sum(pregrad, axis=(0, 2))), scale * jnp.einsum('rcw,rfw->cf', outgrad.astype(jnp.float32), hidden.astype(jnp.float32)), scale * lax.optimization_barrier(jnp.sum(cot_f * branch * wet, axis=(0, 2))))
        cotangent = inputgrad
    stacked = [jnp.stack([results[section][member] for section in range(N_SECTION)]) for member in range(7)]
    return (stacked[0], stacked[1], stacked[2], stacked[3], stacked[4], stacked[5], stacked[6])
```

```python
import math

import jax
import jax.numpy as jnp
from jax import lax
from jax.sharding import PartitionSpec as P

KS = 7
CAP = 2


norm_eps = 1e-06
tanh_root = math.sqrt(2.0 / math.pi)
cubic_coef = 0.044715


def padded_2(cells, sides, width):
    for axis, dim in sides:
        count = lax.axis_size(axis)
        ends = count - 1
        head = lax.slice_in_dim(cells, 0, width, axis=dim)
        tail = lax.slice_in_dim(cells, cells.shape[dim] - width, cells.shape[dim], axis=dim)
        cells = jnp.concatenate(
            [
                lax.ppermute(tail, axis, [(i, (i + 1) % count) for i in range(ends)]),
                cells,
                lax.ppermute(head, axis, [((i + 1) % count, i) for i in range(ends)]),
            ],
            axis=dim,
        )
    return cells


def shifted(value, axis, steps):
    count = lax.axis_size(axis)
    initial, last = (max(0, -steps), min(count, count - steps))
    return lax.ppermute(value, axis, [(source, source + steps) for source in range(initial, last)])


def extend_cols(source, margin):
    return jnp.concatenate([source[..., -margin:], source, source[..., :margin]], axis=-1)


def depthwise(padded, kernel, row_count, col_count):
    running = jnp.zeros((row_count, padded.shape[1], col_count), jnp.float32)
    for tap_row in range(KS):
        for tap_col in range(KS):
            weight_col = kernel[tap_row * KS + tap_col][:, None]
            running = running + weight_col * padded[
                tap_row : tap_row + row_count, :, tap_col : tap_col + col_count
            ].astype(jnp.float32)
    return running


def transpose_conv(padded, kernel, row_count, col_count):
    running = jnp.zeros((row_count, padded.shape[1], col_count), jnp.float32)
    for tap_row in range(KS):
        for tap_col in range(KS):
            weight_col = kernel[tap_row * KS + tap_col][:, None]
            first_row = KS - 1 - tap_row
            first_col = KS - 1 - tap_col
            running = running + weight_col * padded[
                first_row : first_row + row_count, :, first_col : first_col + col_count
            ].astype(jnp.float32)
    return running


def kernel_taps(fieldlow, padded, row_count, col_count):
    grads = []
    source = fieldlow.astype(jnp.float32)
    for tap_row in range(KS):
        for tap_col in range(KS):
            window = padded[tap_row : tap_row + row_count, :, tap_col : tap_col + col_count].astype(
                jnp.float32
            )
            grads.append(jnp.sum(source * window, axis=(0, 2)))
    return jnp.stack(grads)


def normalize(source):
    center = source - jnp.mean(source, axis=1, keepdims=True)
    inverse = 1.0 / jnp.sqrt(jnp.mean(center * center, axis=1, keepdims=True) + norm_eps)
    return (center * inverse, inverse)


def gelu_parts(preact):
    inner = tanh_root * (preact + cubic_coef * preact * preact * preact)
    hyper = jnp.tanh(inner)
    value = 0.5 * preact * (1.0 + hyper)
    slope = 0.5 * (1.0 + hyper) + 0.5 * preact * (1.0 - hyper * hyper) * tanh_root * (
        1.0 + 3.0 * cubic_coef * preact * preact
    )
    return (value, slope)


def flipped(value, dims):
    pairs = []
    for tile in range(64):
        core, x, z = tile % 2, tile // 2 % 4, tile // 8
        dim = dims[core]
        if dim == "core":
            core = 1 - core
        elif dim == "x0":
            x = x ^ 1
        elif dim == "x1":
            x = 3 - x
        elif dim == "z0":
            z = z ^ 1
        elif dim == "z1":
            z = (3 - z) % 8 if z < 4 else 11 - z
        elif dim == "z2":
            z = 7 - z
        pairs.append((tile, z * 8 + x * 2 + core))
    return lax.ppermute(value, "tile", pairs)


def total(value):
    rows = value.shape[0]
    core = lax.axis_index("tile") % 2
    tile = lax.axis_index("tile")
    x, z = tile // 2 % 4, tile // 8
    half, part = rows // 2, rows // 4

    def add(first, second):
        return (first.astype(jnp.float32) + second.astype(jnp.float32)).astype(jnp.bfloat16)

    low, high = value[:half], value[half:]
    first = core == 0
    value = add(
        jnp.where(first, low, high), flipped(jnp.where(first, high, low), ("core", "core"))
    )
    low, high = value[:part], value[part:]
    first = (jnp.where(core == 0, x, z) + 1) // 2 % 2 == 0
    value = add(jnp.where(first, low, high), flipped(jnp.where(first, high, low), ("x0", "z0")))
    for dims in (("x1", "z1"), ("z0", "z2"), ("z1", "x0"), ("z2", "x1")):
        value = add(value, flipped(value, dims))
    other = flipped(value, ("x0", "z0"))
    value = jnp.concatenate([jnp.where(first, value, other), jnp.where(first, other, value)])
    other = flipped(value, ("core", "core"))
    first = core == 0
    return jnp.concatenate([jnp.where(first, value, other), jnp.where(first, other, value)])


def body(acts, cot_top, land, owners, dw_kernel, ln_gain, w_up, b_up, w_down, layer_scale):
    source = acts[0]
    kernel = dw_kernel[0]
    gain = ln_gain[0][:, None]
    up_mat = w_up[0]
    bias = b_up[0][:, None]
    down_mat = w_down[0]
    layer = layer_scale[0][:, None]
    tiles_dev = land.shape[0]
    slot_count = owners.shape[0]
    row_count, chan_count, col_count = source.shape
    tile_rows = row_count // tiles_dev
    tile_size = tile_rows * chan_count * col_count
    section_count = lax.axis_size("section")
    section_now = lax.axis_index("section")
    scale = 1.0 / math.sqrt(lax.axis_size("tile") * row_count * col_count)
    offset = lax.axis_index("tile") * tiles_dev
    local = jnp.arange(tiles_dev, dtype=jnp.int32)
    places = jnp.arange(CAP, dtype=jnp.int32)
    slot_ids = jnp.arange(slot_count, dtype=jnp.int32)
    kept_map = owners[None, :] == (offset + local)[:, None]
    kept = jnp.any(kept_map, axis=1)
    sent = (land == 1) & jnp.logical_not(kept)
    sent_int = sent.astype(jnp.int32)
    sent_rank = jnp.cumsum(sent_int) - sent_int
    send_hits = sent[None, :] & (sent_rank[None, :] == places[:, None])
    send_index = jnp.sum(send_hits.astype(jnp.int32) * local[None, :], axis=1)
    send_valid = jnp.any(send_hits, axis=1)
    own_slot = jnp.any(kept_map, axis=0)
    own_index = jnp.sum(kept_map.astype(jnp.int32) * local[:, None], axis=0)
    left_index = jnp.minimum(slot_ids, CAP - 1)
    padded = extend_cols(padded_2(source, (("tile", 0),), 3), 3)
    field = depthwise(padded, kernel, row_count, col_count)
    wet_work = jnp.repeat(land.astype(jnp.float32), tile_rows)[:, None, None]
    nhat, inverse = normalize(field)
    normed = (nhat * gain).astype(jnp.bfloat16)
    preact = jnp.einsum("rcw,cf->rfw", normed, up_mat, preferred_element_type=jnp.float32) + bias
    value, slope = gelu_parts(preact)
    hidden = value.astype(jnp.bfloat16)
    branch = jnp.einsum("rfw,cf->rcw", hidden, down_mat, preferred_element_type=jnp.float32)
    cotangent = cot_top
    for turn in range(section_count):
        active = section_now == section_count - 1 - turn
        cot_work = cotangent
        outgrad = (cot_work.astype(jnp.float32) * layer * wet_work).astype(jnp.bfloat16)
        pregrad = (
            jnp.einsum("rcw,cf->rfw", outgrad, down_mat, preferred_element_type=jnp.float32) * slope
        )
        lowgrad = pregrad.astype(jnp.bfloat16)
        bias_turn = jnp.sum(pregrad, axis=(0, 2))
        featgrad = jnp.einsum("rfw,cf->rcw", lowgrad, up_mat, preferred_element_type=jnp.float32)
        gain_turn = jnp.sum(featgrad * nhat, axis=(0, 2))
        scaled = featgrad * gain
        fieldgrad = inverse * (
            scaled
            - jnp.mean(scaled, axis=1, keepdims=True)
            - nhat * jnp.mean(scaled * nhat, axis=1, keepdims=True)
        )
        fieldlow = fieldgrad.astype(jnp.bfloat16)
        grad_pad = extend_cols(padded_2(fieldlow, (("tile", 0),), 3), 3)
        inputgrad = (
            cotangent.astype(jnp.float32) + transpose_conv(grad_pad, kernel, row_count, col_count)
        ).astype(jnp.bfloat16)
        if turn == 0:
            cot_keep, out_keep, low_keep, bias_keep = (cot_work, outgrad, lowgrad, bias_turn)
            gain_keep, field_keep, input_keep = (gain_turn, fieldlow, inputgrad)
        else:
            cot_keep = jnp.where(active, cot_work, cot_keep)
            out_keep = jnp.where(active, outgrad, out_keep)
            low_keep = jnp.where(active, lowgrad, low_keep)
            bias_keep = jnp.where(active, bias_turn, bias_keep)
            gain_keep = jnp.where(active, gain_turn, gain_keep)
            field_keep = jnp.where(active, fieldlow, field_keep)
            input_keep = jnp.where(active, inputgrad, input_keep)
        if turn + 1 < section_count:
            cotangent = shifted(inputgrad, "section", -1)
    grad_down = jnp.einsum("rcw,rfw->cf", out_keep, hidden, preferred_element_type=jnp.float32)
    grad_up = jnp.einsum("rcw,rfw->cf", normed, low_keep, preferred_element_type=jnp.float32)
    grad_scale = jnp.sum(cot_keep.astype(jnp.float32) * branch * wet_work, axis=(0, 2))
    grad_kernel = kernel_taps(field_keep, padded, row_count, col_count)
    hidden_count = bias_keep.shape[0]
    small = jnp.concatenate([grad_kernel.reshape(-1), gain_keep, bias_keep, grad_scale])
    small = jnp.pad(small, (0, 32 * hidden_count - small.shape[0])).reshape(32, hidden_count)
    packed = total(jnp.concatenate([grad_up, grad_down, small]).astype(jnp.bfloat16))
    packed = packed.astype(jnp.float32)
    small = packed[2 * chan_count :].reshape(-1)
    ends = [0]
    for size in (KS * KS * chan_count, chan_count, hidden_count, chan_count):
        ends.append(ends[-1] + size)
    pieces = [small[a:b] for a, b in zip(ends[:-1], ends[1:])]
    summed = (
        pieces[0].reshape(KS * KS, chan_count),
        pieces[1],
        packed[:chan_count],
        pieces[2],
        packed[chan_count : 2 * chan_count],
        pieces[3],
    )
    flat = input_keep.reshape(tiles_dev, tile_size)
    arrived = shifted(
        jnp.take(flat, send_index, axis=0) * send_valid[:, None].astype(input_keep.dtype), "tile", 1
    )
    arrange_flat = input_keep.reshape(tiles_dev, tile_size)
    mine = jnp.take(arrange_flat, own_index, axis=0) * own_slot[:, None].astype(input_keep.dtype)
    borrowed = jnp.take(arrived, left_index, axis=0) * jnp.logical_not(own_slot)[:, None].astype(
        input_keep.dtype
    )
    slotted = (mine + borrowed).reshape(slot_count * tile_rows, chan_count, col_count)
    return (
        slotted[None],
        (scale * summed[0])[None],
        (scale * summed[1])[None],
        (scale * summed[2])[None],
        (scale * summed[3])[None],
        (scale * summed[4])[None],
        (scale * summed[5])[None],
    )


def solution(mesh):
    in_specs = (
        P("section", "tile", None, None),
        P("tile", None, None),
        P("tile"),
        P("tile"),
        P("section", None, None),
        P("section", None),
        P("section", None, None),
        P("section", None),
        P("section", None, None),
        P("section", None),
    )
    out_specs = (
        P("section", "tile", None, None),
        P("section", None, None),
        P("section", None),
        P("section", None, None),
        P("section", None),
        P("section", None, None),
        P("section", None),
    )
    return jax.shard_map(body, mesh=mesh, in_specs=in_specs, out_specs=out_specs, check_vma=False)
```

```python
import functools
import math

import jax
import jax.numpy as jnp
from jax import lax
from jax.experimental import pallas as pl
from jax.experimental.pallas import tpu as pltpu
from jax.sharding import PartitionSpec as P

KS = 7
CAP = 2
SECTIONS = 4
TILES = 64
MARGIN = 3
BLOCK = 16

norm_eps = 1e-06
tanh_root = math.sqrt(2.0 / math.pi)
cubic_coef = 0.044715

f32 = jnp.float32
bf16 = jnp.bfloat16

SECTION, ODD, KEEP, NEAR, MATE, FAR, OFFSET = range(7)


def split_tile(tile):
    return tile % 2, tile // 2 % 4, tile // 8


def flip_x0(x):
    return x ^ 1


def flip_x1(x):
    return 3 - x


def flip_z0(z):
    return z ^ 1


def flip_z1(z):
    return 3 - z if z < 4 else 11 - z


def flip_z2(z):
    return 7 - z


flips = {"x0": flip_x0, "x1": flip_x1, "z0": flip_z0, "z1": flip_z1, "z2": flip_z2}


def moved(value, dims, swap):
    pairs = []
    for tile in range(TILES):
        core, x, z = split_tile(tile)
        dim = dims[core]
        if dim in ("x0", "x1"):
            x = flips[dim](x)
        elif dim:
            z = flips[dim](z)
        core = 1 - core if swap else core
        pairs.append((tile, z * 8 + x * 2 + core))
    return lax.ppermute(value, "tile", pairs)


def halo(inner, outer, sections):
    within, across = [], []
    for section in sections:
        for tile in range(TILES):
            within.append((section * TILES + tile, section * TILES + (tile ^ 1)))
            other = tile + 1 if tile % 2 else tile - 1
            if 0 <= other < TILES:
                across.append((section * TILES + tile, section * TILES + other))
    axes = ("section", "tile")
    outer = lax.ppermute(outer, axes, across)
    inner = lax.ppermute(inner, axes, within)
    return inner, outer


def call(body, out_shape, smem, operands, scratch=(), cost=(0, 0)):
    spec = [pl.BlockSpec(memory_space=pltpu.SMEM)] * smem
    spec += [pl.BlockSpec(memory_space=pltpu.VMEM)] * (len(operands) - smem)
    outs = jax.tree.map(lambda _: pl.BlockSpec(memory_space=pltpu.VMEM), out_shape)
    return pl.pallas_call(
        body,
        out_shape=out_shape,
        in_specs=spec,
        out_specs=outs,
        scratch_shapes=list(scratch),
        compiler_params=pltpu.CompilerParams(vmem_limit_bytes=32 * 1024 * 1024),
        cost_estimate=pl.CostEstimate(flops=cost[0], bytes_accessed=cost[1], transcendentals=0),
    )(*operands)


def shape(dims, dtype):
    return jax.ShapeDtypeStruct(dims, dtype)


def fill_rows(rows_ref, odd, own, inner, outer):
    count = own.shape[0]
    rows_ref[MARGIN : MARGIN + count] = own[...]
    rows_ref[:MARGIN] = jnp.where(odd, inner[...], outer[...])
    rows_ref[MARGIN + count :] = jnp.where(odd, outer[...], inner[...])


def edges(odd, value_ref, inner_ref, outer_ref):
    count = value_ref.shape[0]
    head = value_ref[:MARGIN]
    tail = value_ref[count - MARGIN :]
    inner_ref[...] = jnp.where(odd, head, tail)
    outer_ref[...] = jnp.where(odd, tail, head)


def taps_sum(rows_ref, cols_ref, start, count, backward):
    coefs = cols_ref[pl.ds(start, BLOCK), :]
    rows = [
        rows_ref[row, pl.ds(start, BLOCK), :].astype(f32) for row in range(count + 2 * MARGIN)
    ]
    sums = [None] * count
    for tap_col in range(KS):
        shift = (tap_col - MARGIN if backward else MARGIN - tap_col) % 128
        weights = [
            jnp.broadcast_to(
                coefs[:, tap_row * KS + tap_col : tap_row * KS + tap_col + 1], rows[0].shape
            )
            for tap_row in range(KS)
        ]
        for row in range(count):
            part = None
            for tap_row in range(KS):
                place = row + (KS - 1 - tap_row if backward else tap_row)
                term = weights[tap_row] * rows[place]
                part = term if part is None else part + term
            if shift:
                part = pltpu.roll(part, shift, 1)
            sums[row] = part if sums[row] is None else sums[row] + part
    return sums


def forward_kernel(
    meta, acts, inner, outer, cols, up_t, bias, nhat_ref, inv_ref, hidden_ref, slope_ref, rows_ref, field_ref, normed_ref
):
    count, chans, width = acts.shape
    fill_rows(rows_ref, meta[ODD] == 1, acts, inner, outer)

    def step(index, carry):
        start = pl.multiple_of(index * BLOCK, BLOCK)
        sums = taps_sum(rows_ref, cols, start, count, False)
        for row in range(count):
            field_ref[pl.ds(start, BLOCK), row * width : (row + 1) * width] = sums[row]
        return carry

    lax.fori_loop(0, chans // BLOCK, step, 0)
    gain = cols[:, KS * KS : KS * KS + 1]
    for row in range(count):
        part = slice(row * width, (row + 1) * width)
        field = field_ref[:, part]
        center = field - jnp.mean(field, axis=0, keepdims=True)
        inverse = 1.0 / jnp.sqrt(jnp.mean(center * center, axis=0, keepdims=True) + norm_eps)
        nhat = center * inverse
        nhat_ref[:, part] = nhat
        inv_ref[:, part] = inverse
        normed_ref[:, part] = (nhat * gain).astype(bf16)
    units = up_t.shape[0]
    chunk = 128
    for first in range(0, units, chunk):
        part = slice(first, first + chunk)
        preact = jnp.dot(up_t[part], normed_ref[...], preferred_element_type=f32) + bias[part]
        square = preact * preact
        hyper = jnp.tanh(preact * (tanh_root + tanh_root * cubic_coef * square))
        half = 0.5 + 0.5 * hyper
        hidden_ref[part] = (preact * half).astype(bf16)
        slope = half * (
            1.0 + preact * (1.0 - hyper) * (tanh_root + 3.0 * cubic_coef * tanh_root * square)
        )
        slope_ref[part] = slope.astype(bf16)


def mlp_backward(cots, land, cols, down_t, up, slope, nhat, inv, out_ref, low_ref, field_ref, sums=None):
    width = cots[0].shape[1]
    count = len(cots)
    gain = cols[:, KS * KS : KS * KS + 1]
    layer = cols[:, KS * KS + 1 : KS * KS + 2]
    for row in range(count):
        wet = land[row].astype(f32)
        out_ref[:, row * width : (row + 1) * width] = (cots[row] * layer * wet).astype(bf16)
    units = down_t.shape[0]
    chunk = 128
    for first in range(0, units, chunk):
        part = slice(first, first + chunk)
        pregrad = jnp.dot(down_t[part], out_ref[...], preferred_element_type=f32)
        pregrad = pregrad * slope[part].astype(f32)
        low_ref[part] = pregrad.astype(bf16)
        if sums is not None:
            sums[0][part] = sum(
                pregrad[:, row * width : (row + 1) * width] for row in range(count)
            )
    featgrad = jnp.dot(up[...], low_ref[...], preferred_element_type=f32)
    gains = None
    for row in range(count):
        part = slice(row * width, (row + 1) * width)
        feat = featgrad[:, part]
        own = nhat[:, part]
        scaled = feat * gain
        mean = jnp.mean(scaled, axis=0, keepdims=True)
        cross = jnp.mean(scaled * own, axis=0, keepdims=True)
        field_ref[row] = (inv[:, part] * (scaled - mean - own * cross)).astype(bf16)
        if sums is not None:
            term = feat * own
            gains = term if gains is None else gains + term
    if sums is not None:
        sums[1][...] = gains


def turn_kernel(
    section, meta, land, cot, cols, down_t, up, slope, nhat, inv, field_ref, inner_ref, outer_ref, out_ref, low_ref
):
    @pl.when(meta[SECTION] == section)
    def _():
        cots = [cot[row].astype(f32) for row in range(cot.shape[0])]
        mlp_backward(cots, land, cols, down_t, up, slope, nhat, inv, out_ref, low_ref, field_ref)
        edges(meta[ODD] == 1, field_ref, inner_ref, outer_ref)


def conv_rows(meta, field, inner, outer, cot, cols, result_ref, rows_ref):
    count, chans, width = field.shape
    fill_rows(rows_ref, meta[ODD] == 1, field, inner, outer)

    def step(index, carry):
        start = pl.multiple_of(index * BLOCK, BLOCK)
        sums = taps_sum(rows_ref, cols, start, count, True)
        for row in range(count):
            own = cot[row, pl.ds(start, BLOCK), :].astype(f32)
            result_ref[row, pl.ds(start, BLOCK), :] = (own + sums[row]).astype(bf16)
        return carry

    lax.fori_loop(0, chans // BLOCK, step, 0)


def conv_kernel(section, meta, field, inner, outer, cot, cols, result_ref, rows_ref):
    @pl.when(meta[SECTION] == section)
    def _():
        conv_rows(meta, field, inner, outer, cot, cols, result_ref, rows_ref)


def last_conv_kernel(
    meta, land, owners, field, inner, outer, cot, cols, third, second, first, result_ref, sent_ref, rows_ref
):
    for section, kept in ((3, third), (2, second), (1, first)):

        @pl.when(meta[SECTION] == section)
        def _():
            result_ref[...] = kept[...]

    @pl.when(meta[SECTION] == 0)
    def _():
        conv_rows(meta, field, inner, outer, cot, cols, result_ref, rows_ref)

    sent_ref[...] = jnp.zeros_like(sent_ref)
    rank = jnp.int32(0)
    for local in range(result_ref.shape[0]):
        kept = jnp.bool_(False)
        for slot in range(owners.shape[0]):
            kept = kept | (owners[slot] == meta[OFFSET] + local)
        sent = (land[local] == 1) & jnp.logical_not(kept)
        for place in range(CAP):

            @pl.when(sent & (rank == place))
            def _():
                sent_ref[place] = result_ref[local]

        rank = rank + sent.astype(jnp.int32)


def slots_kernel(meta, owners, result, arrived, slots_ref):
    for slot in range(slots_ref.shape[0]):
        slots_ref[slot] = arrived[min(slot, CAP - 1)]
        for local in range(result.shape[0]):

            @pl.when(owners[slot] == meta[OFFSET] + local)
            def _():
                slots_ref[slot] = result[local]


def last_kernel(
    meta,
    land,
    cot_top,
    cot_2,
    cot_1,
    cot_0,
    cols,
    layer_row,
    down_t,
    down,
    up,
    slope,
    nhat,
    inv,
    hidden,
    acts,
    inner,
    outer,
    field_ref,
    field_inner_ref,
    field_outer_ref,
    keep_ref,
    near_ref,
    mate_ref,
    far_ref,
    out_ref,
    low_ref,
    bias_ref,
    gain_ref,
    rows_ref,
    taps_ref,
    packed_ref,
    cot_ref,
):
    count, chans, width = acts.shape
    units = slope.shape[0]
    odd = meta[ODD] == 1
    for section, cot in ((3, cot_top), (2, cot_2), (1, cot_1), (0, cot_0)):

        @pl.when(meta[SECTION] == section)
        def _():
            cot_ref[...] = cot[...]

    cots = [cot_ref[row].astype(f32) for row in range(count)]
    mlp_backward(
        cots, land, cols, down_t, up, slope, nhat, inv, out_ref, low_ref, field_ref, (bias_ref, gain_ref)
    )
    edges(odd, field_ref, field_inner_ref, field_outer_ref)
    gain = cols[:, KS * KS : KS * KS + 1]
    normed = (nhat[...] * gain).astype(bf16)
    turned = (((1,), (1,)), ((), ()))
    grad_up = lax.dot_general(normed, low_ref[...], turned, preferred_element_type=f32)
    packed_ref[:chans] = grad_up.astype(bf16)
    grad_down = lax.dot_general(out_ref[...], hidden[...], turned, preferred_element_type=f32)
    packed_ref[chans : 2 * chans] = grad_down.astype(bf16)
    product = grad_down * down[...].astype(f32)
    product = sum(product[:, first : first + 128] for first in range(0, units, 128))

    fill_rows(rows_ref, odd, acts, inner, outer)

    def step(index, carry):
        start = pl.multiple_of(index * BLOCK, BLOCK)
        rows = [
            rows_ref[row, pl.ds(start, BLOCK), :].astype(f32) for row in range(count + 2 * MARGIN)
        ]
        fields = [field_ref[row, pl.ds(start, BLOCK), :].astype(f32) for row in range(count)]
        lane = lax.broadcasted_iota(jnp.int32, (BLOCK, 128), 1)
        grads = jnp.zeros((BLOCK, 128), f32)
        for tap_col in range(KS):
            shift = (tap_col - MARGIN) % 128
            turned_fields = [pltpu.roll(field, shift, 1) if shift else field for field in fields]
            for tap_row in range(KS):
                part = None
                for row in range(count):
                    term = turned_fields[row] * rows[row + tap_row]
                    part = term if part is None else part + term
                grads = jnp.where(
                    lane == tap_row * KS + tap_col, jnp.sum(part, axis=1, keepdims=True), grads
                )
        taps_ref[pl.ds(start, BLOCK), :] = grads
        return carry

    lax.fori_loop(0, chans // BLOCK, step, 0)
    base = 2 * chans
    taps = jnp.transpose(taps_ref[...])[:56]
    zeros = jnp.zeros((56, units - chans), f32)
    bias_row = jnp.sum(jnp.transpose(bias_ref[...]), axis=0, keepdims=True)
    gain_row = jnp.sum(jnp.transpose(gain_ref[...]), axis=0, keepdims=True)
    scale_row = jnp.sum(jnp.transpose(product), axis=0, keepdims=True) / layer_row[...]
    gap = jnp.zeros((1, 256 - chans), f32)
    rest = jnp.zeros((1, units - 256 - chans), f32)
    pair_row = jnp.concatenate([gain_row, gap, scale_row, rest], axis=1)
    small = jnp.concatenate(
        [jnp.concatenate([taps, zeros], axis=1), bias_row, pair_row, jnp.zeros((6, units), f32)]
    )
    packed_ref[base : base + 64] = small.astype(bf16)
    part_rows = keep_ref.shape[0]
    for place, target in ((KEEP, keep_ref), (NEAR, near_ref), (MATE, mate_ref), (FAR, far_ref)):
        start = pl.multiple_of(meta[place] * part_rows, 16)
        target[...] = packed_ref[pl.ds(start, part_rows), :]


def finish_kernel(
    scale, meta, keep, near, mate, far, kernel_ref, gain_ref, up_ref, bias_ref, down_ref, scale_ref, packed_ref
):
    part_rows = keep.shape[0]
    for place, source in ((KEEP, keep), (NEAR, near), (MATE, mate), (FAR, far)):
        start = pl.multiple_of(meta[place] * part_rows, 16)
        packed_ref[pl.ds(start, part_rows), :] = source[...]
    chans = up_ref.shape[0]
    up_ref[...] = packed_ref[:chans].astype(f32) * scale
    down_ref[...] = packed_ref[chans : 2 * chans].astype(f32) * scale
    small = packed_ref[2 * chans :].astype(f32) * scale
    kernel_ref[...] = small[: KS * KS, :chans]
    bias_ref[...] = small[56:57]
    gain_ref[...] = small[57:58, :chans]
    scale_ref[...] = small[57:58, 256 : 256 + chans]


def added(*values):
    return sum(value.astype(f32) for value in values).astype(bf16)


def body(acts, cot_top, land, owners, dw_kernel, ln_gain, w_up, b_up, w_down, layer_scale):
    source = acts[0]
    count, chans, width = source.shape
    units = w_up.shape[2]
    cells = count * width
    tile_now = lax.axis_index("tile")
    section_now = lax.axis_index("section")
    scale = 1.0 / math.sqrt(lax.axis_size("tile") * cells)
    core, x, z = split_tile(tile_now)
    bit_x, bit_z = (x + 1) // 2 % 2, (z + 1) // 2 % 2
    bit = jnp.where(core == 0, bit_x, bit_z)
    mate_bit = jnp.where(core == 0, bit_z, bit_x)
    meta = jnp.stack(
        [
            section_now,
            core,
            2 * core + bit,
            2 * core + 1 - bit,
            2 * (1 - core) + mate_bit,
            2 * (1 - core) + 1 - mate_bit,
            tile_now * count,
            core,
        ]
    ).astype(jnp.int32)

    odd = core == 1
    head, tail = source[:MARGIN], source[count - MARGIN :]
    acts_inner, acts_outer = halo(
        jnp.where(odd, head, tail), jnp.where(odd, tail, head), range(SECTIONS)
    )
    cols = jnp.concatenate([dw_kernel[0], ln_gain, layer_scale]).T
    up, down = w_up[0], w_down[0]
    up_t, down_t = up.T, down.T
    bias = b_up.reshape(units, 1)

    padded = pltpu.VMEM((count + 2 * MARGIN, chans, width), bf16)
    nhat, inv, hidden, slope = call(
        forward_kernel,
        (
            shape((chans, cells), f32),
            shape((1, cells), f32),
            shape((units, cells), bf16),
            shape((units, cells), bf16),
        ),
        1,
        (meta, source, acts_inner, acts_outer, cols, up_t, bias),
        (padded, pltpu.VMEM((chans, cells), f32), pltpu.VMEM((chans, cells), bf16)),
    )

    rows_shape = shape((count, chans, width), bf16)
    edge_shape = shape((MARGIN, chans, width), bf16)
    outgrads = pltpu.VMEM((chans, cells), bf16)
    lowgrads = pltpu.VMEM((units, cells), bf16)
    cots, results = [cot_top], []
    for section in range(SECTIONS - 1, 0, -1):
        field, inner, outer = call(
            functools.partial(turn_kernel, section),
            (rows_shape, edge_shape, edge_shape),
            2,
            (meta, land, cots[-1], cols, down_t, up, slope, nhat, inv),
            (outgrads, lowgrads),
        )
        inner, outer = halo(inner, outer, (section,))
        result = call(
            functools.partial(conv_kernel, section),
            rows_shape,
            1,
            (meta, field, inner, outer, cots[-1], cols),
            (padded,),
        )
        results.append(result)
        pairs = [
            (section * TILES + tile, (section - 1) * TILES + tile) for tile in range(TILES)
        ]
        cots.append(lax.ppermute(result, ("section", "tile"), pairs))

    part = shape(((2 * chans + 64) // 4, units), bf16)
    field, inner, outer, keep, near, mate, far = call(
        last_kernel,
        (rows_shape, edge_shape, edge_shape, part, part, part, part),
        2,
        (meta, land, *cots, cols, layer_scale, down_t, down, up, slope, nhat, inv, hidden)
        + (source, acts_inner, acts_outer),
        (
            outgrads,
            lowgrads,
            pltpu.VMEM((units, width), f32),
            pltpu.VMEM((chans, width), f32),
            padded,
            pltpu.VMEM((chans, 128), f32),
            pltpu.VMEM((2 * chans + 64, units), bf16),
            pltpu.VMEM((count, chans, width), bf16),
        ),
    )
    far = moved(far, ("z0", "x0"), True)
    near = moved(near, ("x0", "z0"), False)
    mate = moved(mate, ("", ""), True)
    total = added(keep, near, mate, far)
    for dims in (("x1", "z1"), ("z0", "z2"), ("z1", "x0"), ("z2", "x1")):
        total = added(total, moved(total, dims, False))
    far = moved(total, ("x0", "z0"), True)
    near = moved(total, ("x0", "z0"), False)
    mate = moved(total, ("", ""), True)
    grads = call(
        functools.partial(finish_kernel, scale),
        (
            shape((KS * KS, chans), f32),
            shape((1, chans), f32),
            shape((chans, units), f32),
            shape((1, units), f32),
            shape((chans, units), f32),
            shape((1, chans), f32),
        ),
        1,
        (meta, total, near, mate, far),
        (pltpu.VMEM((2 * chans + 64, units), bf16),),
    )

    inner, outer = halo(inner, outer, (0,))
    result, sent = call(
        last_conv_kernel,
        (rows_shape, shape((CAP, chans, width), bf16)),
        3,
        (meta, land, owners, field, inner, outer, cots[-1], cols, *results),
        (padded,),
    )
    arrived = lax.ppermute(sent, "tile", [(tile, tile + 1) for tile in range(TILES - 1)])
    slotted = call(
        slots_kernel,
        shape((owners.shape[0], chans, width), bf16),
        2,
        (meta, owners, result, arrived),
    )
    grad_kernel, grad_gain, grad_up, grad_bias, grad_down, grad_scale = grads
    return (
        slotted[None],
        grad_kernel[None],
        grad_gain,
        grad_up[None],
        grad_bias,
        grad_down[None],
        grad_scale,
    )


def solution(mesh):
    in_specs = (
        P("section", "tile", None, None),
        P("tile", None, None),
        P("tile"),
        P("tile"),
        P("section", None, None),
        P("section", None),
        P("section", None, None),
        P("section", None),
        P("section", None, None),
        P("section", None),
    )
    out_specs = (
        P("section", "tile", None, None),
        P("section", None, None),
        P("section", None),
        P("section", None, None),
        P("section", None),
        P("section", None, None),
        P("section", None),
    )
    return jax.shard_map(body, mesh=mesh, in_specs=in_specs, out_specs=out_specs, check_vma=False)
```

```python
import functools
import math

import jax
import jax.numpy as jnp
from jax import lax
from jax.experimental import pallas as pl
from jax.experimental.pallas import tpu as pltpu
from jax.sharding import PartitionSpec as P

KS = 7
CAP = 2
SECTIONS = 4
TILES = 64
MARGIN = 3
BLOCK = 16
UNROLL = 4

norm_eps = 1e-06
tanh_root = math.sqrt(2.0 / math.pi)
cubic_coef = 0.044715

f32 = jnp.float32
bf16 = jnp.bfloat16

SECTION, ODD, KEEP, NEAR, MATE, FAR, OFFSET, INSIDE = range(8)
PLACES = 8


def split_tile(tile):
    return tile % 2, tile // 2 % 4, tile // 8


def flip_x0(x):
    return x ^ 1


def flip_x1(x):
    return 3 - x


def flip_z0(z):
    return z ^ 1


def flip_z1(z):
    return 3 - z if z < 4 else 11 - z


def flip_z2(z):
    return 7 - z


flips = {"x0": flip_x0, "x1": flip_x1, "z0": flip_z0, "z1": flip_z1, "z2": flip_z2}


def moved(value, dims, swap):
    pairs = []
    for tile in range(TILES):
        core, x, z = split_tile(tile)
        dim = dims[core]
        if dim in ("x0", "x1"):
            x = flips[dim](x)
        elif dim:
            z = flips[dim](z)
        core = 1 - core if swap else core
        pairs.append((tile, z * 8 + x * 2 + core))
    return lax.ppermute(value, "tile", pairs)


def halo(inner, outer):
    across = [(tile, (tile + 1 if tile % 2 else tile - 1) % TILES) for tile in range(TILES)]
    outer = lax.ppermute(outer, "tile", across)
    inner = lax.ppermute(inner, "tile", [(tile, tile ^ 1) for tile in range(TILES)])
    return inner, outer


def call(body, out_shape, smem, operands, scratch=(), cost=(0, 0)):
    spec = [pl.BlockSpec(memory_space=pltpu.SMEM)] * smem
    spec += [pl.BlockSpec(memory_space=pltpu.VMEM)] * (len(operands) - smem)
    outs = jax.tree.map(lambda _: pl.BlockSpec(memory_space=pltpu.VMEM), out_shape)
    return pl.pallas_call(
        body,
        out_shape=out_shape,
        in_specs=spec,
        out_specs=outs,
        scratch_shapes=list(scratch),
        compiler_params=pltpu.CompilerParams(vmem_limit_bytes=32 * 1024 * 1024),
        cost_estimate=pl.CostEstimate(flops=cost[0], bytes_accessed=cost[1], transcendentals=0),
    )(*operands)


def shape(dims, dtype):
    return jax.ShapeDtypeStruct(dims, dtype)


def fill_rows(rows_ref, meta, own, inner, outer):
    count = own.shape[0]
    odd = meta[ODD] == 1
    far_rows = jnp.where(meta[INSIDE] == 1, outer[...], jnp.zeros_like(outer))
    near_rows = inner[...]
    rows_ref[MARGIN : MARGIN + count] = own[...]
    rows_ref[:MARGIN] = jnp.where(odd, near_rows, far_rows)
    rows_ref[MARGIN + count : 2 * MARGIN + count] = jnp.where(odd, far_rows, near_rows)
    rows_ref[2 * MARGIN + count :] = jnp.zeros((1,) + own.shape[1:], bf16)


def edges(odd, value_ref, inner_ref, outer_ref):
    count = value_ref.shape[0]
    head = value_ref[:MARGIN]
    tail = value_ref[count - MARGIN :]
    inner_ref[...] = jnp.where(odd, head, tail)
    outer_ref[...] = jnp.where(odd, tail, head)


def prepare_kernel(cols, forth_ref, back_ref):
    high = cols[...].astype(bf16)
    low = (cols[...] - high.astype(f32)).astype(bf16)
    chans, taps = cols.shape
    wide = KS * 128
    tap = lax.broadcasted_iota(jnp.int32, (taps, wide), 0)
    place = lax.broadcasted_iota(jnp.int32, (taps, wide), 1)
    tap_col, tap_row = place >> 7, (place >> 4) & (PLACES - 1)
    own = lax.broadcasted_iota(jnp.int32, (chans, wide), 0) & (BLOCK - 1)
    diagonal = own == (lax.broadcasted_iota(jnp.int32, (chans, wide), 1) & (BLOCK - 1))
    for target, row in ((forth_ref, tap_row), (back_ref, KS - 1 - tap_row)):
        hit = (tap == row * KS + tap_col) & (tap_row < KS)
        spread = jnp.where(hit, 1.0, 0.0).astype(bf16)
        for half, value in enumerate((high, low)):
            filled = jnp.dot(value, spread, preferred_element_type=f32)
            filled = jnp.where(diagonal, filled, 0.0).astype(bf16)
            for block in range(chans // BLOCK):
                for col in range(KS):
                    target[
                        block, col * BLOCK : (col + 1) * BLOCK, half * 128 : (half + 1) * 128
                    ] = filled[block * BLOCK : (block + 1) * BLOCK, col * 128 : (col + 1) * 128]


def stacked(rows_ref, start, count):
    rows = [rows_ref[row, pl.ds(start, BLOCK), :] for row in range(count + PLACES - 1)]
    return jnp.concatenate(
        [jnp.concatenate(rows[place : place + count], axis=1) for place in range(PLACES)], axis=0
    )


def taps_sum(rows_ref, taps_mat, block, count, backward):
    windows = stacked(rows_ref, pl.multiple_of(block * BLOCK, BLOCK), count)
    parts = jnp.dot(
        taps_mat[block], jnp.concatenate([windows, windows], axis=0), preferred_element_type=f32
    )
    sums = []
    for row in range(count):
        total = None
        for tap_col in range(KS):
            shift = (tap_col - MARGIN if backward else MARGIN - tap_col) % 128
            part = parts[tap_col * BLOCK : (tap_col + 1) * BLOCK, row * 128 : (row + 1) * 128]
            if shift:
                part = pltpu.roll(part, shift, 1)
            total = part if total is None else total + part
        sums.append(total)
    return sums


def forward_kernel(
    meta, acts, inner, outer, taps_mat, cols, up_t, bias, nhat_ref, inv_ref, hidden_ref, slope_ref, rows_ref, field_ref, normed_ref
):
    count, chans, width = acts.shape
    fill_rows(rows_ref, meta, acts, inner, outer)

    def step(index, carry):
        start = pl.multiple_of(index * BLOCK, BLOCK)
        sums = taps_sum(rows_ref, taps_mat, index, count, False)
        for row in range(count):
            field_ref[pl.ds(start, BLOCK), row * width : (row + 1) * width] = sums[row]
        return carry

    lax.fori_loop(0, chans // BLOCK, step, 0, unroll=UNROLL)
    gain = cols[:, KS * KS : KS * KS + 1]
    for row in range(count):
        part = slice(row * width, (row + 1) * width)
        field = field_ref[:, part]
        center = field - jnp.mean(field, axis=0, keepdims=True)
        inverse = 1.0 / jnp.sqrt(jnp.mean(center * center, axis=0, keepdims=True) + norm_eps)
        nhat = center * inverse
        nhat_ref[:, part] = nhat
        inv_ref[:, part] = inverse
        normed_ref[:, part] = (nhat * gain).astype(bf16)
    units = up_t.shape[0]
    chunk = 128
    for first in range(0, units, chunk):
        part = slice(first, first + chunk)
        preact = jnp.dot(up_t[part], normed_ref[...], preferred_element_type=f32) + bias[part]
        square = preact * preact
        hyper = jnp.tanh(preact * (tanh_root + tanh_root * cubic_coef * square))
        half = 0.5 + 0.5 * hyper
        hidden_ref[part] = (preact * half).astype(bf16)
        slope = half * (
            1.0 + preact * (1.0 - hyper) * (tanh_root + 3.0 * cubic_coef * tanh_root * square)
        )
        slope_ref[part] = slope.astype(bf16)


def mlp_backward(cots, land, cols, down_t, up, slope, nhat, inv, out_ref, low_ref, field_ref, sums=None):
    width = cots[0].shape[1]
    count = len(cots)
    gain = cols[:, KS * KS : KS * KS + 1]
    layer = cols[:, KS * KS + 1 : KS * KS + 2]
    for row in range(count):
        wet = land[row].astype(f32)
        out_ref[:, row * width : (row + 1) * width] = (cots[row] * layer * wet).astype(bf16)
    units = down_t.shape[0]
    chunk = 128
    for first in range(0, units, chunk):
        part = slice(first, first + chunk)
        pregrad = jnp.dot(down_t[part], out_ref[...], preferred_element_type=f32)
        pregrad = pregrad * slope[part].astype(f32)
        low_ref[part] = pregrad.astype(bf16)
        if sums is not None:
            sums[0][part] = sum(
                pregrad[:, row * width : (row + 1) * width] for row in range(count)
            )
    featgrad = jnp.dot(up[...], low_ref[...], preferred_element_type=f32)
    gains = None
    for row in range(count):
        part = slice(row * width, (row + 1) * width)
        feat = featgrad[:, part]
        own = nhat[:, part]
        scaled = feat * gain
        mean = jnp.mean(scaled, axis=0, keepdims=True)
        cross = jnp.mean(scaled * own, axis=0, keepdims=True)
        field_ref[row] = (inv[:, part] * (scaled - mean - own * cross)).astype(bf16)
        if sums is not None:
            term = feat * own
            gains = term if gains is None else gains + term
    if sums is not None:
        sums[1][...] = gains


def turn_kernel(
    section, meta, land, cot, cols, down_t, up, slope, nhat, inv, field_ref, inner_ref, outer_ref, out_ref, low_ref
):
    @pl.when(meta[SECTION] == section)
    def _():
        cots = [cot[row].astype(f32) for row in range(cot.shape[0])]
        mlp_backward(cots, land, cols, down_t, up, slope, nhat, inv, out_ref, low_ref, field_ref)
        edges(meta[ODD] == 1, field_ref, inner_ref, outer_ref)


def conv_rows(meta, field, inner, outer, cot, taps_mat, result_ref, rows_ref):
    count, chans, width = field.shape
    fill_rows(rows_ref, meta, field, inner, outer)

    def step(index, carry):
        start = pl.multiple_of(index * BLOCK, BLOCK)
        sums = taps_sum(rows_ref, taps_mat, index, count, True)
        for row in range(count):
            own = cot[row, pl.ds(start, BLOCK), :].astype(f32)
            result_ref[row, pl.ds(start, BLOCK), :] = (own + sums[row]).astype(bf16)
        return carry

    lax.fori_loop(0, chans // BLOCK, step, 0, unroll=UNROLL)


def conv_kernel(section, meta, field, inner, outer, cot, taps_mat, result_ref, rows_ref):
    @pl.when(meta[SECTION] == section)
    def _():
        conv_rows(meta, field, inner, outer, cot, taps_mat, result_ref, rows_ref)


def last_conv_kernel(
    meta, land, owners, field, inner, outer, cot, taps_mat, third, second, first, result_ref, sent_ref, rows_ref
):
    for section, kept in ((3, third), (2, second), (1, first)):

        @pl.when(meta[SECTION] == section)
        def _():
            result_ref[...] = kept[...]

    @pl.when(meta[SECTION] == 0)
    def _():
        conv_rows(meta, field, inner, outer, cot, taps_mat, result_ref, rows_ref)

    sent_ref[...] = jnp.zeros_like(sent_ref)
    rank = jnp.int32(0)
    for local in range(result_ref.shape[0]):
        kept = jnp.bool_(False)
        for slot in range(owners.shape[0]):
            kept = kept | (owners[slot] == meta[OFFSET] + local)
        sent = (land[local] == 1) & jnp.logical_not(kept)
        for place in range(CAP):

            @pl.when(sent & (rank == place))
            def _():
                sent_ref[place] = result_ref[local]

        rank = rank + sent.astype(jnp.int32)


def slots_kernel(meta, owners, result, arrived, slots_ref):
    for slot in range(slots_ref.shape[0]):
        slots_ref[slot] = arrived[min(slot, CAP - 1)]
        for local in range(result.shape[0]):

            @pl.when(owners[slot] == meta[OFFSET] + local)
            def _():
                slots_ref[slot] = result[local]


def last_kernel(
    meta,
    land,
    cot_top,
    cot_2,
    cot_1,
    cot_0,
    cols,
    layer_row,
    down_t,
    down,
    up,
    slope,
    nhat,
    inv,
    hidden,
    acts,
    inner,
    outer,
    field_ref,
    field_inner_ref,
    field_outer_ref,
    keep_ref,
    near_ref,
    mate_ref,
    far_ref,
    out_ref,
    low_ref,
    bias_ref,
    gain_ref,
    rows_ref,
    packed_ref,
    cot_ref,
):
    count, chans, width = acts.shape
    units = slope.shape[0]
    odd = meta[ODD] == 1
    for section, cot in ((3, cot_top), (2, cot_2), (1, cot_1), (0, cot_0)):

        @pl.when(meta[SECTION] == section)
        def _():
            cot_ref[...] = cot[...]

    cots = [cot_ref[row].astype(f32) for row in range(count)]
    mlp_backward(
        cots, land, cols, down_t, up, slope, nhat, inv, out_ref, low_ref, field_ref, (bias_ref, gain_ref)
    )
    edges(odd, field_ref, field_inner_ref, field_outer_ref)
    gain = cols[:, KS * KS : KS * KS + 1]
    normed = (nhat[...] * gain).astype(bf16)
    turned = (((1,), (1,)), ((), ()))
    grad_up = lax.dot_general(normed, low_ref[...], turned, preferred_element_type=f32)
    packed_ref[:chans] = grad_up
    grad_down = lax.dot_general(out_ref[...], hidden[...], turned, preferred_element_type=f32)
    packed_ref[chans : 2 * chans] = grad_down
    product = grad_down * down[...].astype(f32)
    product = sum(product[:, first : first + 128] for first in range(0, units, 128))

    fill_rows(rows_ref, meta, acts, inner, outer)
    base = 2 * chans
    shifts = [(tap_col - MARGIN) % 128 for tap_col in range(KS)]
    own = lax.broadcasted_iota(jnp.int32, (BLOCK, 128), 0)
    diagonal = own == (lax.broadcasted_iota(jnp.int32, (BLOCK, 128), 1) & (BLOCK - 1))
    for block in range(chans // BLOCK):
        start = block * BLOCK
        windows = stacked(rows_ref, start, count)
        fields = [field_ref[row, start : start + BLOCK, :].astype(f32) for row in range(count)]
        rolled = jnp.concatenate(
            [
                jnp.concatenate(
                    [pltpu.roll(field, shift, 1) if shift else field for field in fields], axis=1
                )
                for shift in shifts
            ],
            axis=0,
        ).astype(bf16)
        crossed = lax.dot_general(rolled, windows, turned, preferred_element_type=f32)
        first = base + block // 6 * 8
        lanes = slice(block % 6 * 128, block % 6 * 128 + 128)
        for tap_col in range(KS):
            part = jnp.where(diagonal, crossed[tap_col * BLOCK : (tap_col + 1) * BLOCK], 0.0)
            packed_ref[first + tap_col : first + tap_col + 1, lanes] = jnp.sum(
                part, axis=0, keepdims=True
            )
        packed_ref[first + KS : first + PLACES, lanes] = jnp.zeros((1, 128), f32)
    bias_row = jnp.sum(jnp.transpose(bias_ref[...]), axis=0, keepdims=True)
    gain_row = jnp.sum(jnp.transpose(gain_ref[...]), axis=0, keepdims=True)
    scale_row = jnp.sum(jnp.transpose(product), axis=0, keepdims=True) / layer_row[...]
    packed_ref[base + 16 :] = jnp.zeros((packed_ref.shape[0] - base - 16, units), f32)
    packed_ref[base + 16 : base + 17] = bias_row
    packed_ref[base + 17 : base + 18, :chans] = gain_row
    packed_ref[base + 17 : base + 18, 256 : 256 + chans] = scale_row
    part_rows = keep_ref.shape[0]
    for place, target in ((KEEP, keep_ref), (NEAR, near_ref), (MATE, mate_ref), (FAR, far_ref)):
        start = pl.multiple_of(meta[place] * part_rows, 8)
        target[...] = packed_ref[pl.ds(start, part_rows), :].astype(bf16)


def finish_kernel(
    scale, meta, keep, near, mate, far, kernel_ref, gain_ref, up_ref, bias_ref, down_ref, scale_ref, packed_ref
):
    part_rows = keep.shape[0]
    for place, source in ((KEEP, keep), (NEAR, near), (MATE, mate), (FAR, far)):
        start = pl.multiple_of(meta[place] * part_rows, 8)
        packed_ref[pl.ds(start, part_rows), :] = source[...].astype(f32) * scale
    chans = up_ref.shape[0]
    base = 2 * chans
    up_ref[...] = packed_ref[:chans]
    down_ref[...] = packed_ref[chans:base]
    lane = lax.broadcasted_iota(jnp.int32, (PLACES, 128), 1) >> 4
    blocks = chans // BLOCK
    for tap_row in range(KS):
        halves = []
        for first in range(0, blocks, PLACES):
            half = jnp.zeros((PLACES, 128), f32)
            for block in range(first, min(first + PLACES, blocks)):
                rows = slice(base + block // 6 * 8, base + block // 6 * 8 + 8)
                part = packed_ref[rows, block % 6 * 128 : block % 6 * 128 + 128]
                shift = (block - first - tap_row) * BLOCK % 128
                if shift:
                    part = pltpu.roll(part, shift, 1)
                half = jnp.where(lane == block - first, part, half)
            halves.append(half)
        line = jnp.concatenate(halves, axis=1)
        kernel_ref[tap_row * KS : (tap_row + 1) * KS] = line[:KS, :chans]
    bias_ref[...] = packed_ref[base + 16 : base + 17]
    gain_ref[...] = packed_ref[base + 17 : base + 18, :chans]
    scale_ref[...] = packed_ref[base + 17 : base + 18, 256 : 256 + chans]


def added(*values):
    return sum(value.astype(f32) for value in values).astype(bf16)


def body(acts, cot_top, land, owners, dw_kernel, ln_gain, w_up, b_up, w_down, layer_scale):
    source = acts[0]
    count, chans, width = source.shape
    units = w_up.shape[2]
    cells = count * width
    tile_now = lax.axis_index("tile")
    section_now = lax.axis_index("section")
    scale = 1.0 / math.sqrt(lax.axis_size("tile") * cells)
    core, x, z = split_tile(tile_now)
    bit_x, bit_z = (x + 1) // 2 % 2, (z + 1) // 2 % 2
    bit = jnp.where(core == 0, bit_x, bit_z)
    mate_bit = jnp.where(core == 0, bit_z, bit_x)
    meta = jnp.stack(
        [
            section_now,
            core,
            2 * core + bit,
            2 * core + 1 - bit,
            2 * (1 - core) + mate_bit,
            2 * (1 - core) + 1 - mate_bit,
            tile_now * count,
            jnp.where((tile_now == 0) | (tile_now == TILES - 1), 0, 1),
        ]
    ).astype(jnp.int32)

    odd = core == 1
    head, tail = source[:MARGIN], source[count - MARGIN :]
    acts_inner, acts_outer = halo(jnp.where(odd, head, tail), jnp.where(odd, tail, head))
    unused = jnp.zeros((64 - KS * KS - 2, chans), f32)
    cols = jnp.concatenate([dw_kernel[0], ln_gain, layer_scale, unused]).T
    taps_shape = shape((chans // BLOCK, KS * BLOCK, 256), bf16)
    forth, back = call(prepare_kernel, (taps_shape, taps_shape), 0, (cols,), cost=(10**9, 10**7))
    up, down = w_up[0], w_down[0]
    up_t, down_t = up.T, down.T
    bias = b_up.reshape(units, 1)

    padded = pltpu.VMEM((count + PLACES - 1, chans, width), bf16)
    nhat, inv, hidden, slope = call(
        forward_kernel,
        (
            shape((chans, cells), f32),
            shape((1, cells), f32),
            shape((units, cells), bf16),
            shape((units, cells), bf16),
        ),
        1,
        (meta, source, acts_inner, acts_outer, forth, cols, up_t, bias),
        (padded, pltpu.VMEM((chans, cells), f32), pltpu.VMEM((chans, cells), bf16)),
    )

    rows_shape = shape((count, chans, width), bf16)
    edge_shape = shape((MARGIN, chans, width), bf16)
    outgrads = pltpu.VMEM((chans, cells), bf16)
    lowgrads = pltpu.VMEM((units, cells), bf16)
    cots, results = [cot_top], []
    for section in range(SECTIONS - 1, 0, -1):
        field, inner, outer = call(
            functools.partial(turn_kernel, section),
            (rows_shape, edge_shape, edge_shape),
            2,
            (meta, land, cots[-1], cols, down_t, up, slope, nhat, inv),
            (outgrads, lowgrads),
        )
        inner, outer = halo(inner, outer)
        result = call(
            functools.partial(conv_kernel, section),
            rows_shape,
            1,
            (meta, field, inner, outer, cots[-1], back),
            (padded,),
        )
        results.append(result)
        pairs = [(place, (place - 1) % SECTIONS) for place in range(SECTIONS)]
        cots.append(lax.ppermute(result, "section", pairs))

    part = shape(((2 * chans + 32) // 4, units), bf16)
    field, inner, outer, keep, near, mate, far = call(
        last_kernel,
        (rows_shape, edge_shape, edge_shape, part, part, part, part),
        2,
        (meta, land, *cots, cols, layer_scale, down_t, down, up, slope, nhat, inv, hidden)
        + (source, acts_inner, acts_outer),
        (
            outgrads,
            lowgrads,
            pltpu.VMEM((units, width), f32),
            pltpu.VMEM((chans, width), f32),
            padded,
            pltpu.VMEM((2 * chans + 32, units), f32),
            pltpu.VMEM((count, chans, width), bf16),
        ),
    )
    far = moved(far, ("z0", "x0"), True)
    near = moved(near, ("x0", "z0"), False)
    mate = moved(mate, ("", ""), True)
    total = added(keep, near, mate, far)
    orders = (("x1", "z1"), ("z0", "z2"), ("z1", "x0"), ("z2", "x1"))
    total, inner, outer = lax.optimization_barrier((total, inner, outer))
    total = added(total, moved(total, orders[0], False))
    inner, outer = halo(inner, outer)
    total, inner, outer = lax.optimization_barrier((total, inner, outer))
    total = added(total, moved(total, orders[1], False))
    result, sent = call(
        last_conv_kernel,
        (rows_shape, shape((CAP, chans, width), bf16)),
        3,
        (meta, land, owners, field, inner, outer, cots[-1], back, *results),
        (padded,),
    )
    total, result, sent = lax.optimization_barrier((total, result, sent))
    total = added(total, moved(total, orders[2], False))
    arrived = lax.ppermute(sent, "tile", [(tile, (tile + 1) % TILES) for tile in range(TILES)])
    total, result, arrived = lax.optimization_barrier((total, result, arrived))
    total = added(total, moved(total, orders[3], False))
    slotted = call(
        slots_kernel,
        shape((owners.shape[0], chans, width), bf16),
        2,
        (meta, owners, result, arrived),
    )
    total, slotted = lax.optimization_barrier((total, slotted))
    far = moved(total, ("x0", "z0"), True)
    near = moved(total, ("x0", "z0"), False)
    mate = moved(total, ("", ""), True)
    grads = call(
        functools.partial(finish_kernel, scale),
        (
            shape((KS * KS, chans), f32),
            shape((1, chans), f32),
            shape((chans, units), f32),
            shape((1, units), f32),
            shape((chans, units), f32),
            shape((1, chans), f32),
        ),
        1,
        (meta, total, near, mate, far),
        (pltpu.VMEM((2 * chans + 32, units), f32),),
    )

    grad_kernel, grad_gain, grad_up, grad_bias, grad_down, grad_scale = grads
    return (
        slotted[None],
        grad_kernel[None],
        grad_gain,
        grad_up[None],
        grad_bias,
        grad_down[None],
        grad_scale,
    )


def solution(mesh):
    in_specs = (
        P("section", "tile", None, None),
        P("tile", None, None),
        P("tile"),
        P("tile"),
        P("section", None, None),
        P("section", None),
        P("section", None, None),
        P("section", None),
        P("section", None, None),
        P("section", None),
    )
    out_specs = (
        P("section", "tile", None, None),
        P("section", None, None),
        P("section", None),
        P("section", None, None),
        P("section", None),
        P("section", None, None),
        P("section", None),
    )
    return jax.shard_map(body, mesh=mesh, in_specs=in_specs, out_specs=out_specs, check_vma=False)
```

```python
import functools
import math

import jax
import jax.numpy as jnp
from jax import lax
from jax.experimental import pallas as pl
from jax.experimental.pallas import tpu as pltpu
from jax.sharding import PartitionSpec as P

KS = 7
CAP = 2
SECTIONS = 4
TILES = 64
MARGIN = 3
BLOCK = 16
UNROLL = 4

norm_eps = 1e-06
tanh_root = math.sqrt(2.0 / math.pi)
cubic_coef = 0.044715

f32 = jnp.float32
bf16 = jnp.bfloat16

SECTION, ODD, KEEP, NEAR, MATE, FAR, OFFSET, INSIDE, LAND = range(9)
PLACES = 8
OWNERS = LAND + 5


def split_tile(tile):
    return tile % 2, tile // 2 % 4, tile // 8


def flip_x0(x):
    return x ^ 1


def flip_x1(x):
    return 3 - x


def flip_z0(z):
    return z ^ 1


def flip_z1(z):
    return 3 - z if z < 4 else 11 - z


def flip_z2(z):
    return 7 - z


flips = {"x0": flip_x0, "x1": flip_x1, "z0": flip_z0, "z1": flip_z1, "z2": flip_z2}


def moved(value, dims, swap):
    pairs = []
    for tile in range(TILES):
        core, x, z = split_tile(tile)
        dim = dims[core]
        if dim in ("x0", "x1"):
            x = flips[dim](x)
        elif dim:
            z = flips[dim](z)
        core = 1 - core if swap else core
        pairs.append((tile, z * 8 + x * 2 + core))
    return lax.ppermute(value, "tile", pairs)


def halo(inner, outer):
    across = [(tile, (tile + 1 if tile % 2 else tile - 1) % TILES) for tile in range(TILES)]
    outer = lax.ppermute(outer, "tile", across)
    inner = lax.ppermute(inner, "tile", [(tile, tile ^ 1) for tile in range(TILES)])
    return inner, outer


def call(body, out_shape, smem, operands, scratch=(), cost=(0, 0)):
    spec = [pl.BlockSpec(memory_space=pltpu.SMEM)] * smem
    spec += [pl.BlockSpec(memory_space=pltpu.VMEM)] * (len(operands) - smem)
    outs = jax.tree.map(lambda _: pl.BlockSpec(memory_space=pltpu.VMEM), out_shape)
    return pl.pallas_call(
        body,
        out_shape=out_shape,
        in_specs=spec,
        out_specs=outs,
        scratch_shapes=list(scratch),
        compiler_params=pltpu.CompilerParams(vmem_limit_bytes=32 * 1024 * 1024),
        cost_estimate=pl.CostEstimate(flops=cost[0], bytes_accessed=cost[1], transcendentals=0),
    )(*operands)


def shape(dims, dtype):
    return jax.ShapeDtypeStruct(dims, dtype)


def fill_rows(rows_ref, meta, own, inner, outer):
    count = own.shape[0]
    odd = meta[ODD] == 1
    far_rows = jnp.where(meta[INSIDE] == 1, outer[...], jnp.zeros_like(outer))
    near_rows = inner[...]
    rows_ref[MARGIN : MARGIN + count] = own[...]
    rows_ref[:MARGIN] = jnp.where(odd, near_rows, far_rows)
    rows_ref[MARGIN + count : 2 * MARGIN + count] = jnp.where(odd, far_rows, near_rows)
    rows_ref[2 * MARGIN + count :] = jnp.zeros((1,) + own.shape[1:], bf16)


def edges(odd, value_ref, inner_ref, outer_ref):
    count = value_ref.shape[0]
    head = value_ref[:MARGIN]
    tail = value_ref[count - MARGIN :]
    inner_ref[...] = jnp.where(odd, head, tail)
    outer_ref[...] = jnp.where(odd, tail, head)


def prepare_kernel(
    kernel, gain, layer, bias, up, down, cols, forth_ref, back_ref, up_t_ref, down_t_ref, bias_ref, lines_ref
):
    lines_ref[...] = jnp.zeros_like(lines_ref)
    lines_ref[: KS * KS] = kernel[...]
    lines_ref[KS * KS : KS * KS + 1] = gain[...]
    lines_ref[KS * KS + 1 : KS * KS + 2] = layer[...]
    cols[...] = jnp.transpose(lines_ref[...])
    up_t_ref[...] = jnp.transpose(up[...].astype(f32)).astype(bf16)
    down_t_ref[...] = jnp.transpose(down[...].astype(f32)).astype(bf16)
    bias_ref[...] = jnp.transpose(jnp.broadcast_to(bias[...], (8, bias.shape[1])))
    high = cols[...].astype(bf16)
    low = (cols[...] - high.astype(f32)).astype(bf16)
    chans, taps = cols.shape
    wide = KS * 128
    tap = lax.broadcasted_iota(jnp.int32, (taps, wide), 0)
    place = lax.broadcasted_iota(jnp.int32, (taps, wide), 1)
    tap_col, tap_row = place >> 7, (place >> 4) & (PLACES - 1)
    own = lax.broadcasted_iota(jnp.int32, (chans, wide), 0) & (BLOCK - 1)
    diagonal = own == (lax.broadcasted_iota(jnp.int32, (chans, wide), 1) & (BLOCK - 1))
    for target, row in ((forth_ref, tap_row), (back_ref, KS - 1 - tap_row)):
        hit = (tap == row * KS + tap_col) & (tap_row < KS)
        spread = jnp.where(hit, 1.0, 0.0).astype(bf16)
        for half, value in enumerate((high, low)):
            filled = jnp.dot(value, spread, preferred_element_type=f32)
            filled = jnp.where(diagonal, filled, 0.0).astype(bf16)
            for block in range(chans // BLOCK):
                for col in range(KS):
                    target[
                        block, col * BLOCK : (col + 1) * BLOCK, half * 128 : (half + 1) * 128
                    ] = filled[block * BLOCK : (block + 1) * BLOCK, col * 128 : (col + 1) * 128]


def stacked(rows_ref, start, count):
    rows = [rows_ref[row, pl.ds(start, BLOCK), :] for row in range(count + PLACES - 1)]
    return jnp.concatenate(
        [jnp.concatenate(rows[place : place + count], axis=1) for place in range(PLACES)], axis=0
    )


def taps_sum(rows_ref, taps_mat, block, count, backward):
    windows = stacked(rows_ref, pl.multiple_of(block * BLOCK, BLOCK), count)
    parts = jnp.dot(
        taps_mat[block], jnp.concatenate([windows, windows], axis=0), preferred_element_type=f32
    )
    sums = []
    for row in range(count):
        total = None
        for tap_col in range(KS):
            shift = (tap_col - MARGIN if backward else MARGIN - tap_col) % 128
            part = parts[tap_col * BLOCK : (tap_col + 1) * BLOCK, row * 128 : (row + 1) * 128]
            if shift:
                part = pltpu.roll(part, shift, 1)
            total = part if total is None else total + part
        sums.append(total)
    return sums


def forward_kernel(
    meta, acts, inner, outer, taps_mat, cols, up_t, bias, nhat_ref, inv_ref, hidden_ref, slope_ref, rows_ref, field_ref, normed_ref
):
    count, chans, width = acts.shape
    fill_rows(rows_ref, meta, acts, inner, outer)

    def step(index, carry):
        start = pl.multiple_of(index * BLOCK, BLOCK)
        sums = taps_sum(rows_ref, taps_mat, index, count, False)
        for row in range(count):
            field_ref[pl.ds(start, BLOCK), row * width : (row + 1) * width] = sums[row]
        return carry

    lax.fori_loop(0, chans // BLOCK, step, 0, unroll=UNROLL)
    gain = cols[:, KS * KS : KS * KS + 1]
    for row in range(count):
        part = slice(row * width, (row + 1) * width)
        field = field_ref[:, part]
        center = field - jnp.mean(field, axis=0, keepdims=True)
        inverse = 1.0 / jnp.sqrt(jnp.mean(center * center, axis=0, keepdims=True) + norm_eps)
        nhat = center * inverse
        nhat_ref[:, part] = nhat
        inv_ref[:, part] = inverse
        normed_ref[:, part] = (nhat * gain).astype(bf16)
    units = up_t.shape[0]
    chunk = 128
    for first in range(0, units, chunk):
        part = slice(first, first + chunk)
        preact = jnp.dot(up_t[part], normed_ref[...], preferred_element_type=f32) + bias[part, :1]
        square = preact * preact
        hyper = jnp.tanh(preact * (tanh_root + tanh_root * cubic_coef * square))
        half = 0.5 + 0.5 * hyper
        hidden_ref[part] = (preact * half).astype(bf16)
        slope = half * (
            1.0 + preact * (1.0 - hyper) * (tanh_root + 3.0 * cubic_coef * tanh_root * square)
        )
        slope_ref[part] = slope.astype(bf16)


def mlp_backward(cots, meta, cols, down_t, up, slope, nhat, inv, out_ref, low_ref, field_ref, sums=None):
    width = cots[0].shape[1]
    count = len(cots)
    gain = cols[:, KS * KS : KS * KS + 1]
    layer = cols[:, KS * KS + 1 : KS * KS + 2]
    for row in range(count):
        wet = meta[LAND + row].astype(f32)
        out_ref[:, row * width : (row + 1) * width] = (cots[row] * layer * wet).astype(bf16)
    units = down_t.shape[0]
    chunk = 128
    for first in range(0, units, chunk):
        part = slice(first, first + chunk)
        pregrad = jnp.dot(down_t[part], out_ref[...], preferred_element_type=f32)
        pregrad = pregrad * slope[part].astype(f32)
        low_ref[part] = pregrad.astype(bf16)
        if sums is not None:
            sums[0][part] = sum(
                pregrad[:, row * width : (row + 1) * width] for row in range(count)
            )
    featgrad = jnp.dot(up[...], low_ref[...], preferred_element_type=f32)
    gains = None
    for row in range(count):
        part = slice(row * width, (row + 1) * width)
        feat = featgrad[:, part]
        own = nhat[:, part]
        scaled = feat * gain
        mean = jnp.mean(scaled, axis=0, keepdims=True)
        cross = jnp.mean(scaled * own, axis=0, keepdims=True)
        field_ref[row] = (inv[:, part] * (scaled - mean - own * cross)).astype(bf16)
        if sums is not None:
            term = feat * own
            gains = term if gains is None else gains + term
    if sums is not None:
        sums[1][...] = gains


def turn_kernel(
    section, meta, cot, cols, down_t, up, slope, nhat, inv, field_ref, inner_ref, outer_ref, out_ref, low_ref
):
    @pl.when(meta[SECTION] == section)
    def _():
        cots = [cot[row].astype(f32) for row in range(cot.shape[0])]
        mlp_backward(cots, meta, cols, down_t, up, slope, nhat, inv, out_ref, low_ref, field_ref)
        edges(meta[ODD] == 1, field_ref, inner_ref, outer_ref)


def conv_rows(meta, field, inner, outer, cot, taps_mat, result_ref, rows_ref):
    count, chans, width = field.shape
    fill_rows(rows_ref, meta, field, inner, outer)

    def step(index, carry):
        start = pl.multiple_of(index * BLOCK, BLOCK)
        sums = taps_sum(rows_ref, taps_mat, index, count, True)
        for row in range(count):
            own = cot[row, pl.ds(start, BLOCK), :].astype(f32)
            result_ref[row, pl.ds(start, BLOCK), :] = (own + sums[row]).astype(bf16)
        return carry

    lax.fori_loop(0, chans // BLOCK, step, 0, unroll=UNROLL)


def conv_kernel(section, meta, field, inner, outer, cot, taps_mat, result_ref, rows_ref):
    @pl.when(meta[SECTION] == section)
    def _():
        conv_rows(meta, field, inner, outer, cot, taps_mat, result_ref, rows_ref)


def last_conv_kernel(
    meta, field, inner, outer, cot, taps_mat, third, second, first, result_ref, sent_ref, rows_ref
):
    for section, kept in ((3, third), (2, second), (1, first)):

        @pl.when(meta[SECTION] == section)
        def _():
            result_ref[...] = kept[...]

    @pl.when(meta[SECTION] == 0)
    def _():
        conv_rows(meta, field, inner, outer, cot, taps_mat, result_ref, rows_ref)

    sent_ref[...] = jnp.zeros_like(sent_ref)
    rank = jnp.int32(0)
    for local in range(result_ref.shape[0]):
        kept = jnp.bool_(False)
        for slot in range(OWNERS, meta.shape[0]):
            kept = kept | (meta[slot] == meta[OFFSET] + local)
        sent = (meta[LAND + local] == 1) & jnp.logical_not(kept)
        for place in range(CAP):

            @pl.when(sent & (rank == place))
            def _():
                sent_ref[place] = result_ref[local]

        rank = rank + sent.astype(jnp.int32)


def slots_kernel(meta, result, arrived, slots_ref):
    for slot in range(slots_ref.shape[0]):
        slots_ref[slot] = arrived[min(slot, CAP - 1)]
        for local in range(result.shape[0]):

            @pl.when(meta[OWNERS + slot] == meta[OFFSET] + local)
            def _():
                slots_ref[slot] = result[local]


def last_kernel(
    meta,
    cot_top,
    cot_2,
    cot_1,
    cot_0,
    cols,
    layer_row,
    down_t,
    down,
    up,
    slope,
    nhat,
    inv,
    hidden,
    acts,
    inner,
    outer,
    field_ref,
    field_inner_ref,
    field_outer_ref,
    keep_ref,
    near_ref,
    mate_ref,
    far_ref,
    out_ref,
    low_ref,
    bias_ref,
    gain_ref,
    rows_ref,
    packed_ref,
    cot_ref,
):
    count, chans, width = acts.shape
    units = slope.shape[0]
    odd = meta[ODD] == 1
    for section, cot in ((3, cot_top), (2, cot_2), (1, cot_1), (0, cot_0)):

        @pl.when(meta[SECTION] == section)
        def _():
            cot_ref[...] = cot[...]

    cots = [cot_ref[row].astype(f32) for row in range(count)]
    mlp_backward(
        cots, meta, cols, down_t, up, slope, nhat, inv, out_ref, low_ref, field_ref, (bias_ref, gain_ref)
    )
    edges(odd, field_ref, field_inner_ref, field_outer_ref)
    gain = cols[:, KS * KS : KS * KS + 1]
    normed = (nhat[...] * gain).astype(bf16)
    turned = (((1,), (1,)), ((), ()))
    grad_up = lax.dot_general(normed, low_ref[...], turned, preferred_element_type=f32)
    packed_ref[:chans] = grad_up
    grad_down = lax.dot_general(out_ref[...], hidden[...], turned, preferred_element_type=f32)
    packed_ref[chans : 2 * chans] = grad_down
    product = grad_down * down[...].astype(f32)
    product = sum(product[:, first : first + 128] for first in range(0, units, 128))

    fill_rows(rows_ref, meta, acts, inner, outer)
    base = 2 * chans
    shifts = [(tap_col - MARGIN) % 128 for tap_col in range(KS)]
    own = lax.broadcasted_iota(jnp.int32, (BLOCK, 128), 0)
    diagonal = own == (lax.broadcasted_iota(jnp.int32, (BLOCK, 128), 1) & (BLOCK - 1))
    for block in range(chans // BLOCK):
        start = block * BLOCK
        windows = stacked(rows_ref, start, count)
        fields = [field_ref[row, start : start + BLOCK, :].astype(f32) for row in range(count)]
        rolled = jnp.concatenate(
            [
                jnp.concatenate(
                    [pltpu.roll(field, shift, 1) if shift else field for field in fields], axis=1
                )
                for shift in shifts
            ],
            axis=0,
        ).astype(bf16)
        crossed = lax.dot_general(rolled, windows, turned, preferred_element_type=f32)
        first = base + block // 6 * 8
        lanes = slice(block % 6 * 128, block % 6 * 128 + 128)
        for tap_col in range(KS):
            part = jnp.where(diagonal, crossed[tap_col * BLOCK : (tap_col + 1) * BLOCK], 0.0)
            packed_ref[first + tap_col : first + tap_col + 1, lanes] = jnp.sum(
                part, axis=0, keepdims=True
            )
        packed_ref[first + KS : first + PLACES, lanes] = jnp.zeros((1, 128), f32)
    bias_row = jnp.sum(jnp.transpose(bias_ref[...]), axis=0, keepdims=True)
    gain_row = jnp.sum(jnp.transpose(gain_ref[...]), axis=0, keepdims=True)
    scale_row = jnp.sum(jnp.transpose(product), axis=0, keepdims=True) / layer_row[...]
    packed_ref[base + 16 :] = jnp.zeros((packed_ref.shape[0] - base - 16, units), f32)
    packed_ref[base + 16 : base + 17] = bias_row
    packed_ref[base + 17 : base + 18, :chans] = gain_row
    packed_ref[base + 17 : base + 18, 256 : 256 + chans] = scale_row
    part_rows = keep_ref.shape[0]
    for place, target in ((KEEP, keep_ref), (NEAR, near_ref), (MATE, mate_ref), (FAR, far_ref)):
        start = pl.multiple_of(meta[place] * part_rows, 8)
        target[...] = packed_ref[pl.ds(start, part_rows), :].astype(bf16)


def finish_kernel(
    scale, meta, keep, near, mate, far, kernel_ref, gain_ref, up_ref, bias_ref, down_ref, scale_ref, packed_ref
):
    part_rows = keep.shape[0]
    for place, source in ((KEEP, keep), (NEAR, near), (MATE, mate), (FAR, far)):
        start = pl.multiple_of(meta[place] * part_rows, 8)
        packed_ref[pl.ds(start, part_rows), :] = source[...].astype(f32) * scale
    chans = up_ref.shape[1]
    base = 2 * chans
    up_ref[0] = packed_ref[:chans]
    down_ref[0] = packed_ref[chans:base]
    lane = lax.broadcasted_iota(jnp.int32, (PLACES, 128), 1) >> 4
    blocks = chans // BLOCK
    for tap_row in range(KS):
        halves = []
        for first in range(0, blocks, PLACES):
            half = jnp.zeros((PLACES, 128), f32)
            for block in range(first, min(first + PLACES, blocks)):
                rows = slice(base + block // 6 * 8, base + block // 6 * 8 + 8)
                part = packed_ref[rows, block % 6 * 128 : block % 6 * 128 + 128]
                shift = (block - first - tap_row) * BLOCK % 128
                if shift:
                    part = pltpu.roll(part, shift, 1)
                half = jnp.where(lane == block - first, part, half)
            halves.append(half)
        line = jnp.concatenate(halves, axis=1)
        kernel_ref[0, tap_row * KS : (tap_row + 1) * KS] = line[:KS, :chans]
    bias_ref[...] = packed_ref[base + 16 : base + 17]
    gain_ref[...] = packed_ref[base + 17 : base + 18, :chans]
    scale_ref[...] = packed_ref[base + 17 : base + 18, 256 : 256 + chans]


def added(*values):
    return sum(value.astype(f32) for value in values).astype(bf16)


def body(acts, cot_top, land, owners, dw_kernel, ln_gain, w_up, b_up, w_down, layer_scale):
    source = acts[0]
    count, chans, width = source.shape
    units = w_up.shape[2]
    cells = count * width
    tile_now = lax.axis_index("tile")
    section_now = lax.axis_index("section")
    scale = 1.0 / math.sqrt(lax.axis_size("tile") * cells)
    core, x, z = split_tile(tile_now)
    bit_x, bit_z = (x + 1) // 2 % 2, (z + 1) // 2 % 2
    bit = jnp.where(core == 0, bit_x, bit_z)
    mate_bit = jnp.where(core == 0, bit_z, bit_x)
    numbers = [
        section_now,
        core,
        2 * core + bit,
        2 * core + 1 - bit,
        2 * (1 - core) + mate_bit,
        2 * (1 - core) + 1 - mate_bit,
        tile_now * count,
        jnp.where((tile_now == 0) | (tile_now == TILES - 1), 0, 1),
    ]
    meta = jnp.concatenate([jnp.stack(numbers).astype(jnp.int32), land, owners])

    odd = core == 1
    head, tail = source[:MARGIN], source[count - MARGIN :]
    acts_inner, acts_outer = halo(jnp.where(odd, head, tail), jnp.where(odd, tail, head))
    up, down = w_up[0], w_down[0]
    taps_shape = shape((chans // BLOCK, KS * BLOCK, 256), bf16)
    cols, forth, back, up_t, down_t, bias = call(
        prepare_kernel,
        (
            shape((chans, 64), f32),
            taps_shape,
            taps_shape,
            shape((units, chans), bf16),
            shape((units, chans), bf16),
            shape((units, 8), f32),
        ),
        0,
        (dw_kernel[0], ln_gain, layer_scale, b_up, up, down),
        (pltpu.VMEM((64, chans), f32),),
        cost=(10**9, 10**7),
    )

    padded = pltpu.VMEM((count + PLACES - 1, chans, width), bf16)
    nhat, inv, hidden, slope = call(
        forward_kernel,
        (
            shape((chans, cells), f32),
            shape((1, cells), f32),
            shape((units, cells), bf16),
            shape((units, cells), bf16),
        ),
        1,
        (meta, source, acts_inner, acts_outer, forth, cols, up_t, bias),
        (padded, pltpu.VMEM((chans, cells), f32), pltpu.VMEM((chans, cells), bf16)),
    )

    rows_shape = shape((count, chans, width), bf16)
    edge_shape = shape((MARGIN, chans, width), bf16)
    outgrads = pltpu.VMEM((chans, cells), bf16)
    lowgrads = pltpu.VMEM((units, cells), bf16)
    cots, results = [cot_top], []
    for section in range(SECTIONS - 1, 0, -1):
        field, inner, outer = call(
            functools.partial(turn_kernel, section),
            (rows_shape, edge_shape, edge_shape),
            1,
            (meta, cots[-1], cols, down_t, up, slope, nhat, inv),
            (outgrads, lowgrads),
        )
        inner, outer = halo(inner, outer)
        result = call(
            functools.partial(conv_kernel, section),
            rows_shape,
            1,
            (meta, field, inner, outer, cots[-1], back),
            (padded,),
        )
        results.append(result)
        pairs = [(place, (place - 1) % SECTIONS) for place in range(SECTIONS)]
        cots.append(lax.ppermute(result, "section", pairs))

    part = shape(((2 * chans + 64) // 4, units), bf16)
    field, inner, outer, keep, near, mate, far = call(
        last_kernel,
        (rows_shape, edge_shape, edge_shape, part, part, part, part),
        1,
        (meta, *cots, cols, layer_scale, down_t, down, up, slope, nhat, inv, hidden)
        + (source, acts_inner, acts_outer),
        (
            outgrads,
            lowgrads,
            pltpu.VMEM((units, width), f32),
            pltpu.VMEM((chans, width), f32),
            padded,
            pltpu.VMEM((2 * chans + 64, units), f32),
            pltpu.VMEM((count, chans, width), bf16),
        ),
    )
    far = moved(far, ("z0", "x0"), True)
    near = moved(near, ("x0", "z0"), False)
    mate = moved(mate, ("", ""), True)
    total = added(keep, near, mate, far)
    orders = (("x1", "z1"), ("z0", "z2"), ("z1", "x0"), ("z2", "x1"))
    total, inner, outer = lax.optimization_barrier((total, inner, outer))
    half = total.shape[0] // 2
    first = jnp.where(core == 0, x // 2, (z + 2) // 4 % 2) == 0
    kept = jnp.where(first, total[:half], total[half:])
    given = jnp.where(first, total[half:], total[:half])
    total = added(kept, moved(given, orders[0], False))
    inner, outer = halo(inner, outer)
    total = added(total, moved(total, orders[1], False))
    result, sent = call(
        last_conv_kernel,
        (rows_shape, shape((CAP, chans, width), bf16)),
        1,
        (meta, field, inner, outer, cots[-1], back, *results),
        (padded,),
    )
    total, result, sent = lax.optimization_barrier((total, result, sent))
    total = added(total, moved(total, orders[2], False))
    arrived = lax.ppermute(sent, "tile", [(tile, (tile + 1) % TILES) for tile in range(TILES)])
    total = added(total, moved(total, orders[3], False))
    total, arrived = lax.optimization_barrier((total, arrived))
    slotted = call(
        slots_kernel,
        shape((owners.shape[0], chans, width), bf16),
        1,
        (meta, result, arrived),
    )
    other = moved(total, orders[0], False)
    total = jnp.concatenate([jnp.where(first, total, other), jnp.where(first, other, total)])
    total, slotted = lax.optimization_barrier((total, slotted))
    far = moved(total, ("x0", "z0"), True)
    near = moved(total, ("x0", "z0"), False)
    mate = moved(total, ("", ""), True)
    grads = call(
        functools.partial(finish_kernel, scale),
        (
            shape((1, KS * KS, chans), f32),
            shape((1, chans), f32),
            shape((1, chans, units), f32),
            shape((1, units), f32),
            shape((1, chans, units), f32),
            shape((1, chans), f32),
        ),
        1,
        (meta, total, near, mate, far),
        (pltpu.VMEM((2 * chans + 64, units), f32),),
    )

    grad_kernel, grad_gain, grad_up, grad_bias, grad_down, grad_scale = grads
    return (
        slotted[None],
        grad_kernel,
        grad_gain,
        grad_up,
        grad_bias,
        grad_down,
        grad_scale,
    )


def solution(mesh):
    in_specs = (
        P("section", "tile", None, None),
        P("tile", None, None),
        P("tile"),
        P("tile"),
        P("section", None, None),
        P("section", None),
        P("section", None, None),
        P("section", None),
        P("section", None, None),
        P("section", None),
    )
    out_specs = (
        P("section", "tile", None, None),
        P("section", None, None),
        P("section", None),
        P("section", None, None),
        P("section", None),
        P("section", None, None),
        P("section", None),
    )
    return jax.shard_map(body, mesh=mesh, in_specs=in_specs, out_specs=out_specs, check_vma=False)
```

```python
import functools
import math

import jax
import jax.numpy as jnp
from jax import lax
from jax.experimental import pallas as pl
from jax.experimental.pallas import tpu as pltpu
from jax.sharding import PartitionSpec as P

KS = 7
CAP = 2
SECTIONS = 4
TILES = 64
MARGIN = 3
BLOCK = 16
UNROLL = 4

norm_eps = 1e-06
tanh_root = math.sqrt(2.0 / math.pi)
cubic_coef = 0.044715

f32 = jnp.float32
bf16 = jnp.bfloat16

SECTION, ODD, KEEP, NEAR, MATE, FAR, OFFSET, INSIDE, LAND = range(9)
PLACES = 8
OWNERS = LAND + 5


def split_tile(tile):
    return tile % 2, tile // 2 % 4, tile // 8


def flip_x0(x):
    return x ^ 1


def flip_x1(x):
    return 3 - x


def flip_z0(z):
    return z ^ 1


def flip_z1(z):
    return 3 - z if z < 4 else 11 - z


def flip_z2(z):
    return 7 - z


flips = {"x0": flip_x0, "x1": flip_x1, "z0": flip_z0, "z1": flip_z1, "z2": flip_z2}


def moved(value, dims, swap):
    pairs = []
    for tile in range(TILES):
        core, x, z = split_tile(tile)
        dim = dims[core]
        if dim in ("x0", "x1"):
            x = flips[dim](x)
        elif dim:
            z = flips[dim](z)
        core = 1 - core if swap else core
        pairs.append((tile, z * 8 + x * 2 + core))
    return lax.ppermute(value, "tile", pairs)


def halo(inner, outer):
    across = [(tile, (tile + 1 if tile % 2 else tile - 1) % TILES) for tile in range(TILES)]
    outer = lax.ppermute(outer, "tile", across)
    inner = lax.ppermute(inner, "tile", [(tile, tile ^ 1) for tile in range(TILES)])
    return inner, outer


def call(body, out_shape, smem, operands, scratch=(), cost=(0, 0)):
    spec = [pl.BlockSpec(memory_space=pltpu.SMEM)] * smem
    spec += [pl.BlockSpec(memory_space=pltpu.VMEM)] * (len(operands) - smem)
    outs = jax.tree.map(lambda _: pl.BlockSpec(memory_space=pltpu.VMEM), out_shape)
    return pl.pallas_call(
        body,
        out_shape=out_shape,
        in_specs=spec,
        out_specs=outs,
        scratch_shapes=list(scratch),
        compiler_params=pltpu.CompilerParams(vmem_limit_bytes=32 * 1024 * 1024),
        cost_estimate=pl.CostEstimate(flops=cost[0], bytes_accessed=cost[1], transcendentals=0),
    )(*operands)


def shape(dims, dtype):
    return jax.ShapeDtypeStruct(dims, dtype)


def fill_rows(rows_ref, meta, own, inner, outer):
    count = own.shape[0]
    odd = meta[ODD] == 1
    far_rows = jnp.where(meta[INSIDE] == 1, outer[...], jnp.zeros_like(outer))
    near_rows = inner[...]
    rows_ref[MARGIN : MARGIN + count] = own[...]
    rows_ref[:MARGIN] = jnp.where(odd, near_rows, far_rows)
    rows_ref[MARGIN + count : 2 * MARGIN + count] = jnp.where(odd, far_rows, near_rows)
    rows_ref[2 * MARGIN + count :] = jnp.zeros((1,) + own.shape[1:], bf16)


def edges(odd, value_ref, inner_ref, outer_ref):
    count = value_ref.shape[0]
    head = value_ref[:MARGIN]
    tail = value_ref[count - MARGIN :]
    inner_ref[...] = jnp.where(odd, head, tail)
    outer_ref[...] = jnp.where(odd, tail, head)


def fill_taps(cols, targets):
    high = cols[...].astype(bf16)
    low = (cols[...] - high.astype(f32)).astype(bf16)
    chans, taps = cols.shape
    wide = KS * 128
    tap = lax.broadcasted_iota(jnp.int32, (taps, wide), 0)
    place = lax.broadcasted_iota(jnp.int32, (taps, wide), 1)
    tap_col, tap_row = place >> 7, (place >> 4) & (PLACES - 1)
    own = lax.broadcasted_iota(jnp.int32, (chans, wide), 0) & (BLOCK - 1)
    diagonal = own == (lax.broadcasted_iota(jnp.int32, (chans, wide), 1) & (BLOCK - 1))
    for target, row in zip(targets, (tap_row, KS - 1 - tap_row)):
        if target is None:
            continue
        hit = (tap == row * KS + tap_col) & (tap_row < KS)
        spread = jnp.where(hit, 1.0, 0.0).astype(bf16)
        for half, value in enumerate((high, low)):
            filled = jnp.dot(value, spread, preferred_element_type=f32)
            filled = jnp.where(diagonal, filled, 0.0).astype(bf16)
            for block in range(chans // BLOCK):
                for col in range(KS):
                    target[
                        block, col * BLOCK : (col + 1) * BLOCK, half * 128 : (half + 1) * 128
                    ] = filled[block * BLOCK : (block + 1) * BLOCK, col * 128 : (col + 1) * 128]


def prepare_kernel(
    kernel, gain, layer, bias, up, down, cols, forth_ref, back_ref, up_t_ref, down_t_ref, bias_ref, lines_ref
):
    lines_ref[...] = jnp.zeros_like(lines_ref)
    lines_ref[: KS * KS] = kernel[...]
    lines_ref[KS * KS : KS * KS + 1] = gain[...]
    lines_ref[KS * KS + 1 : KS * KS + 2] = layer[...]
    cols[...] = jnp.transpose(lines_ref[...])
    up_t_ref[...] = jnp.transpose(up[...].astype(f32)).astype(bf16)
    down_t_ref[...] = jnp.transpose(down[...].astype(f32)).astype(bf16)
    bias_ref[...] = jnp.transpose(jnp.broadcast_to(bias[...], (8, bias.shape[1])))
    fill_taps(cols, (forth_ref, back_ref))


def stacked(rows_ref, start, count):
    rows = [rows_ref[row, pl.ds(start, BLOCK), :] for row in range(count + PLACES - 1)]
    return jnp.concatenate(
        [jnp.concatenate(rows[place : place + count], axis=1) for place in range(PLACES)], axis=0
    )


def taps_sum(rows_ref, taps_mat, block, count, backward):
    windows = stacked(rows_ref, pl.multiple_of(block * BLOCK, BLOCK), count)
    parts = jnp.dot(
        taps_mat[block], jnp.concatenate([windows, windows], axis=0), preferred_element_type=f32
    )
    sums = []
    for row in range(count):
        total = None
        for tap_col in range(KS):
            shift = (tap_col - MARGIN if backward else MARGIN - tap_col) % 128
            part = parts[tap_col * BLOCK : (tap_col + 1) * BLOCK, row * 128 : (row + 1) * 128]
            if shift:
                part = pltpu.roll(part, shift, 1)
            total = part if total is None else total + part
        sums.append(total)
    return sums


def forward_kernel(
    meta, acts, inner, outer, taps_mat, cols, up_t, bias, bias_row, nhat_ref, inv_ref, hidden_ref, slope_ref, note_ref, rows_ref, field_ref, normed_ref
):
    count, chans, width = acts.shape
    fill_rows(rows_ref, meta, acts, inner, outer)

    def step(index, carry):
        start = pl.multiple_of(index * BLOCK, BLOCK)
        sums = taps_sum(rows_ref, taps_mat, index, count, False)
        for row in range(count):
            field_ref[pl.ds(start, BLOCK), row * width : (row + 1) * width] = sums[row]
        return carry

    lax.fori_loop(0, chans // BLOCK, step, 0, unroll=UNROLL)
    gain = cols[:, KS * KS : KS * KS + 1]
    for row in range(count):
        part = slice(row * width, (row + 1) * width)
        field = field_ref[:, part]
        center = field - jnp.mean(field, axis=0, keepdims=True)
        inverse = 1.0 / jnp.sqrt(jnp.mean(center * center, axis=0, keepdims=True) + norm_eps)
        nhat = center * inverse
        nhat_ref[:, part] = nhat
        inv_ref[:, part] = inverse
        normed_ref[:, part] = (nhat * gain).astype(bf16)
    cells = count * width
    note_ref[:chans, :cells] = nhat_ref[...].astype(bf16)
    high, low = two_parts(cols[...])
    note_ref[:chans, cells:] = jnp.concatenate([high, low], axis=1).astype(bf16)
    parts = two_parts(bias_row[...])
    padding = jnp.zeros((1, bias_row.shape[1] - cells), f32)
    parts += two_parts(jnp.concatenate([inv_ref[...], padding], axis=1))
    rest = jnp.zeros((BLOCK - len(parts), bias_row.shape[1]), f32)
    note_ref[chans:] = jnp.concatenate([*parts, rest]).astype(bf16)
    mlp_forward(normed_ref, up_t, bias, hidden_ref, slope_ref)


def two_parts(value):
    high = value.astype(bf16).astype(f32)
    return [high, value - high]


def mlp_forward(normed_ref, up_t, bias, hidden_ref, slope_ref):
    units = up_t.shape[0]
    chunk = 128
    for first in range(0, units, chunk):
        part = slice(first, first + chunk)
        preact = jnp.dot(up_t[part], normed_ref[...], preferred_element_type=f32) + bias[part, :1]
        square = preact * preact
        hyper = jnp.tanh(preact * (tanh_root + tanh_root * cubic_coef * square))
        half = 0.5 + 0.5 * hyper
        if hidden_ref is not None:
            hidden_ref[part] = (preact * half).astype(bf16)
        slope = half * (
            1.0 + preact * (1.0 - hyper) * (tanh_root + 3.0 * cubic_coef * tanh_root * square)
        )
        slope_ref[part] = slope.astype(bf16)


def adopt_kernel(
    meta, note, half, other, nhat_ref, inv_ref, slope_ref, cols_ref, back_ref, up_ref, down_t_ref, up_t_ref, bias_ref, normed_ref
):
    chans, cells = nhat_ref.shape
    units = slope_ref.shape[0]
    taps = cols_ref.shape[1]

    @pl.when((meta[SECTION] == SECTIONS - 1) | (meta[SECTION] == 0))
    def _():
        odd = meta[ODD] == 1
        up = jnp.where(odd, other[...], half[...])
        up_ref[...] = up
        up_t_ref[...] = jnp.transpose(up.astype(f32)).astype(bf16)
        down = jnp.where(odd, half[...], other[...])
        down_t_ref[...] = jnp.transpose(down.astype(f32)).astype(bf16)
        nhat = note[:chans, :cells].astype(f32)
        nhat_ref[...] = nhat
        pieces = note[:chans, cells:].astype(f32)
        cols_ref[...] = pieces[:, :taps] + pieces[:, taps:]
        lines = note[chans:].astype(f32)
        bias_row = lines[0:1] + lines[1:2]
        inv_ref[...] = (lines[2:3] + lines[3:4])[:, :cells]
        bias_ref[...] = jnp.transpose(jnp.broadcast_to(bias_row, (8, units)))
        fill_taps(cols_ref, (None, back_ref))
        normed_ref[...] = (nhat * cols_ref[:, KS * KS : KS * KS + 1]).astype(bf16)
        mlp_forward(normed_ref, up_t_ref, bias_ref, None, slope_ref)


def mlp_backward(cots, meta, cols, down_t, up, slope, nhat, inv, out_ref, low_ref, field_ref, sums=None):
    width = cots[0].shape[1]
    count = len(cots)
    gain = cols[:, KS * KS : KS * KS + 1]
    layer = cols[:, KS * KS + 1 : KS * KS + 2]
    for row in range(count):
        wet = meta[LAND + row].astype(f32)
        out_ref[:, row * width : (row + 1) * width] = (cots[row] * layer * wet).astype(bf16)
    units = down_t.shape[0]
    chunk = 128
    for first in range(0, units, chunk):
        part = slice(first, first + chunk)
        pregrad = jnp.dot(down_t[part], out_ref[...], preferred_element_type=f32)
        pregrad = pregrad * slope[part].astype(f32)
        low_ref[part] = pregrad.astype(bf16)
        if sums is not None:
            sums[0][part] = sum(
                pregrad[:, row * width : (row + 1) * width] for row in range(count)
            )
    featgrad = jnp.dot(up[...], low_ref[...], preferred_element_type=f32)
    gains = None
    for row in range(count):
        part = slice(row * width, (row + 1) * width)
        feat = featgrad[:, part]
        own = nhat[:, part]
        scaled = feat * gain
        mean = jnp.mean(scaled, axis=0, keepdims=True)
        cross = jnp.mean(scaled * own, axis=0, keepdims=True)
        field_ref[row] = (inv[:, part] * (scaled - mean - own * cross)).astype(bf16)
        if sums is not None:
            term = feat * own
            gains = term if gains is None else gains + term
    if sums is not None:
        sums[1][...] = gains


def turn_kernel(
    section, meta, cot, cols, down_t, up, slope, nhat, inv, field_ref, inner_ref, outer_ref, out_ref, low_ref
):
    @pl.when(meta[SECTION] == section)
    def _():
        cots = [cot[row].astype(f32) for row in range(cot.shape[0])]
        mlp_backward(cots, meta, cols, down_t, up, slope, nhat, inv, out_ref, low_ref, field_ref)
        edges(meta[ODD] == 1, field_ref, inner_ref, outer_ref)


def conv_rows(meta, field, inner, outer, cot, taps_mat, result_ref, rows_ref):
    count, chans, width = field.shape
    fill_rows(rows_ref, meta, field, inner, outer)

    def step(index, carry):
        start = pl.multiple_of(index * BLOCK, BLOCK)
        sums = taps_sum(rows_ref, taps_mat, index, count, True)
        for row in range(count):
            own = cot[row, pl.ds(start, BLOCK), :].astype(f32)
            result_ref[row, pl.ds(start, BLOCK), :] = (own + sums[row]).astype(bf16)
        return carry

    lax.fori_loop(0, chans // BLOCK, step, 0, unroll=UNROLL)


def conv_kernel(section, meta, field, inner, outer, cot, taps_mat, result_ref, rows_ref):
    @pl.when(meta[SECTION] == section)
    def _():
        conv_rows(meta, field, inner, outer, cot, taps_mat, result_ref, rows_ref)


def last_conv_kernel(meta, field, inner, outer, cot, taps_mat, result_ref, sent_ref, rows_ref):
    conv_rows(meta, field, inner, outer, cot, taps_mat, result_ref, rows_ref)
    sent_ref[...] = jnp.zeros_like(sent_ref)
    rank = jnp.int32(0)
    for local in range(result_ref.shape[0]):
        kept = jnp.bool_(False)
        for slot in range(OWNERS, meta.shape[0]):
            kept = kept | (meta[slot] == meta[OFFSET] + local)
        sent = (meta[LAND + local] == 1) & jnp.logical_not(kept)
        for place in range(CAP):

            @pl.when(sent & (rank == place))
            def _():
                sent_ref[place] = result_ref[local]

        rank = rank + sent.astype(jnp.int32)


def slots_kernel(meta, result, arrived, slots_ref):
    for slot in range(slots_ref.shape[0]):
        slots_ref[slot] = arrived[min(slot, CAP - 1)]
        for local in range(result.shape[0]):

            @pl.when(meta[OWNERS + slot] == meta[OFFSET] + local)
            def _():
                slots_ref[slot] = result[local]


def last_kernel(
    meta,
    cot_top,
    cot_2,
    cot_1,
    cot_0,
    cols,
    layer_row,
    down_t,
    down,
    up,
    slope,
    nhat,
    inv,
    hidden,
    acts,
    inner,
    outer,
    cot_ref,
    field_ref,
    field_inner_ref,
    field_outer_ref,
    keep_ref,
    near_ref,
    mate_ref,
    far_ref,
    out_ref,
    low_ref,
    bias_ref,
    gain_ref,
    rows_ref,
    packed_ref,
):
    count, chans, width = acts.shape
    units = slope.shape[0]
    odd = meta[ODD] == 1
    for section, cot in ((3, cot_top), (2, cot_2), (1, cot_1), (0, cot_0)):

        @pl.when(meta[SECTION] == section)
        def _():
            cot_ref[...] = cot[...]

    cots = [cot_ref[row].astype(f32) for row in range(count)]
    mlp_backward(
        cots, meta, cols, down_t, up, slope, nhat, inv, out_ref, low_ref, field_ref, (bias_ref, gain_ref)
    )
    edges(odd, field_ref, field_inner_ref, field_outer_ref)
    gain = cols[:, KS * KS : KS * KS + 1]
    normed = (nhat[...] * gain).astype(bf16)
    turned = (((1,), (1,)), ((), ()))
    grad_up = lax.dot_general(normed, low_ref[...], turned, preferred_element_type=f32)
    packed_ref[:chans] = grad_up
    grad_down = lax.dot_general(out_ref[...], hidden[...], turned, preferred_element_type=f32)
    packed_ref[chans : 2 * chans] = grad_down
    product = grad_down * down[...].astype(f32)
    product = sum(product[:, first : first + 128] for first in range(0, units, 128))

    fill_rows(rows_ref, meta, acts, inner, outer)
    base = 2 * chans
    shifts = [(tap_col - MARGIN) % 128 for tap_col in range(KS)]
    own = lax.broadcasted_iota(jnp.int32, (BLOCK, 128), 0)
    diagonal = own == (lax.broadcasted_iota(jnp.int32, (BLOCK, 128), 1) & (BLOCK - 1))
    for block in range(chans // BLOCK):
        start = block * BLOCK
        windows = stacked(rows_ref, start, count)
        fields = [field_ref[row, start : start + BLOCK, :].astype(f32) for row in range(count)]
        rolled = jnp.concatenate(
            [
                jnp.concatenate(
                    [pltpu.roll(field, shift, 1) if shift else field for field in fields], axis=1
                )
                for shift in shifts
            ],
            axis=0,
        ).astype(bf16)
        crossed = lax.dot_general(rolled, windows, turned, preferred_element_type=f32)
        first = base + block // 6 * 8
        lanes = slice(block % 6 * 128, block % 6 * 128 + 128)
        for tap_col in range(KS):
            part = jnp.where(diagonal, crossed[tap_col * BLOCK : (tap_col + 1) * BLOCK], 0.0)
            packed_ref[first + tap_col : first + tap_col + 1, lanes] = jnp.sum(
                part, axis=0, keepdims=True
            )
        packed_ref[first + KS : first + PLACES, lanes] = jnp.zeros((1, 128), f32)
    bias_row = jnp.sum(jnp.transpose(bias_ref[...]), axis=0, keepdims=True)
    gain_row = jnp.sum(jnp.transpose(gain_ref[...]), axis=0, keepdims=True)
    scale_row = jnp.sum(jnp.transpose(product), axis=0, keepdims=True) / layer_row[...]
    packed_ref[base + 16 :] = jnp.zeros((packed_ref.shape[0] - base - 16, units), f32)
    packed_ref[base + 16 : base + 17] = bias_row
    packed_ref[base + 17 : base + 18, :chans] = gain_row
    packed_ref[base + 17 : base + 18, 256 : 256 + chans] = scale_row
    part_rows = keep_ref.shape[0]
    for place, target in ((KEEP, keep_ref), (NEAR, near_ref), (MATE, mate_ref), (FAR, far_ref)):
        start = pl.multiple_of(meta[place] * part_rows, 8)
        target[...] = packed_ref[pl.ds(start, part_rows), :].astype(bf16)


def finish_kernel(
    scale, meta, keep, near, mate, far, kernel_ref, gain_ref, up_ref, bias_ref, down_ref, scale_ref, packed_ref
):
    part_rows = keep.shape[0]
    for place, source in ((KEEP, keep), (NEAR, near), (MATE, mate), (FAR, far)):
        start = pl.multiple_of(meta[place] * part_rows, 8)
        packed_ref[pl.ds(start, part_rows), :] = source[...].astype(f32) * scale
    chans = up_ref.shape[1]
    base = 2 * chans
    up_ref[0] = packed_ref[:chans]
    down_ref[0] = packed_ref[chans:base]
    lane = lax.broadcasted_iota(jnp.int32, (PLACES, 128), 1) >> 4
    blocks = chans // BLOCK
    for tap_row in range(KS):
        halves = []
        for first in range(0, blocks, PLACES):
            half = jnp.zeros((PLACES, 128), f32)
            for block in range(first, min(first + PLACES, blocks)):
                rows = slice(base + block // 6 * 8, base + block // 6 * 8 + 8)
                part = packed_ref[rows, block % 6 * 128 : block % 6 * 128 + 128]
                shift = (block - first - tap_row) * BLOCK % 128
                if shift:
                    part = pltpu.roll(part, shift, 1)
                half = jnp.where(lane == block - first, part, half)
            halves.append(half)
        line = jnp.concatenate(halves, axis=1)
        kernel_ref[0, tap_row * KS : (tap_row + 1) * KS] = line[:KS, :chans]
    bias_ref[...] = packed_ref[base + 16 : base + 17]
    gain_ref[...] = packed_ref[base + 17 : base + 18, :chans]
    scale_ref[...] = packed_ref[base + 17 : base + 18, 256 : 256 + chans]


def added(*values):
    return sum(value.astype(f32) for value in values).astype(bf16)


def body(acts, cot_top, land, owners, dw_kernel, ln_gain, w_up, b_up, w_down, layer_scale):
    source = acts[0]
    count, chans, width = source.shape
    units = w_up.shape[2]
    cells = count * width
    tile_now = lax.axis_index("tile")
    section_now = lax.axis_index("section")
    scale = 1.0 / math.sqrt(lax.axis_size("tile") * cells)
    core, x, z = split_tile(tile_now)
    bit_x, bit_z = (x + 1) // 2 % 2, (z + 1) // 2 % 2
    bit = jnp.where(core == 0, bit_x, bit_z)
    mate_bit = jnp.where(core == 0, bit_z, bit_x)
    numbers = [
        section_now,
        core,
        2 * core + bit,
        2 * core + 1 - bit,
        2 * (1 - core) + mate_bit,
        2 * (1 - core) + 1 - mate_bit,
        tile_now * count,
        jnp.where((tile_now == 0) | (tile_now == TILES - 1), 0, 1),
    ]
    meta = jnp.concatenate([jnp.stack(numbers).astype(jnp.int32), land, owners])

    odd = core == 1
    head, tail = source[:MARGIN], source[count - MARGIN :]
    acts_inner, acts_outer = halo(jnp.where(odd, head, tail), jnp.where(odd, tail, head))
    up, down = w_up[0], w_down[0]
    swaps = [(section, section ^ 1) for section in range(SECTIONS)]
    taps_shape = shape((chans // BLOCK, KS * BLOCK, 256), bf16)
    weights_t = shape((units, chans), bf16)
    cols_shape = shape((chans, 64), f32)
    cols, forth, back, up_t, down_t, bias = call(
        prepare_kernel,
        (cols_shape, taps_shape, taps_shape, weights_t, weights_t, shape((units, 8), f32)),
        0,
        (dw_kernel[0], ln_gain, layer_scale, b_up, up, down),
        (pltpu.VMEM((64, chans), f32),),
        cost=(10**9, 10**7),
    )
    half = lax.ppermute(jnp.where(odd, down, up), "section", swaps)

    padded = pltpu.VMEM((count + PLACES - 1, chans, width), bf16)
    nhat_shape, inv_shape = shape((chans, cells), f32), shape((1, cells), f32)
    unit_shape = shape((units, cells), bf16)
    nhat, inv, hidden, slope, own_note = call(
        forward_kernel,
        (nhat_shape, inv_shape, unit_shape, unit_shape, shape((chans + BLOCK, units), bf16)),
        1,
        (meta, source, acts_inner, acts_outer, forth, cols, up_t, bias, b_up),
        (padded, pltpu.VMEM((chans, cells), f32), pltpu.VMEM((chans, cells), bf16)),
    )
    note = lax.ppermute(own_note, "section", swaps)

    rows_shape = shape((count, chans, width), bf16)
    edge_shape = shape((MARGIN, chans, width), bf16)
    outgrads = pltpu.VMEM((chans, cells), bf16)
    lowgrads = pltpu.VMEM((units, cells), bf16)

    def turn_field(plane, cot, params):
        field_cols, field_down_t, field_up, field_slope, field_nhat, field_inv, _ = params
        return call(
            functools.partial(turn_kernel, plane),
            (rows_shape, edge_shape, edge_shape),
            1,
            (meta, cot, field_cols, field_down_t, field_up, field_slope, field_nhat, field_inv),
            (outgrads, lowgrads),
        )

    def turn_input(plane, cot, params, field, inner, outer):
        return call(
            functools.partial(conv_kernel, plane),
            rows_shape,
            1,
            (meta, field, inner, outer, cot, params[-1]),
            (padded,),
        )

    top = SECTIONS - 1
    params = (cols, down_t, up, slope, nhat, inv, back)
    field, inner, outer = turn_field(top, cot_top, params)
    half, field = lax.optimization_barrier((half, field))
    inner, outer = halo(inner, outer)
    other = moved(half, ("", ""), True)
    adopted = call(
        adopt_kernel,
        (nhat_shape, inv_shape, unit_shape, cols_shape, taps_shape, shape((chans, units), bf16))
        + (weights_t, weights_t, shape((units, 8), f32)),
        1,
        (meta, note, half, other),
        (pltpu.VMEM((chans, cells), bf16),),
        cost=(10**9, 10**7),
    )
    next_nhat, next_inv, next_slope, next_cols, next_back, next_up, next_down_t = adopted[:7]
    adopted = (next_cols, next_down_t, next_up, next_slope, next_nhat, next_inv, next_back)
    cot_2 = turn_input(top, cot_top, params, field, inner, outer)
    own_2 = lax.ppermute(cot_2, "section", swaps)

    field, inner, outer = turn_field(top, cot_2, adopted)
    inner, outer = halo(inner, outer)
    cot_1 = turn_input(top, cot_2, adopted, field, inner, outer)
    cot_1 = lax.ppermute(cot_1, "section", [(0, top), (top, 0), (1, 2), (2, 1)])
    own_1 = lax.ppermute(cot_1, "section", swaps)

    field, inner, outer = turn_field(0, cot_1, adopted)
    inner, outer = halo(inner, outer)
    cot_0 = turn_input(0, cot_1, adopted, field, inner, outer)

    part = shape(((2 * chans + 32) // 4, units), bf16)
    cot_own, field, inner, outer, keep, near, mate, far = call(
        last_kernel,
        (rows_shape, rows_shape, edge_shape, edge_shape, part, part, part, part),
        1,
        (meta, cot_top, own_2, own_1, cot_0, cols, layer_scale, down_t, down, up, slope, nhat, inv, hidden)
        + (source, acts_inner, acts_outer),
        (
            outgrads,
            lowgrads,
            pltpu.VMEM((units, width), f32),
            pltpu.VMEM((chans, width), f32),
            padded,
            pltpu.VMEM((2 * chans + 32, units), f32),
        ),
    )
    far = moved(far, ("z0", "x0"), True)
    near = moved(near, ("x0", "z0"), False)
    mate = moved(mate, ("", ""), True)
    total = added(keep, near, mate, far)
    orders = (("x1", "z1"), ("z0", "z2"), ("z1", "x0"), ("z2", "x1"))
    total, inner, outer = lax.optimization_barrier((total, inner, outer))
    total = added(total, moved(total, orders[0], False))
    inner, outer = halo(inner, outer)
    total, inner, outer = lax.optimization_barrier((total, inner, outer))
    total = added(total, moved(total, orders[1], False))
    result, sent = call(
        last_conv_kernel,
        (rows_shape, shape((CAP, chans, width), bf16)),
        1,
        (meta, field, inner, outer, cot_own, back),
        (padded,),
    )
    total, result, sent = lax.optimization_barrier((total, result, sent))
    total = added(total, moved(total, orders[2], False))
    arrived = lax.ppermute(sent, "tile", [(tile, (tile + 1) % TILES) for tile in range(TILES)])
    total = added(total, moved(total, orders[3], False))
    total, arrived = lax.optimization_barrier((total, arrived))
    slotted = call(
        slots_kernel,
        shape((owners.shape[0], chans, width), bf16),
        1,
        (meta, result, arrived),
    )
    far = moved(total, ("x0", "z0"), True)
    near = moved(total, ("x0", "z0"), False)
    mate = moved(total, ("", ""), True)
    grads = call(
        functools.partial(finish_kernel, scale),
        (
            shape((1, KS * KS, chans), f32),
            shape((1, chans), f32),
            shape((1, chans, units), f32),
            shape((1, units), f32),
            shape((1, chans, units), f32),
            shape((1, chans), f32),
        ),
        1,
        (meta, total, near, mate, far),
        (pltpu.VMEM((2 * chans + 32, units), f32),),
    )

    grad_kernel, grad_gain, grad_up, grad_bias, grad_down, grad_scale = grads
    return (
        slotted[None],
        grad_kernel,
        grad_gain,
        grad_up,
        grad_bias,
        grad_down,
        grad_scale,
    )


def solution(mesh):
    in_specs = (
        P("section", "tile", None, None),
        P("tile", None, None),
        P("tile"),
        P("tile"),
        P("section", None, None),
        P("section", None),
        P("section", None, None),
        P("section", None),
        P("section", None, None),
        P("section", None),
    )
    out_specs = (
        P("section", "tile", None, None),
        P("section", None, None),
        P("section", None),
        P("section", None, None),
        P("section", None),
        P("section", None, None),
        P("section", None),
    )
    return jax.shard_map(body, mesh=mesh, in_specs=in_specs, out_specs=out_specs, check_vma=False)
```

```python
import functools
import math

import jax
import jax.numpy as jnp
from jax import lax
from jax.experimental import pallas as pl
from jax.experimental.pallas import tpu as pltpu
from jax.sharding import PartitionSpec as P

KS = 7
CAP = 2
SECTIONS = 4
TILES = 64
MARGIN = 3
BLOCK = 16
UNROLL = 4

norm_eps = 1e-06
tanh_root = math.sqrt(2.0 / math.pi)
cubic_coef = 0.044715

f32 = jnp.float32
bf16 = jnp.bfloat16

SECTION, ODD, KEEP, NEAR, MATE, FAR, OFFSET, INSIDE, LAND = range(9)
PLACES = 8
OWNERS = LAND + 5


def split_tile(tile):
    return tile % 2, tile // 2 % 4, tile // 8


def flip_x0(x):
    return x ^ 1


def flip_x1(x):
    return 3 - x


def flip_z0(z):
    return z ^ 1


def flip_z1(z):
    return 3 - z if z < 4 else 11 - z


def flip_z2(z):
    return 7 - z


flips = {"x0": flip_x0, "x1": flip_x1, "z0": flip_z0, "z1": flip_z1, "z2": flip_z2}


def moved(value, dims, swap):
    pairs = []
    for tile in range(TILES):
        core, x, z = split_tile(tile)
        dim = dims[core]
        if dim in ("x0", "x1"):
            x = flips[dim](x)
        elif dim:
            z = flips[dim](z)
        core = 1 - core if swap else core
        pairs.append((tile, z * 8 + x * 2 + core))
    return lax.ppermute(value, "tile", pairs)


def halo(inner, outer):
    across = [(tile, (tile + 1 if tile % 2 else tile - 1) % TILES) for tile in range(TILES)]
    outer = lax.ppermute(outer, "tile", across)
    inner = lax.ppermute(inner, "tile", [(tile, tile ^ 1) for tile in range(TILES)])
    return inner, outer


def call(body, out_shape, smem, operands, scratch=(), cost=(0, 0)):
    spec = [pl.BlockSpec(memory_space=pltpu.SMEM)] * smem
    spec += [pl.BlockSpec(memory_space=pltpu.VMEM)] * (len(operands) - smem)
    outs = jax.tree.map(lambda _: pl.BlockSpec(memory_space=pltpu.VMEM), out_shape)
    return pl.pallas_call(
        body,
        out_shape=out_shape,
        in_specs=spec,
        out_specs=outs,
        scratch_shapes=list(scratch),
        compiler_params=pltpu.CompilerParams(vmem_limit_bytes=32 * 1024 * 1024),
        cost_estimate=pl.CostEstimate(flops=cost[0], bytes_accessed=cost[1], transcendentals=0),
    )(*operands)


def shape(dims, dtype):
    return jax.ShapeDtypeStruct(dims, dtype)


def fill_rows(rows_ref, meta, own, inner, outer):
    count = own.shape[0]
    odd = meta[ODD] == 1
    far_rows = jnp.where(meta[INSIDE] == 1, outer[...], jnp.zeros_like(outer))
    near_rows = inner[...]
    rows_ref[MARGIN : MARGIN + count] = own[...]
    rows_ref[:MARGIN] = jnp.where(odd, near_rows, far_rows)
    rows_ref[MARGIN + count : 2 * MARGIN + count] = jnp.where(odd, far_rows, near_rows)
    rows_ref[2 * MARGIN + count :] = jnp.zeros((1,) + own.shape[1:], bf16)


def edges(odd, value_ref, inner_ref, outer_ref):
    count = value_ref.shape[0]
    head = value_ref[:MARGIN]
    tail = value_ref[count - MARGIN :]
    inner_ref[...] = jnp.where(odd, head, tail)
    outer_ref[...] = jnp.where(odd, tail, head)


def fill_taps(cols, targets):
    high = cols[...].astype(bf16)
    low = (cols[...] - high.astype(f32)).astype(bf16)
    chans, taps = cols.shape
    wide = KS * 128
    tap = lax.broadcasted_iota(jnp.int32, (taps, wide), 0)
    place = lax.broadcasted_iota(jnp.int32, (taps, wide), 1)
    tap_col, tap_row = place >> 7, (place >> 4) & (PLACES - 1)
    own = lax.broadcasted_iota(jnp.int32, (chans, wide), 0) & (BLOCK - 1)
    diagonal = own == (lax.broadcasted_iota(jnp.int32, (chans, wide), 1) & (BLOCK - 1))
    for target, row in zip(targets, (tap_row, KS - 1 - tap_row)):
        if target is None:
            continue
        hit = (tap == row * KS + tap_col) & (tap_row < KS)
        spread = jnp.where(hit, 1.0, 0.0).astype(bf16)
        for half, value in enumerate((high, low)):
            filled = jnp.dot(value, spread, preferred_element_type=f32)
            filled = jnp.where(diagonal, filled, 0.0).astype(bf16)
            for block in range(chans // BLOCK):
                for col in range(KS):
                    target[
                        block, col * BLOCK : (col + 1) * BLOCK, half * 128 : (half + 1) * 128
                    ] = filled[block * BLOCK : (block + 1) * BLOCK, col * 128 : (col + 1) * 128]


def prepare_kernel(
    kernel, gain, layer, bias, up, down, cols, forth_ref, back_ref, up_t_ref, down_t_ref, bias_ref, lines_ref
):
    lines_ref[...] = jnp.zeros_like(lines_ref)
    lines_ref[: KS * KS] = kernel[...]
    lines_ref[KS * KS : KS * KS + 1] = gain[...]
    lines_ref[KS * KS + 1 : KS * KS + 2] = layer[...]
    cols[...] = jnp.transpose(lines_ref[...])
    up_t_ref[...] = jnp.transpose(up[...].astype(f32)).astype(bf16)
    down_t_ref[...] = jnp.transpose(down[...].astype(f32)).astype(bf16)
    bias_ref[...] = jnp.transpose(jnp.broadcast_to(bias[...], (8, bias.shape[1])))
    fill_taps(cols, (forth_ref, back_ref))


def stacked(rows_ref, start, count):
    rows = [rows_ref[row, pl.ds(start, BLOCK), :] for row in range(count + PLACES - 1)]
    return jnp.concatenate(
        [jnp.concatenate(rows[place : place + count], axis=1) for place in range(PLACES)], axis=0
    )


def taps_sum(rows_ref, taps_mat, block, count, backward):
    windows = stacked(rows_ref, pl.multiple_of(block * BLOCK, BLOCK), count)
    parts = jnp.dot(
        taps_mat[block], jnp.concatenate([windows, windows], axis=0), preferred_element_type=f32
    )
    sums = []
    for row in range(count):
        total = None
        for tap_col in range(KS):
            shift = (tap_col - MARGIN if backward else MARGIN - tap_col) % 128
            part = parts[tap_col * BLOCK : (tap_col + 1) * BLOCK, row * 128 : (row + 1) * 128]
            if shift:
                part = pltpu.roll(part, shift, 1)
            total = part if total is None else total + part
        sums.append(total)
    return sums


def forward_kernel(
    meta, acts, inner, outer, taps_mat, cols, up_t, bias, bias_row, nhat_ref, inv_ref, hidden_ref, slope_ref, note_ref, rows_ref, field_ref, normed_ref
):
    count, chans, width = acts.shape
    fill_rows(rows_ref, meta, acts, inner, outer)

    def step(index, carry):
        start = pl.multiple_of(index * BLOCK, BLOCK)
        sums = taps_sum(rows_ref, taps_mat, index, count, False)
        for row in range(count):
            field_ref[pl.ds(start, BLOCK), row * width : (row + 1) * width] = sums[row]
        return carry

    lax.fori_loop(0, chans // BLOCK, step, 0, unroll=UNROLL)
    gain = cols[:, KS * KS : KS * KS + 1]
    for row in range(count):
        part = slice(row * width, (row + 1) * width)
        field = field_ref[:, part]
        center = field - jnp.mean(field, axis=0, keepdims=True)
        inverse = 1.0 / jnp.sqrt(jnp.mean(center * center, axis=0, keepdims=True) + norm_eps)
        nhat = center * inverse
        nhat_ref[:, part] = nhat
        inv_ref[:, part] = inverse
        normed_ref[:, part] = (nhat * gain).astype(bf16)
    cells = count * width
    note_ref[:chans, :cells] = nhat_ref[...].astype(bf16)
    high, low = two_parts(cols[...])
    note_ref[:chans, cells:] = jnp.concatenate([high, low], axis=1).astype(bf16)
    parts = two_parts(bias_row[...])
    padding = jnp.zeros((1, bias_row.shape[1] - cells), f32)
    parts += two_parts(jnp.concatenate([inv_ref[...], padding], axis=1))
    rest = jnp.zeros((BLOCK - len(parts), bias_row.shape[1]), f32)
    note_ref[chans:] = jnp.concatenate([*parts, rest]).astype(bf16)
    mlp_forward(normed_ref, up_t, bias, hidden_ref, slope_ref)


def two_parts(value):
    high = value.astype(bf16).astype(f32)
    return [high, value - high]


def mlp_forward(normed_ref, up_t, bias, hidden_ref, slope_ref):
    units = up_t.shape[0]
    chunk = 128
    for first in range(0, units, chunk):
        part = slice(first, first + chunk)
        preact = jnp.dot(up_t[part], normed_ref[...], preferred_element_type=f32) + bias[part, :1]
        square = preact * preact
        hyper = jnp.tanh(preact * (tanh_root + tanh_root * cubic_coef * square))
        half = 0.5 + 0.5 * hyper
        if hidden_ref is not None:
            hidden_ref[part] = (preact * half).astype(bf16)
        slope = half * (
            1.0 + preact * (1.0 - hyper) * (tanh_root + 3.0 * cubic_coef * tanh_root * square)
        )
        slope_ref[part] = slope.astype(bf16)


def adopt_kernel(
    meta, note, half, other, nhat_ref, inv_ref, slope_ref, cols_ref, back_ref, up_ref, down_t_ref, up_t_ref, bias_ref, normed_ref
):
    chans, cells = nhat_ref.shape
    units = slope_ref.shape[0]
    taps = cols_ref.shape[1]

    @pl.when((meta[SECTION] == SECTIONS - 1) | (meta[SECTION] == 0))
    def _():
        odd = meta[ODD] == 1
        up = jnp.where(odd, other[...], half[...])
        up_ref[...] = up
        up_t_ref[...] = jnp.transpose(up.astype(f32)).astype(bf16)
        down = jnp.where(odd, half[...], other[...])
        down_t_ref[...] = jnp.transpose(down.astype(f32)).astype(bf16)
        nhat = note[:chans, :cells].astype(f32)
        nhat_ref[...] = nhat
        pieces = note[:chans, cells:].astype(f32)
        cols_ref[...] = pieces[:, :taps] + pieces[:, taps:]
        lines = note[chans:].astype(f32)
        bias_row = lines[0:1] + lines[1:2]
        inv_ref[...] = (lines[2:3] + lines[3:4])[:, :cells]
        bias_ref[...] = jnp.transpose(jnp.broadcast_to(bias_row, (8, units)))
        fill_taps(cols_ref, (None, back_ref))
        normed_ref[...] = (nhat * cols_ref[:, KS * KS : KS * KS + 1]).astype(bf16)
        mlp_forward(normed_ref, up_t_ref, bias_ref, None, slope_ref)


def mlp_backward(cots, meta, cols, down_t, up, slope, nhat, inv, out_ref, low_ref, field_ref, sums=None):
    width = cots[0].shape[1]
    count = len(cots)
    gain = cols[:, KS * KS : KS * KS + 1]
    layer = cols[:, KS * KS + 1 : KS * KS + 2]
    for row in range(count):
        wet = meta[LAND + row].astype(f32)
        out_ref[:, row * width : (row + 1) * width] = (cots[row] * layer * wet).astype(bf16)
    units = down_t.shape[0]
    chunk = 128
    for first in range(0, units, chunk):
        part = slice(first, first + chunk)
        pregrad = jnp.dot(down_t[part], out_ref[...], preferred_element_type=f32)
        pregrad = pregrad * slope[part].astype(f32)
        low_ref[part] = pregrad.astype(bf16)
        if sums is not None:
            sums[0][part] = sum(
                pregrad[:, row * width : (row + 1) * width] for row in range(count)
            )
    featgrad = jnp.dot(up[...], low_ref[...], preferred_element_type=f32)
    gains = None
    for row in range(count):
        part = slice(row * width, (row + 1) * width)
        feat = featgrad[:, part]
        own = nhat[:, part]
        scaled = feat * gain
        mean = jnp.mean(scaled, axis=0, keepdims=True)
        cross = jnp.mean(scaled * own, axis=0, keepdims=True)
        field_ref[row] = (inv[:, part] * (scaled - mean - own * cross)).astype(bf16)
        if sums is not None:
            term = feat * own
            gains = term if gains is None else gains + term
    if sums is not None:
        sums[1][...] = gains


def turn_kernel(
    section, meta, cot, cols, down_t, up, slope, nhat, inv, field_ref, inner_ref, outer_ref, out_ref, low_ref
):
    @pl.when(meta[SECTION] == section)
    def _():
        cots = [cot[row].astype(f32) for row in range(cot.shape[0])]
        mlp_backward(cots, meta, cols, down_t, up, slope, nhat, inv, out_ref, low_ref, field_ref)
        edges(meta[ODD] == 1, field_ref, inner_ref, outer_ref)


def conv_rows(meta, field, inner, outer, cot, taps_mat, result_ref, rows_ref):
    count, chans, width = field.shape
    fill_rows(rows_ref, meta, field, inner, outer)

    def step(index, carry):
        start = pl.multiple_of(index * BLOCK, BLOCK)
        sums = taps_sum(rows_ref, taps_mat, index, count, True)
        for row in range(count):
            own = cot[row, pl.ds(start, BLOCK), :].astype(f32)
            result_ref[row, pl.ds(start, BLOCK), :] = (own + sums[row]).astype(bf16)
        return carry

    lax.fori_loop(0, chans // BLOCK, step, 0, unroll=UNROLL)


def conv_kernel(section, meta, field, inner, outer, cot, taps_mat, result_ref, rows_ref):
    @pl.when(meta[SECTION] == section)
    def _():
        conv_rows(meta, field, inner, outer, cot, taps_mat, result_ref, rows_ref)


def middle_kernel(
    plane,
    meta,
    field,
    inner,
    outer,
    cot,
    taps_mat,
    cols,
    down_t,
    up,
    slope,
    nhat,
    inv,
    result_ref,
    field_ref,
    inner_ref,
    outer_ref,
    rows_ref,
    out_ref,
    low_ref,
):
    @pl.when(meta[SECTION] == plane)
    def _():
        conv_rows(meta, field, inner, outer, cot, taps_mat, result_ref, rows_ref)
        cots = [result_ref[row].astype(f32) for row in range(result_ref.shape[0])]
        mlp_backward(cots, meta, cols, down_t, up, slope, nhat, inv, out_ref, low_ref, field_ref)
        edges(meta[ODD] == 1, field_ref, inner_ref, outer_ref)


def last_conv_kernel(meta, field, inner, outer, cot, taps_mat, result_ref, sent_ref, rows_ref):
    conv_rows(meta, field, inner, outer, cot, taps_mat, result_ref, rows_ref)
    sent_ref[...] = jnp.zeros_like(sent_ref)
    rank = jnp.int32(0)
    for local in range(result_ref.shape[0]):
        kept = jnp.bool_(False)
        for slot in range(OWNERS, meta.shape[0]):
            kept = kept | (meta[slot] == meta[OFFSET] + local)
        sent = (meta[LAND + local] == 1) & jnp.logical_not(kept)
        for place in range(CAP):

            @pl.when(sent & (rank == place))
            def _():
                sent_ref[place] = result_ref[local]

        rank = rank + sent.astype(jnp.int32)


def slots_kernel(meta, result, arrived, slots_ref):
    for slot in range(slots_ref.shape[0]):
        slots_ref[slot] = arrived[min(slot, CAP - 1)]
        for local in range(result.shape[0]):

            @pl.when(meta[OWNERS + slot] == meta[OFFSET] + local)
            def _():
                slots_ref[slot] = result[local]


def last_kernel(
    meta,
    cot_top,
    cot_2,
    cot_1,
    turn_field,
    turn_inner,
    turn_outer,
    turn_cot,
    turn_mat,
    cols,
    layer_row,
    down_t,
    down,
    up,
    slope,
    nhat,
    inv,
    hidden,
    acts,
    inner,
    outer,
    cot_ref,
    field_ref,
    field_inner_ref,
    field_outer_ref,
    keep_ref,
    near_ref,
    mate_ref,
    far_ref,
    out_ref,
    low_ref,
    bias_ref,
    gain_ref,
    rows_ref,
    packed_ref,
):
    count, chans, width = acts.shape
    units = slope.shape[0]
    odd = meta[ODD] == 1
    for section, cot in ((3, cot_top), (2, cot_2), (1, cot_1)):

        @pl.when(meta[SECTION] == section)
        def _():
            cot_ref[...] = cot[...]

    @pl.when(meta[SECTION] == 0)
    def _():
        conv_rows(meta, turn_field, turn_inner, turn_outer, turn_cot, turn_mat, cot_ref, rows_ref)

    cots = [cot_ref[row].astype(f32) for row in range(count)]
    mlp_backward(
        cots, meta, cols, down_t, up, slope, nhat, inv, out_ref, low_ref, field_ref, (bias_ref, gain_ref)
    )
    edges(odd, field_ref, field_inner_ref, field_outer_ref)
    gain = cols[:, KS * KS : KS * KS + 1]
    normed = (nhat[...] * gain).astype(bf16)
    turned = (((1,), (1,)), ((), ()))
    grad_up = lax.dot_general(normed, low_ref[...], turned, preferred_element_type=f32)
    packed_ref[:chans] = grad_up
    grad_down = lax.dot_general(out_ref[...], hidden[...], turned, preferred_element_type=f32)
    packed_ref[chans : 2 * chans] = grad_down
    product = grad_down * down[...].astype(f32)
    product = sum(product[:, first : first + 128] for first in range(0, units, 128))

    fill_rows(rows_ref, meta, acts, inner, outer)
    base = 2 * chans
    shifts = [(tap_col - MARGIN) % 128 for tap_col in range(KS)]
    own = lax.broadcasted_iota(jnp.int32, (BLOCK, 128), 0)
    diagonal = own == (lax.broadcasted_iota(jnp.int32, (BLOCK, 128), 1) & (BLOCK - 1))
    for block in range(chans // BLOCK):
        start = block * BLOCK
        windows = stacked(rows_ref, start, count)
        fields = [field_ref[row, start : start + BLOCK, :].astype(f32) for row in range(count)]
        rolled = jnp.concatenate(
            [
                jnp.concatenate(
                    [pltpu.roll(field, shift, 1) if shift else field for field in fields], axis=1
                )
                for shift in shifts
            ],
            axis=0,
        ).astype(bf16)
        crossed = lax.dot_general(rolled, windows, turned, preferred_element_type=f32)
        first = base + block // 6 * 8
        lanes = slice(block % 6 * 128, block % 6 * 128 + 128)
        for tap_col in range(KS):
            part = jnp.where(diagonal, crossed[tap_col * BLOCK : (tap_col + 1) * BLOCK], 0.0)
            packed_ref[first + tap_col : first + tap_col + 1, lanes] = jnp.sum(
                part, axis=0, keepdims=True
            )
        packed_ref[first + KS : first + PLACES, lanes] = jnp.zeros((1, 128), f32)
    bias_row = jnp.sum(jnp.transpose(bias_ref[...]), axis=0, keepdims=True)
    gain_row = jnp.sum(jnp.transpose(gain_ref[...]), axis=0, keepdims=True)
    scale_row = jnp.sum(jnp.transpose(product), axis=0, keepdims=True) / layer_row[...]
    packed_ref[base + 16 :] = jnp.zeros((packed_ref.shape[0] - base - 16, units), f32)
    packed_ref[base + 16 : base + 17] = bias_row
    packed_ref[base + 17 : base + 18, :chans] = gain_row
    packed_ref[base + 17 : base + 18, 256 : 256 + chans] = scale_row
    part_rows = keep_ref.shape[0]
    for place, target in ((KEEP, keep_ref), (NEAR, near_ref), (MATE, mate_ref), (FAR, far_ref)):
        start = pl.multiple_of(meta[place] * part_rows, 8)
        target[...] = packed_ref[pl.ds(start, part_rows), :].astype(bf16)


def finish_kernel(
    scale, meta, keep, near, mate, far, kernel_ref, gain_ref, up_ref, bias_ref, down_ref, scale_ref, packed_ref
):
    part_rows = keep.shape[0]
    for place, source in ((KEEP, keep), (NEAR, near), (MATE, mate), (FAR, far)):
        start = pl.multiple_of(meta[place] * part_rows, 8)
        packed_ref[pl.ds(start, part_rows), :] = source[...].astype(f32) * scale
    chans = up_ref.shape[1]
    base = 2 * chans
    up_ref[0] = packed_ref[:chans]
    down_ref[0] = packed_ref[chans:base]
    lane = lax.broadcasted_iota(jnp.int32, (PLACES, 128), 1) >> 4
    blocks = chans // BLOCK
    for tap_row in range(KS):
        halves = []
        for first in range(0, blocks, PLACES):
            half = jnp.zeros((PLACES, 128), f32)
            for block in range(first, min(first + PLACES, blocks)):
                rows = slice(base + block // 6 * 8, base + block // 6 * 8 + 8)
                part = packed_ref[rows, block % 6 * 128 : block % 6 * 128 + 128]
                shift = (block - first - tap_row) * BLOCK % 128
                if shift:
                    part = pltpu.roll(part, shift, 1)
                half = jnp.where(lane == block - first, part, half)
            halves.append(half)
        line = jnp.concatenate(halves, axis=1)
        for tap_col in range(KS):
            kernel_ref[tap_row * KS + tap_col] = line[tap_col : tap_col + 1, :chans]
    bias_ref[...] = packed_ref[base + 16 : base + 17]
    gain_ref[...] = packed_ref[base + 17 : base + 18, :chans]
    scale_ref[...] = packed_ref[base + 17 : base + 18, 256 : 256 + chans]


def added(*values):
    return sum(value.astype(f32) for value in values).astype(bf16)


def body(acts, cot_top, land, owners, dw_kernel, ln_gain, w_up, b_up, w_down, layer_scale):
    source = acts[0]
    count, chans, width = source.shape
    units = w_up.shape[2]
    cells = count * width
    tile_now = lax.axis_index("tile")
    section_now = lax.axis_index("section")
    scale = 1.0 / math.sqrt(lax.axis_size("tile") * cells)
    core, x, z = split_tile(tile_now)
    bit_x, bit_z = (x + 1) // 2 % 2, (z + 1) // 2 % 2
    bit = jnp.where(core == 0, bit_x, bit_z)
    mate_bit = jnp.where(core == 0, bit_z, bit_x)
    numbers = [
        section_now,
        core,
        2 * core + bit,
        2 * core + 1 - bit,
        2 * (1 - core) + mate_bit,
        2 * (1 - core) + 1 - mate_bit,
        tile_now * count,
        jnp.where((tile_now == 0) | (tile_now == TILES - 1), 0, 1),
    ]
    meta = jnp.concatenate([jnp.stack(numbers).astype(jnp.int32), land, owners])

    odd = core == 1
    head, tail = source[:MARGIN], source[count - MARGIN :]
    acts_inner, acts_outer = halo(jnp.where(odd, head, tail), jnp.where(odd, tail, head))
    up, down = w_up[0], w_down[0]
    swaps = [(section, section ^ 1) for section in range(SECTIONS)]
    taps_shape = shape((chans // BLOCK, KS * BLOCK, 256), bf16)
    weights_t = shape((units, chans), bf16)
    cols_shape = shape((chans, 64), f32)
    cols, forth, back, up_t, down_t, bias = call(
        prepare_kernel,
        (cols_shape, taps_shape, taps_shape, weights_t, weights_t, shape((units, 8), f32)),
        0,
        (dw_kernel[0], ln_gain, layer_scale, b_up, up, down),
        (pltpu.VMEM((64, chans), f32),),
        cost=(10**9, 10**7),
    )
    half = lax.ppermute(jnp.where(odd, down, up), "section", swaps)

    padded = pltpu.VMEM((count + PLACES - 1, chans, width), bf16)
    nhat_shape, inv_shape = shape((chans, cells), f32), shape((1, cells), f32)
    unit_shape = shape((units, cells), bf16)
    nhat, inv, hidden, slope, own_note = call(
        forward_kernel,
        (nhat_shape, inv_shape, unit_shape, unit_shape, shape((chans + BLOCK, units), bf16)),
        1,
        (meta, source, acts_inner, acts_outer, forth, cols, up_t, bias, b_up),
        (padded, pltpu.VMEM((chans, cells), f32), pltpu.VMEM((chans, cells), bf16)),
    )
    note = lax.ppermute(own_note, "section", swaps)

    rows_shape = shape((count, chans, width), bf16)
    edge_shape = shape((MARGIN, chans, width), bf16)
    outgrads = pltpu.VMEM((chans, cells), bf16)
    lowgrads = pltpu.VMEM((units, cells), bf16)

    def turn_field(plane, cot, params):
        field_cols, field_down_t, field_up, field_slope, field_nhat, field_inv = params
        return call(
            functools.partial(turn_kernel, plane),
            (rows_shape, edge_shape, edge_shape),
            1,
            (meta, cot, field_cols, field_down_t, field_up, field_slope, field_nhat, field_inv),
            (outgrads, lowgrads),
        )

    top = SECTIONS - 1
    field, inner, outer = turn_field(top, cot_top, (cols, down_t, up, slope, nhat, inv))
    half, field = lax.optimization_barrier((half, field))
    inner, outer = halo(inner, outer)
    other = moved(half, ("", ""), True)
    adopted = call(
        adopt_kernel,
        (nhat_shape, inv_shape, unit_shape, cols_shape, taps_shape, shape((chans, units), bf16))
        + (weights_t, weights_t, shape((units, 8), f32)),
        1,
        (meta, note, half, other),
        (pltpu.VMEM((chans, cells), bf16),),
        cost=(10**9, 10**7),
    )
    next_nhat, next_inv, next_slope, next_cols, next_back, next_up, next_down_t = adopted[:7]
    cot_2, field, inner, outer = call(
        functools.partial(middle_kernel, top),
        (rows_shape, rows_shape, edge_shape, edge_shape),
        1,
        (meta, field, inner, outer, cot_top, back, next_cols, next_down_t, next_up)
        + (next_slope, next_nhat, next_inv),
        (padded, outgrads, lowgrads),
    )
    own_2 = lax.ppermute(cot_2, "section", swaps)
    inner, outer = halo(inner, outer)
    cot_1 = call(
        functools.partial(conv_kernel, top),
        rows_shape,
        1,
        (meta, field, inner, outer, cot_2, next_back),
        (padded,),
    )
    cot_1 = lax.ppermute(cot_1, "section", [(0, top), (top, 0), (1, 2), (2, 1)])
    own_1 = lax.ppermute(cot_1, "section", swaps)

    adopted = (next_cols, next_down_t, next_up, next_slope, next_nhat, next_inv)
    field, inner, outer = turn_field(0, cot_1, adopted)
    inner, outer = halo(inner, outer)

    part = shape(((2 * chans + 32) // 4, units), bf16)
    cot_own, field, inner, outer, keep, near, mate, far = call(
        last_kernel,
        (rows_shape, rows_shape, edge_shape, edge_shape, part, part, part, part),
        1,
        (meta, cot_top, own_2, own_1, field, inner, outer, cot_1, next_back, cols, layer_scale, down_t, down, up, slope, nhat, inv, hidden)
        + (source, acts_inner, acts_outer),
        (
            outgrads,
            lowgrads,
            pltpu.VMEM((units, width), f32),
            pltpu.VMEM((chans, width), f32),
            padded,
            pltpu.VMEM((2 * chans + 32, units), f32),
        ),
    )
    far = moved(far, ("z0", "x0"), True)
    near = moved(near, ("x0", "z0"), False)
    mate = moved(mate, ("", ""), True)
    total = added(keep, near, mate, far)
    orders = (("x1", "z1"), ("z0", "z2"), ("z1", "x0"), ("z2", "x1"))
    total = added(total, moved(total, orders[0], False))
    total, inner, outer = lax.optimization_barrier((total, inner, outer))
    total = added(total, moved(total, orders[1], False))
    inner, outer = halo(inner, outer)
    total, inner, outer = lax.optimization_barrier((total, inner, outer))
    total = added(total, moved(total, orders[2], False))
    result, sent = call(
        last_conv_kernel,
        (rows_shape, shape((CAP, chans, width), bf16)),
        1,
        (meta, field, inner, outer, cot_own, back),
        (padded,),
    )
    total, result, sent = lax.optimization_barrier((total, result, sent))
    total = added(total, moved(total, orders[3], False))
    arrived = lax.ppermute(sent, "tile", [(tile, (tile + 1) % TILES) for tile in range(TILES)])
    total, arrived = lax.optimization_barrier((total, arrived))
    slotted = call(
        slots_kernel,
        shape((owners.shape[0], chans, width), bf16),
        1,
        (meta, result, arrived),
    )
    far = moved(total, ("x0", "z0"), True)
    near = moved(total, ("x0", "z0"), False)
    mate = moved(total, ("", ""), True)
    grads = call(
        functools.partial(finish_kernel, scale),
        (
            shape((KS * KS, 1, chans), f32),
            shape((1, chans), f32),
            shape((1, chans, units), f32),
            shape((1, units), f32),
            shape((1, chans, units), f32),
            shape((1, chans), f32),
        ),
        1,
        (meta, total, near, mate, far),
        (pltpu.VMEM((2 * chans + 32, units), f32),),
    )

    grad_kernel, grad_gain, grad_up, grad_bias, grad_down, grad_scale = grads
    return (
        slotted[None],
        jnp.transpose(grad_kernel, (1, 0, 2)),
        grad_gain,
        grad_up,
        grad_bias,
        grad_down,
        grad_scale,
    )


def solution(mesh):
    in_specs = (
        P("section", "tile", None, None),
        P("tile", None, None),
        P("tile"),
        P("tile"),
        P("section", None, None),
        P("section", None),
        P("section", None, None),
        P("section", None),
        P("section", None, None),
        P("section", None),
    )
    out_specs = (
        P("section", "tile", None, None),
        P("section", None, None),
        P("section", None),
        P("section", None, None),
        P("section", None),
        P("section", None, None),
        P("section", None),
    )
    return jax.shard_map(body, mesh=mesh, in_specs=in_specs, out_specs=out_specs, check_vma=False)
```

```python
import functools
import math

import jax
import jax.numpy as jnp
from jax import lax
from jax.experimental import pallas as pl
from jax.experimental.pallas import tpu as pltpu
from jax.sharding import PartitionSpec as P

KS = 7
CAP = 2
SECTIONS = 4
TILES = 64
MARGIN = 3
BLOCK = 16
UNROLL = 12

norm_eps = 1e-06
tanh_root = math.sqrt(2.0 / math.pi)
cubic_coef = 0.044715

f32 = jnp.float32
bf16 = jnp.bfloat16

SECTION, ODD, KEEP, NEAR, MATE, FAR, OFFSET, INSIDE, LAND = range(9)
PLACES = 8
OWNERS = LAND + 5


def split_tile(tile):
    return tile % 2, tile // 2 % 4, tile // 8


def flip_x0(x):
    return x ^ 1


def flip_x1(x):
    return 3 - x


def flip_z0(z):
    return z ^ 1


def flip_z1(z):
    return 3 - z if z < 4 else 11 - z


def flip_z2(z):
    return 7 - z


flips = {"x0": flip_x0, "x1": flip_x1, "z0": flip_z0, "z1": flip_z1, "z2": flip_z2}


def moved(value, dims, swap):
    pairs = []
    for tile in range(TILES):
        core, x, z = split_tile(tile)
        dim = dims[core]
        if dim in ("x0", "x1"):
            x = flips[dim](x)
        elif dim:
            z = flips[dim](z)
        core = 1 - core if swap else core
        pairs.append((tile, z * 8 + x * 2 + core))
    return lax.ppermute(value, "tile", pairs)


def within(value):
    return lax.ppermute(value, "tile", [(tile, tile ^ 1) for tile in range(TILES)])


def across(value):
    pairs = [(tile, (tile + 1 if tile % 2 else tile - 1) % TILES) for tile in range(TILES)]
    return lax.ppermute(value, "tile", pairs)


def halo(inner, outer):
    outer = across(outer)
    return within(inner), outer


def call(body, out_shape, smem, operands, scratch=(), cost=(0, 0)):
    spec = [pl.BlockSpec(memory_space=pltpu.SMEM)] * smem
    spec += [pl.BlockSpec(memory_space=pltpu.VMEM)] * (len(operands) - smem)
    outs = jax.tree.map(lambda _: pl.BlockSpec(memory_space=pltpu.VMEM), out_shape)
    return pl.pallas_call(
        body,
        out_shape=out_shape,
        in_specs=spec,
        out_specs=outs,
        scratch_shapes=list(scratch),
        compiler_params=pltpu.CompilerParams(vmem_limit_bytes=32 * 1024 * 1024),
        cost_estimate=pl.CostEstimate(flops=cost[0], bytes_accessed=cost[1], transcendentals=0),
    )(*operands)


def shape(dims, dtype):
    return jax.ShapeDtypeStruct(dims, dtype)


def fill_rows(rows_ref, meta, own, inner, outer):
    count = own.shape[0]
    odd = meta[ODD] == 1
    far_rows = jnp.where(meta[INSIDE] == 1, outer[...], jnp.zeros_like(outer))
    near_rows = inner[...]
    rows_ref[MARGIN : MARGIN + count] = own[...]
    rows_ref[:MARGIN] = jnp.where(odd, near_rows, far_rows)
    rows_ref[MARGIN + count : 2 * MARGIN + count] = jnp.where(odd, far_rows, near_rows)
    rows_ref[2 * MARGIN + count :] = jnp.zeros((1,) + own.shape[1:], bf16)


def edges(odd, value_ref, inner_ref, outer_ref):
    count = value_ref.shape[0]
    head = value_ref[:MARGIN]
    tail = value_ref[count - MARGIN :]
    inner_ref[...] = jnp.where(odd, head, tail)
    outer_ref[...] = jnp.where(odd, tail, head)


def fill_taps(cols, targets):
    high = cols[...].astype(bf16)
    low = (cols[...] - high.astype(f32)).astype(bf16)
    chans, taps = cols.shape
    wide = KS * 128
    tap = lax.broadcasted_iota(jnp.int32, (taps, wide), 0)
    place = lax.broadcasted_iota(jnp.int32, (taps, wide), 1)
    tap_col, tap_row = place >> 7, (place >> 4) & (PLACES - 1)
    own = lax.broadcasted_iota(jnp.int32, (chans, wide), 0) & (BLOCK - 1)
    diagonal = own == (lax.broadcasted_iota(jnp.int32, (chans, wide), 1) & (BLOCK - 1))
    for target, row in zip(targets, (tap_row, KS - 1 - tap_row)):
        if target is None:
            continue
        hit = (tap == row * KS + tap_col) & (tap_row < KS)
        spread = jnp.where(hit, 1.0, 0.0).astype(bf16)
        for half, value in enumerate((high, low)):
            filled = jnp.dot(value, spread, preferred_element_type=f32)
            filled = jnp.where(diagonal, filled, 0.0).astype(bf16)
            for block in range(chans // BLOCK):
                for col in range(KS):
                    target[
                        block, col * BLOCK : (col + 1) * BLOCK, half * 128 : (half + 1) * 128
                    ] = filled[block * BLOCK : (block + 1) * BLOCK, col * 128 : (col + 1) * 128]


def prepare_kernel(
    kernel, gain, layer, bias, up, down, cols, forth_ref, back_ref, up_t_ref, down_t_ref, bias_ref, lines_ref
):
    lines_ref[...] = jnp.zeros_like(lines_ref)
    lines_ref[: KS * KS] = kernel[...]
    lines_ref[KS * KS : KS * KS + 1] = gain[...]
    lines_ref[KS * KS + 1 : KS * KS + 2] = layer[...]
    cols[...] = jnp.transpose(lines_ref[...])
    up_t_ref[...] = jnp.transpose(up[...].astype(f32)).astype(bf16)
    down_t_ref[...] = jnp.transpose(down[...].astype(f32)).astype(bf16)
    bias_ref[...] = jnp.transpose(jnp.broadcast_to(bias[...], (8, bias.shape[1])))
    fill_taps(cols, (forth_ref, back_ref))


def stacked(rows_ref, start, count):
    rows = [rows_ref[row, pl.ds(start, BLOCK), :] for row in range(count + PLACES - 1)]
    return jnp.concatenate(
        [jnp.concatenate(rows[place : place + count], axis=1) for place in range(PLACES)], axis=0
    )


def taps_sum(rows_ref, taps_mat, block, count, backward):
    windows = stacked(rows_ref, pl.multiple_of(block * BLOCK, BLOCK), count)
    parts = jnp.dot(
        taps_mat[block], jnp.concatenate([windows, windows], axis=0), preferred_element_type=f32
    )
    sums = []
    for row in range(count):
        total = None
        for tap_col in range(KS):
            shift = (tap_col - MARGIN if backward else MARGIN - tap_col) % 128
            part = parts[tap_col * BLOCK : (tap_col + 1) * BLOCK, row * 128 : (row + 1) * 128]
            if shift:
                part = pltpu.roll(part, shift, 1)
            total = part if total is None else total + part
        sums.append(total)
    return sums


def forward_kernel(
    meta, acts, inner, outer, taps_mat, cols, up_t, bias, bias_row, nhat_ref, inv_ref, hidden_ref, slope_ref, note_ref, rows_ref, field_ref, normed_ref
):
    count, chans, width = acts.shape
    fill_rows(rows_ref, meta, acts, inner, outer)

    def step(index, carry):
        start = pl.multiple_of(index * BLOCK, BLOCK)
        sums = taps_sum(rows_ref, taps_mat, index, count, False)
        for row in range(count):
            field_ref[pl.ds(start, BLOCK), row * width : (row + 1) * width] = sums[row]
        return carry

    lax.fori_loop(0, chans // BLOCK, step, 0, unroll=UNROLL)
    gain = cols[:, KS * KS : KS * KS + 1]
    for row in range(count):
        part = slice(row * width, (row + 1) * width)
        field = field_ref[:, part]
        center = field - jnp.mean(field, axis=0, keepdims=True)
        inverse = 1.0 / jnp.sqrt(jnp.mean(center * center, axis=0, keepdims=True) + norm_eps)
        nhat = center * inverse
        nhat_ref[:, part] = nhat
        inv_ref[:, part] = inverse
        normed_ref[:, part] = (nhat * gain).astype(bf16)
    cells = count * width
    note_ref[:chans, :cells] = nhat_ref[...].astype(bf16)
    high, low = two_parts(cols[...])
    note_ref[:chans, cells:] = jnp.concatenate([high, low], axis=1).astype(bf16)
    parts = two_parts(bias_row[...])
    padding = jnp.zeros((1, bias_row.shape[1] - cells), f32)
    parts += two_parts(jnp.concatenate([inv_ref[...], padding], axis=1))
    rest = jnp.zeros((BLOCK - len(parts), bias_row.shape[1]), f32)
    note_ref[chans:] = jnp.concatenate([*parts, rest]).astype(bf16)
    mlp_forward(normed_ref, up_t, bias, hidden_ref, slope_ref)


def two_parts(value):
    high = value.astype(bf16).astype(f32)
    return [high, value - high]


def mlp_forward(normed_ref, up_t, bias, hidden_ref, slope_ref):
    units = up_t.shape[0]
    chunk = 128
    for first in range(0, units, chunk):
        part = slice(first, first + chunk)
        preact = jnp.dot(up_t[part], normed_ref[...], preferred_element_type=f32) + bias[part, :1]
        square = preact * preact
        hyper = jnp.tanh(preact * (tanh_root + tanh_root * cubic_coef * square))
        half = 0.5 + 0.5 * hyper
        if hidden_ref is not None:
            hidden_ref[part] = (preact * half).astype(bf16)
        slope = half * (
            1.0 + preact * (1.0 - hyper) * (tanh_root + 3.0 * cubic_coef * tanh_root * square)
        )
        slope_ref[part] = slope.astype(bf16)


def adopt_kernel(
    meta, note, half, other, nhat_ref, inv_ref, slope_ref, cols_ref, back_ref, up_ref, down_t_ref, up_t_ref, bias_ref, normed_ref
):
    chans, cells = nhat_ref.shape
    units = slope_ref.shape[0]
    taps = cols_ref.shape[1]

    @pl.when((meta[SECTION] == SECTIONS - 1) | (meta[SECTION] == 0))
    def _():
        odd = meta[ODD] == 1
        up = jnp.where(odd, other[...], half[...])
        up_ref[...] = up
        up_t_ref[...] = jnp.transpose(up.astype(f32)).astype(bf16)
        down = jnp.where(odd, half[...], other[...])
        down_t_ref[...] = jnp.transpose(down.astype(f32)).astype(bf16)
        nhat = note[:chans, :cells].astype(f32)
        nhat_ref[...] = nhat
        pieces = note[:chans, cells:].astype(f32)
        cols_ref[...] = pieces[:, :taps] + pieces[:, taps:]
        lines = note[chans:].astype(f32)
        bias_row = lines[0:1] + lines[1:2]
        inv_ref[...] = (lines[2:3] + lines[3:4])[:, :cells]
        bias_ref[...] = jnp.transpose(jnp.broadcast_to(bias_row, (8, units)))
        fill_taps(cols_ref, (None, back_ref))
        normed_ref[...] = (nhat * cols_ref[:, KS * KS : KS * KS + 1]).astype(bf16)
        mlp_forward(normed_ref, up_t_ref, bias_ref, None, slope_ref)


def mlp_backward(cots, meta, cols, down_t, up, slope, nhat, inv, out_ref, low_ref, field_ref, sums=None):
    width = cots[0].shape[1]
    count = len(cots)
    gain = cols[:, KS * KS : KS * KS + 1]
    layer = cols[:, KS * KS + 1 : KS * KS + 2]
    for row in range(count):
        wet = meta[LAND + row].astype(f32)
        out_ref[:, row * width : (row + 1) * width] = (cots[row] * layer * wet).astype(bf16)
    units = down_t.shape[0]
    chunk = 128
    for first in range(0, units, chunk):
        part = slice(first, first + chunk)
        pregrad = jnp.dot(down_t[part], out_ref[...], preferred_element_type=f32)
        pregrad = pregrad * slope[part].astype(f32)
        low_ref[part] = pregrad.astype(bf16)
        if sums is not None:
            sums[0][part] = sum(
                pregrad[:, row * width : (row + 1) * width] for row in range(count)
            )
    featgrad = jnp.dot(up[...], low_ref[...], preferred_element_type=f32)
    gains = None
    for row in range(count):
        part = slice(row * width, (row + 1) * width)
        feat = featgrad[:, part]
        own = nhat[:, part]
        scaled = feat * gain
        mean = jnp.mean(scaled, axis=0, keepdims=True)
        cross = jnp.mean(scaled * own, axis=0, keepdims=True)
        field_ref[row] = (inv[:, part] * (scaled - mean - own * cross)).astype(bf16)
        if sums is not None:
            term = feat * own
            gains = term if gains is None else gains + term
    if sums is not None:
        sums[1][...] = gains


def turn_kernel(
    section, meta, cot, cols, down_t, up, slope, nhat, inv, field_ref, inner_ref, outer_ref, out_ref, low_ref
):
    @pl.when(meta[SECTION] == section)
    def _():
        cots = [cot[row].astype(f32) for row in range(cot.shape[0])]
        mlp_backward(cots, meta, cols, down_t, up, slope, nhat, inv, out_ref, low_ref, field_ref)
        edges(meta[ODD] == 1, field_ref, inner_ref, outer_ref)


def conv_rows(meta, field, inner, outer, cot, taps_mat, result_ref, rows_ref):
    count, chans, width = field.shape
    fill_rows(rows_ref, meta, field, inner, outer)

    def step(index, carry):
        start = pl.multiple_of(index * BLOCK, BLOCK)
        sums = taps_sum(rows_ref, taps_mat, index, count, True)
        for row in range(count):
            own = cot[row, pl.ds(start, BLOCK), :].astype(f32)
            result_ref[row, pl.ds(start, BLOCK), :] = (own + sums[row]).astype(bf16)
        return carry

    lax.fori_loop(0, chans // BLOCK, step, 0, unroll=UNROLL)


def conv_kernel(section, meta, field, inner, outer, cot, taps_mat, result_ref, rows_ref):
    @pl.when(meta[SECTION] == section)
    def _():
        conv_rows(meta, field, inner, outer, cot, taps_mat, result_ref, rows_ref)


def middle_kernel(
    plane,
    meta,
    field,
    inner,
    outer,
    cot,
    taps_mat,
    cols,
    down_t,
    up,
    slope,
    nhat,
    inv,
    result_ref,
    field_ref,
    inner_ref,
    outer_ref,
    rows_ref,
    out_ref,
    low_ref,
):
    @pl.when(meta[SECTION] == plane)
    def _():
        conv_rows(meta, field, inner, outer, cot, taps_mat, result_ref, rows_ref)
        cots = [result_ref[row].astype(f32) for row in range(result_ref.shape[0])]
        mlp_backward(cots, meta, cols, down_t, up, slope, nhat, inv, out_ref, low_ref, field_ref)
        edges(meta[ODD] == 1, field_ref, inner_ref, outer_ref)


def last_conv_kernel(meta, field, inner, outer, cot, taps_mat, result_ref, sent_ref, rows_ref):
    conv_rows(meta, field, inner, outer, cot, taps_mat, result_ref, rows_ref)
    sent_ref[...] = jnp.zeros_like(sent_ref)
    rank = jnp.int32(0)
    for local in range(result_ref.shape[0]):
        kept = jnp.bool_(False)
        for slot in range(OWNERS, meta.shape[0]):
            kept = kept | (meta[slot] == meta[OFFSET] + local)
        sent = (meta[LAND + local] == 1) & jnp.logical_not(kept)
        for place in range(CAP):

            @pl.when(sent & (rank == place))
            def _():
                sent_ref[place] = result_ref[local]

        rank = rank + sent.astype(jnp.int32)


def slots_kernel(meta, result, arrived, slots_ref):
    for slot in range(slots_ref.shape[0]):
        slots_ref[slot] = arrived[min(slot, CAP - 1)]
        for local in range(result.shape[0]):

            @pl.when(meta[OWNERS + slot] == meta[OFFSET] + local)
            def _():
                slots_ref[slot] = result[local]


def last_kernel(
    meta,
    cot_top,
    cot_2,
    cot_1,
    turn_field,
    turn_inner,
    turn_outer,
    turn_cot,
    turn_mat,
    cols,
    layer_row,
    down_t,
    down,
    up,
    slope,
    nhat,
    inv,
    hidden,
    acts,
    inner,
    outer,
    cot_ref,
    field_ref,
    field_inner_ref,
    field_outer_ref,
    keep_ref,
    near_ref,
    mate_ref,
    far_ref,
    out_ref,
    low_ref,
    bias_ref,
    gain_ref,
    rows_ref,
    packed_ref,
):
    count, chans, width = acts.shape
    units = slope.shape[0]
    odd = meta[ODD] == 1
    for section, cot in ((3, cot_top), (2, cot_2), (1, cot_1)):

        @pl.when(meta[SECTION] == section)
        def _():
            cot_ref[...] = cot[...]

    @pl.when(meta[SECTION] == 0)
    def _():
        conv_rows(meta, turn_field, turn_inner, turn_outer, turn_cot, turn_mat, cot_ref, rows_ref)

    cots = [cot_ref[row].astype(f32) for row in range(count)]
    mlp_backward(
        cots, meta, cols, down_t, up, slope, nhat, inv, out_ref, low_ref, field_ref, (bias_ref, gain_ref)
    )
    edges(odd, field_ref, field_inner_ref, field_outer_ref)
    gain = cols[:, KS * KS : KS * KS + 1]
    normed = (nhat[...] * gain).astype(bf16)
    turned = (((1,), (1,)), ((), ()))
    grad_up = lax.dot_general(normed, low_ref[...], turned, preferred_element_type=f32)
    packed_ref[:chans] = grad_up
    grad_down = lax.dot_general(out_ref[...], hidden[...], turned, preferred_element_type=f32)
    packed_ref[chans : 2 * chans] = grad_down
    product = grad_down * down[...].astype(f32)
    product = sum(product[:, first : first + 128] for first in range(0, units, 128))

    fill_rows(rows_ref, meta, acts, inner, outer)
    base = 2 * chans
    shifts = [(tap_col - MARGIN) % 128 for tap_col in range(KS)]
    own = lax.broadcasted_iota(jnp.int32, (BLOCK, 128), 0)
    diagonal = own == (lax.broadcasted_iota(jnp.int32, (BLOCK, 128), 1) & (BLOCK - 1))
    for block in range(chans // BLOCK):
        start = block * BLOCK
        windows = stacked(rows_ref, start, count)
        fields = [field_ref[row, start : start + BLOCK, :].astype(f32) for row in range(count)]
        rolled = jnp.concatenate(
            [
                jnp.concatenate(
                    [pltpu.roll(field, shift, 1) if shift else field for field in fields], axis=1
                )
                for shift in shifts
            ],
            axis=0,
        ).astype(bf16)
        crossed = lax.dot_general(rolled, windows, turned, preferred_element_type=f32)
        first = base + block // 6 * 8
        lanes = slice(block % 6 * 128, block % 6 * 128 + 128)
        for tap_col in range(KS):
            part = jnp.where(diagonal, crossed[tap_col * BLOCK : (tap_col + 1) * BLOCK], 0.0)
            packed_ref[first + tap_col : first + tap_col + 1, lanes] = jnp.sum(
                part, axis=0, keepdims=True
            )
        packed_ref[first + KS : first + PLACES, lanes] = jnp.zeros((1, 128), f32)
    bias_row = jnp.sum(jnp.transpose(bias_ref[...]), axis=0, keepdims=True)
    gain_row = jnp.sum(jnp.transpose(gain_ref[...]), axis=0, keepdims=True)
    scale_row = jnp.sum(jnp.transpose(product), axis=0, keepdims=True) / layer_row[...]
    packed_ref[base + 16 :] = jnp.zeros((packed_ref.shape[0] - base - 16, units), f32)
    packed_ref[base + 16 : base + 17] = bias_row
    packed_ref[base + 17 : base + 18, :chans] = gain_row
    packed_ref[base + 17 : base + 18, 256 : 256 + chans] = scale_row
    part_rows = keep_ref.shape[0]
    for place, target in ((KEEP, keep_ref), (NEAR, near_ref), (MATE, mate_ref), (FAR, far_ref)):
        start = pl.multiple_of(meta[place] * part_rows, 8)
        target[...] = packed_ref[pl.ds(start, part_rows), :].astype(bf16)


def finish_kernel(
    scale, meta, keep, near, mate, far, kernel_ref, gain_ref, up_ref, bias_ref, down_ref, scale_ref, packed_ref
):
    part_rows = keep.shape[0]
    for place, source in ((KEEP, keep), (NEAR, near), (MATE, mate), (FAR, far)):
        start = pl.multiple_of(meta[place] * part_rows, 8)
        packed_ref[pl.ds(start, part_rows), :] = source[...].astype(f32) * scale
    chans = up_ref.shape[1]
    base = 2 * chans
    up_ref[0] = packed_ref[:chans]
    down_ref[0] = packed_ref[chans:base]
    lane = lax.broadcasted_iota(jnp.int32, (PLACES, 128), 1) >> 4
    blocks = chans // BLOCK
    for tap_row in range(KS):
        halves = []
        for first in range(0, blocks, PLACES):
            half = jnp.zeros((PLACES, 128), f32)
            for block in range(first, min(first + PLACES, blocks)):
                rows = slice(base + block // 6 * 8, base + block // 6 * 8 + 8)
                part = packed_ref[rows, block % 6 * 128 : block % 6 * 128 + 128]
                shift = (block - first - tap_row) * BLOCK % 128
                if shift:
                    part = pltpu.roll(part, shift, 1)
                half = jnp.where(lane == block - first, part, half)
            halves.append(half)
        line = jnp.concatenate(halves, axis=1)
        for tap_col in range(KS):
            kernel_ref[tap_row * KS + tap_col] = line[tap_col : tap_col + 1, :chans]
    bias_ref[...] = packed_ref[base + 16 : base + 17]
    gain_ref[...] = packed_ref[base + 17 : base + 18, :chans]
    scale_ref[...] = packed_ref[base + 17 : base + 18, 256 : 256 + chans]


def added(*values):
    return sum(value.astype(f32) for value in values).astype(bf16)


def body(acts, cot_top, land, owners, dw_kernel, ln_gain, w_up, b_up, w_down, layer_scale):
    source = acts[0]
    count, chans, width = source.shape
    units = w_up.shape[2]
    cells = count * width
    tile_now = lax.axis_index("tile")
    section_now = lax.axis_index("section")
    scale = 1.0 / math.sqrt(lax.axis_size("tile") * cells)
    core, x, z = split_tile(tile_now)
    bit_x, bit_z = (x + 1) // 2 % 2, (z + 1) // 2 % 2
    bit = jnp.where(core == 0, bit_x, bit_z)
    mate_bit = jnp.where(core == 0, bit_z, bit_x)
    numbers = [
        section_now,
        core,
        2 * core + bit,
        2 * core + 1 - bit,
        2 * (1 - core) + mate_bit,
        2 * (1 - core) + 1 - mate_bit,
        tile_now * count,
        jnp.where((tile_now == 0) | (tile_now == TILES - 1), 0, 1),
    ]
    meta = jnp.concatenate([jnp.stack(numbers).astype(jnp.int32), land, owners])

    odd = core == 1
    head, tail = source[:MARGIN], source[count - MARGIN :]
    acts_inner, acts_outer = halo(jnp.where(odd, head, tail), jnp.where(odd, tail, head))
    up, down = w_up[0], w_down[0]
    swaps = [(section, section ^ 1) for section in range(SECTIONS)]
    taps_shape = shape((chans // BLOCK, KS * BLOCK, 256), bf16)
    weights_t = shape((units, chans), bf16)
    cols_shape = shape((chans, 64), f32)
    cols, forth, back, up_t, down_t, bias = call(
        prepare_kernel,
        (cols_shape, taps_shape, taps_shape, weights_t, weights_t, shape((units, 8), f32)),
        0,
        (dw_kernel[0], ln_gain, layer_scale, b_up, up, down),
        (pltpu.VMEM((64, chans), f32),),
        cost=(10**9, 10**7),
    )
    half = lax.ppermute(jnp.where(odd, down, up), "section", swaps)

    padded = pltpu.VMEM((count + PLACES - 1, chans, width), bf16)
    nhat_shape, inv_shape = shape((chans, cells), f32), shape((1, cells), f32)
    unit_shape = shape((units, cells), bf16)
    nhat, inv, hidden, slope, own_note = call(
        forward_kernel,
        (nhat_shape, inv_shape, unit_shape, unit_shape, shape((chans + BLOCK, units), bf16)),
        1,
        (meta, source, acts_inner, acts_outer, forth, cols, up_t, bias, b_up),
        (padded, pltpu.VMEM((chans, cells), f32), pltpu.VMEM((chans, cells), bf16)),
    )
    note = lax.ppermute(own_note, "section", swaps)

    rows_shape = shape((count, chans, width), bf16)
    edge_shape = shape((MARGIN, chans, width), bf16)
    outgrads = pltpu.VMEM((chans, cells), bf16)
    lowgrads = pltpu.VMEM((units, cells), bf16)

    def turn_field(plane, cot, params):
        field_cols, field_down_t, field_up, field_slope, field_nhat, field_inv = params
        return call(
            functools.partial(turn_kernel, plane),
            (rows_shape, edge_shape, edge_shape),
            1,
            (meta, cot, field_cols, field_down_t, field_up, field_slope, field_nhat, field_inv),
            (outgrads, lowgrads),
        )

    top = SECTIONS - 1
    field, inner, outer = turn_field(top, cot_top, (cols, down_t, up, slope, nhat, inv))
    half, field = lax.optimization_barrier((half, field))
    inner, outer = halo(inner, outer)
    other = moved(half, ("", ""), True)
    adopted = call(
        adopt_kernel,
        (nhat_shape, inv_shape, unit_shape, cols_shape, taps_shape, shape((chans, units), bf16))
        + (weights_t, weights_t, shape((units, 8), f32)),
        1,
        (meta, note, half, other),
        (pltpu.VMEM((chans, cells), bf16),),
        cost=(10**9, 10**7),
    )
    next_nhat, next_inv, next_slope, next_cols, next_back, next_up, next_down_t = adopted[:7]
    cot_2, field, inner, outer = call(
        functools.partial(middle_kernel, top),
        (rows_shape, rows_shape, edge_shape, edge_shape),
        1,
        (meta, field, inner, outer, cot_top, back, next_cols, next_down_t, next_up)
        + (next_slope, next_nhat, next_inv),
        (padded, outgrads, lowgrads),
    )
    own_2 = lax.ppermute(cot_2, "section", swaps)
    inner, outer = halo(inner, outer)
    cot_1 = call(
        functools.partial(conv_kernel, top),
        rows_shape,
        1,
        (meta, field, inner, outer, cot_2, next_back),
        (padded,),
    )
    cot_1 = lax.ppermute(cot_1, "section", [(0, top), (top, 0), (1, 2), (2, 1)])
    own_1 = lax.ppermute(cot_1, "section", swaps)

    adopted = (next_cols, next_down_t, next_up, next_slope, next_nhat, next_inv)
    field, inner, outer = turn_field(0, cot_1, adopted)
    inner, outer = halo(inner, outer)

    part = shape(((2 * chans + 32) // 4, units), bf16)
    cot_own, field, inner, outer, keep, near, mate, far = call(
        last_kernel,
        (rows_shape, rows_shape, edge_shape, edge_shape, part, part, part, part),
        1,
        (meta, cot_top, own_2, own_1, field, inner, outer, cot_1, next_back, cols, layer_scale, down_t, down, up, slope, nhat, inv, hidden)
        + (source, acts_inner, acts_outer),
        (
            outgrads,
            lowgrads,
            pltpu.VMEM((units, width), f32),
            pltpu.VMEM((chans, width), f32),
            padded,
            pltpu.VMEM((2 * chans + 32, units), f32),
        ),
    )
    far = moved(far, ("z0", "x0"), True)
    near = moved(near, ("x0", "z0"), False)
    mate = moved(mate, ("", ""), True)
    total = added(keep, near, mate, far)
    orders = (("x1", "z1"), ("z0", "z2"), ("z1", "x0"), ("z2", "x1"))
    total, inner = lax.optimization_barrier((total, inner))
    total = added(total, moved(total, orders[0], False))
    inner = within(inner)
    total, inner, outer = lax.optimization_barrier((total, inner, outer))
    total = added(total, moved(total, orders[1], False))
    outer = across(outer)
    total, outer = lax.optimization_barrier((total, outer))
    total = added(total, moved(total, orders[2], False))
    result, sent = call(
        last_conv_kernel,
        (rows_shape, shape((CAP, chans, width), bf16)),
        1,
        (meta, field, inner, outer, cot_own, back),
        (padded,),
    )
    total, result, sent = lax.optimization_barrier((total, result, sent))
    total = added(total, moved(total, orders[3], False))
    arrived = lax.ppermute(sent, "tile", [(tile, (tile + 1) % TILES) for tile in range(TILES)])
    total, arrived = lax.optimization_barrier((total, arrived))
    slotted = call(
        slots_kernel,
        shape((owners.shape[0], chans, width), bf16),
        1,
        (meta, result, arrived),
    )
    far = moved(total, ("x0", "z0"), True)
    near = moved(total, ("x0", "z0"), False)
    mate = moved(total, ("", ""), True)
    grads = call(
        functools.partial(finish_kernel, scale),
        (
            shape((KS * KS, 1, chans), f32),
            shape((1, chans), f32),
            shape((1, chans, units), f32),
            shape((1, units), f32),
            shape((1, chans, units), f32),
            shape((1, chans), f32),
        ),
        1,
        (meta, total, near, mate, far),
        (pltpu.VMEM((2 * chans + 32, units), f32),),
    )

    grad_kernel, grad_gain, grad_up, grad_bias, grad_down, grad_scale = grads
    return (
        slotted[None],
        jnp.transpose(grad_kernel, (1, 0, 2)),
        grad_gain,
        grad_up,
        grad_bias,
        grad_down,
        grad_scale,
    )


def solution(mesh):
    in_specs = (
        P("section", "tile", None, None),
        P("tile", None, None),
        P("tile"),
        P("tile"),
        P("section", None, None),
        P("section", None),
        P("section", None, None),
        P("section", None),
        P("section", None, None),
        P("section", None),
    )
    out_specs = (
        P("section", "tile", None, None),
        P("section", None, None),
        P("section", None),
        P("section", None, None),
        P("section", None),
        P("section", None, None),
        P("section", None),
    )
    return jax.shard_map(body, mesh=mesh, in_specs=in_specs, out_specs=out_specs, check_vma=False)
```

```python
import functools
import math

import jax
import jax.numpy as jnp
from jax import lax
from jax.experimental import pallas as pl
from jax.experimental.pallas import tpu as pltpu
from jax.sharding import PartitionSpec as P

KS = 7
CAP = 2
SECTIONS = 4
TILES = 64
MARGIN = 3
BLOCK = 16
UNROLL = 12

norm_eps = 1e-06
tanh_root = math.sqrt(2.0 / math.pi)
cubic_coef = 0.044715

f32 = jnp.float32
bf16 = jnp.bfloat16

SECTION, ODD, KEEP, NEAR, MATE, FAR, OFFSET, INSIDE, LAND = range(9)
PLACES = 8
OWNERS = LAND + 5


def split_tile(tile):
    return tile % 2, tile // 2 % 4, tile // 8


def flip_x0(x):
    return x ^ 1


def flip_x1(x):
    return 3 - x


def flip_z0(z):
    return z ^ 1


def flip_z1(z):
    return 3 - z if z < 4 else 11 - z


def flip_z2(z):
    return 7 - z


flips = {"x0": flip_x0, "x1": flip_x1, "z0": flip_z0, "z1": flip_z1, "z2": flip_z2}


def moved(value, dims, swap):
    pairs = []
    for tile in range(TILES):
        core, x, z = split_tile(tile)
        dim = dims[core]
        if dim in ("x0", "x1"):
            x = flips[dim](x)
        elif dim:
            z = flips[dim](z)
        core = 1 - core if swap else core
        pairs.append((tile, z * 8 + x * 2 + core))
    return lax.ppermute(value, "tile", pairs)


def within(value):
    return lax.ppermute(value, "tile", [(tile, tile ^ 1) for tile in range(TILES)])


def across(value):
    pairs = [(tile, (tile + 1 if tile % 2 else tile - 1) % TILES) for tile in range(TILES)]
    return lax.ppermute(value, "tile", pairs)


def halo(inner, outer):
    inner = within(inner)
    return inner, across(outer)


def call(body, out_shape, smem, operands, scratch=(), cost=(0, 0)):
    spec = [pl.BlockSpec(memory_space=pltpu.SMEM)] * smem
    spec += [pl.BlockSpec(memory_space=pltpu.VMEM)] * (len(operands) - smem)
    outs = jax.tree.map(lambda _: pl.BlockSpec(memory_space=pltpu.VMEM), out_shape)
    return pl.pallas_call(
        body,
        out_shape=out_shape,
        in_specs=spec,
        out_specs=outs,
        scratch_shapes=list(scratch),
        compiler_params=pltpu.CompilerParams(vmem_limit_bytes=32 * 1024 * 1024),
        cost_estimate=pl.CostEstimate(flops=cost[0], bytes_accessed=cost[1], transcendentals=0),
    )(*operands)


def shape(dims, dtype):
    return jax.ShapeDtypeStruct(dims, dtype)


def fill_rows(rows_ref, meta, own, inner, outer):
    count = own.shape[0]
    odd = meta[ODD] == 1
    far_rows = jnp.where(meta[INSIDE] == 1, outer[...], jnp.zeros_like(outer))
    near_rows = inner[...]
    rows_ref[MARGIN : MARGIN + count] = own[...]
    rows_ref[:MARGIN] = jnp.where(odd, near_rows, far_rows)
    rows_ref[MARGIN + count : 2 * MARGIN + count] = jnp.where(odd, far_rows, near_rows)
    rows_ref[2 * MARGIN + count :] = jnp.zeros((1,) + own.shape[1:], bf16)


def edges(odd, value_ref, inner_ref, outer_ref):
    count = value_ref.shape[0]
    head = value_ref[:MARGIN]
    tail = value_ref[count - MARGIN :]
    inner_ref[...] = jnp.where(odd, head, tail)
    outer_ref[...] = jnp.where(odd, tail, head)


def fill_taps(cols, targets):
    high = cols[...].astype(bf16)
    low = (cols[...] - high.astype(f32)).astype(bf16)
    chans, taps = cols.shape
    wide = KS * 128
    tap = lax.broadcasted_iota(jnp.int32, (taps, wide), 0)
    place = lax.broadcasted_iota(jnp.int32, (taps, wide), 1)
    tap_col, tap_row = place >> 7, (place >> 4) & (PLACES - 1)
    own = lax.broadcasted_iota(jnp.int32, (chans, wide), 0) & (BLOCK - 1)
    diagonal = own == (lax.broadcasted_iota(jnp.int32, (chans, wide), 1) & (BLOCK - 1))
    for target, row in zip(targets, (tap_row, KS - 1 - tap_row)):
        if target is None:
            continue
        hit = (tap == row * KS + tap_col) & (tap_row < KS)
        spread = jnp.where(hit, 1.0, 0.0).astype(bf16)
        for half, value in enumerate((high, low)):
            filled = jnp.dot(value, spread, preferred_element_type=f32)
            filled = jnp.where(diagonal, filled, 0.0).astype(bf16)
            for block in range(chans // BLOCK):
                for col in range(KS):
                    target[
                        block, col * BLOCK : (col + 1) * BLOCK, half * 128 : (half + 1) * 128
                    ] = filled[block * BLOCK : (block + 1) * BLOCK, col * 128 : (col + 1) * 128]


def prepare_kernel(
    kernel, gain, layer, bias, up, down, cols, forth_ref, back_ref, up_t_ref, down_t_ref, bias_ref, lines_ref
):
    lines_ref[...] = jnp.zeros_like(lines_ref)
    lines_ref[: KS * KS] = kernel[...]
    lines_ref[KS * KS : KS * KS + 1] = gain[...]
    lines_ref[KS * KS + 1 : KS * KS + 2] = layer[...]
    cols[...] = jnp.transpose(lines_ref[...])
    up_t_ref[...] = jnp.transpose(up[...].astype(f32)).astype(bf16)
    down_t_ref[...] = jnp.transpose(down[...].astype(f32)).astype(bf16)
    bias_ref[...] = jnp.transpose(jnp.broadcast_to(bias[...], (8, bias.shape[1])))
    fill_taps(cols, (forth_ref, back_ref))


def stacked(rows_ref, start, count):
    rows = [rows_ref[row, pl.ds(start, BLOCK), :] for row in range(count + PLACES - 1)]
    return jnp.concatenate(
        [jnp.concatenate(rows[place : place + count], axis=1) for place in range(PLACES)], axis=0
    )


def taps_sum(rows_ref, taps_mat, block, count, backward):
    windows = stacked(rows_ref, pl.multiple_of(block * BLOCK, BLOCK), count)
    parts = jnp.dot(
        taps_mat[block], jnp.concatenate([windows, windows], axis=0), preferred_element_type=f32
    )
    sums = []
    for row in range(count):
        total = None
        for tap_col in range(KS):
            shift = (tap_col - MARGIN if backward else MARGIN - tap_col) % 128
            part = parts[tap_col * BLOCK : (tap_col + 1) * BLOCK, row * 128 : (row + 1) * 128]
            if shift:
                part = pltpu.roll(part, shift, 1)
            total = part if total is None else total + part
        sums.append(total)
    return sums


def forward_kernel(
    meta, acts, inner, outer, taps_mat, cols, up_t, bias, bias_row, nhat_ref, inv_ref, hidden_ref, slope_ref, note_ref, rows_ref, field_ref, normed_ref
):
    count, chans, width = acts.shape
    fill_rows(rows_ref, meta, acts, inner, outer)

    def step(index, carry):
        start = pl.multiple_of(index * BLOCK, BLOCK)
        sums = taps_sum(rows_ref, taps_mat, index, count, False)
        for row in range(count):
            field_ref[pl.ds(start, BLOCK), row * width : (row + 1) * width] = sums[row]
        return carry

    lax.fori_loop(0, chans // BLOCK, step, 0, unroll=UNROLL)
    gain = cols[:, KS * KS : KS * KS + 1]
    for row in range(count):
        part = slice(row * width, (row + 1) * width)
        field = field_ref[:, part]
        center = field - jnp.mean(field, axis=0, keepdims=True)
        inverse = 1.0 / jnp.sqrt(jnp.mean(center * center, axis=0, keepdims=True) + norm_eps)
        nhat = center * inverse
        nhat_ref[:, part] = nhat
        inv_ref[:, part] = inverse
        normed_ref[:, part] = (nhat * gain).astype(bf16)
    cells = count * width
    note_ref[:chans, :cells] = nhat_ref[...].astype(bf16)
    high, low = two_parts(cols[...])
    note_ref[:chans, cells:] = jnp.concatenate([high, low], axis=1).astype(bf16)
    parts = two_parts(bias_row[...])
    padding = jnp.zeros((1, bias_row.shape[1] - cells), f32)
    parts += two_parts(jnp.concatenate([inv_ref[...], padding], axis=1))
    rest = jnp.zeros((BLOCK - len(parts), bias_row.shape[1]), f32)
    note_ref[chans:] = jnp.concatenate([*parts, rest]).astype(bf16)
    mlp_forward(normed_ref, up_t, bias, hidden_ref, slope_ref)


def two_parts(value):
    high = value.astype(bf16).astype(f32)
    return [high, value - high]


def mlp_forward(normed_ref, up_t, bias, hidden_ref, slope_ref):
    units = up_t.shape[0]
    chunk = 128
    for first in range(0, units, chunk):
        part = slice(first, first + chunk)
        preact = jnp.dot(up_t[part], normed_ref[...], preferred_element_type=f32) + bias[part, :1]
        square = preact * preact
        hyper = jnp.tanh(preact * (tanh_root + tanh_root * cubic_coef * square))
        half = 0.5 + 0.5 * hyper
        if hidden_ref is not None:
            hidden_ref[part] = (preact * half).astype(bf16)
        slope = half * (
            1.0 + preact * (1.0 - hyper) * (tanh_root + 3.0 * cubic_coef * tanh_root * square)
        )
        slope_ref[part] = slope.astype(bf16)


def adopt_kernel(
    meta, note, half, other, nhat_ref, inv_ref, slope_ref, cols_ref, back_ref, up_ref, down_t_ref, up_t_ref, bias_ref, normed_ref
):
    chans, cells = nhat_ref.shape
    units = slope_ref.shape[0]
    taps = cols_ref.shape[1]

    @pl.when((meta[SECTION] == SECTIONS - 1) | (meta[SECTION] == 0))
    def _():
        odd = meta[ODD] == 1
        up = jnp.where(odd, other[...], half[...])
        up_ref[...] = up
        up_t_ref[...] = jnp.transpose(up.astype(f32)).astype(bf16)
        down = jnp.where(odd, half[...], other[...])
        down_t_ref[...] = jnp.transpose(down.astype(f32)).astype(bf16)
        nhat = note[:chans, :cells].astype(f32)
        nhat_ref[...] = nhat
        pieces = note[:chans, cells:].astype(f32)
        cols_ref[...] = pieces[:, :taps] + pieces[:, taps:]
        lines = note[chans:].astype(f32)
        bias_row = lines[0:1] + lines[1:2]
        inv_ref[...] = (lines[2:3] + lines[3:4])[:, :cells]
        bias_ref[...] = jnp.transpose(jnp.broadcast_to(bias_row, (8, units)))
        fill_taps(cols_ref, (None, back_ref))
        normed_ref[...] = (nhat * cols_ref[:, KS * KS : KS * KS + 1]).astype(bf16)
        mlp_forward(normed_ref, up_t_ref, bias_ref, None, slope_ref)


def mlp_backward(cots, meta, cols, down_t, up, slope, nhat, inv, out_ref, low_ref, field_ref, sums=None):
    width = cots[0].shape[1]
    count = len(cots)
    gain = cols[:, KS * KS : KS * KS + 1]
    layer = cols[:, KS * KS + 1 : KS * KS + 2]
    for row in range(count):
        wet = meta[LAND + row].astype(f32)
        out_ref[:, row * width : (row + 1) * width] = (cots[row] * layer * wet).astype(bf16)
    units = down_t.shape[0]
    chunk = 128
    for first in range(0, units, chunk):
        part = slice(first, first + chunk)
        pregrad = jnp.dot(down_t[part], out_ref[...], preferred_element_type=f32)
        pregrad = pregrad * slope[part].astype(f32)
        low_ref[part] = pregrad.astype(bf16)
        if sums is not None:
            sums[0][part] = sum(
                pregrad[:, row * width : (row + 1) * width] for row in range(count)
            )
    featgrad = jnp.dot(up[...], low_ref[...], preferred_element_type=f32)
    gains = None
    for row in range(count):
        part = slice(row * width, (row + 1) * width)
        feat = featgrad[:, part]
        own = nhat[:, part]
        scaled = feat * gain
        mean = jnp.mean(scaled, axis=0, keepdims=True)
        cross = jnp.mean(scaled * own, axis=0, keepdims=True)
        field_ref[row] = (inv[:, part] * (scaled - mean - own * cross)).astype(bf16)
        if sums is not None:
            term = feat * own
            gains = term if gains is None else gains + term
    if sums is not None:
        sums[1][...] = gains


def turn_kernel(
    section, meta, cot, cols, down_t, up, slope, nhat, inv, field_ref, inner_ref, outer_ref, out_ref, low_ref
):
    @pl.when(meta[SECTION] == section)
    def _():
        cots = [cot[row].astype(f32) for row in range(cot.shape[0])]
        mlp_backward(cots, meta, cols, down_t, up, slope, nhat, inv, out_ref, low_ref, field_ref)
        edges(meta[ODD] == 1, field_ref, inner_ref, outer_ref)


def conv_rows(meta, field, inner, outer, cot, taps_mat, result_ref, rows_ref):
    count, chans, width = field.shape
    fill_rows(rows_ref, meta, field, inner, outer)

    def step(index, carry):
        start = pl.multiple_of(index * BLOCK, BLOCK)
        sums = taps_sum(rows_ref, taps_mat, index, count, True)
        for row in range(count):
            own = cot[row, pl.ds(start, BLOCK), :].astype(f32)
            result_ref[row, pl.ds(start, BLOCK), :] = (own + sums[row]).astype(bf16)
        return carry

    lax.fori_loop(0, chans // BLOCK, step, 0, unroll=UNROLL)


def conv_kernel(section, meta, field, outer, inner, cot, taps_mat, result_ref, rows_ref):
    @pl.when(meta[SECTION] == section)
    def _():
        conv_rows(meta, field, inner, outer, cot, taps_mat, result_ref, rows_ref)


def middle_kernel(
    plane,
    meta,
    field,
    outer,
    inner,
    cot,
    taps_mat,
    cols,
    down_t,
    up,
    slope,
    nhat,
    inv,
    result_ref,
    field_ref,
    inner_ref,
    outer_ref,
    rows_ref,
    out_ref,
    low_ref,
):
    @pl.when(meta[SECTION] == plane)
    def _():
        conv_rows(meta, field, inner, outer, cot, taps_mat, result_ref, rows_ref)
        cots = [result_ref[row].astype(f32) for row in range(result_ref.shape[0])]
        mlp_backward(cots, meta, cols, down_t, up, slope, nhat, inv, out_ref, low_ref, field_ref)
        edges(meta[ODD] == 1, field_ref, inner_ref, outer_ref)


def last_conv_kernel(meta, field, inner, outer, cot, taps_mat, result_ref, sent_ref, rows_ref):
    conv_rows(meta, field, inner, outer, cot, taps_mat, result_ref, rows_ref)
    sent_ref[...] = jnp.zeros_like(sent_ref)
    rank = jnp.int32(0)
    for local in range(result_ref.shape[0]):
        kept = jnp.bool_(False)
        for slot in range(OWNERS, meta.shape[0]):
            kept = kept | (meta[slot] == meta[OFFSET] + local)
        sent = (meta[LAND + local] == 1) & jnp.logical_not(kept)
        for place in range(CAP):

            @pl.when(sent & (rank == place))
            def _():
                sent_ref[place] = result_ref[local]

        rank = rank + sent.astype(jnp.int32)


def slots_kernel(meta, result, arrived, slots_ref):
    for slot in range(slots_ref.shape[0]):
        slots_ref[slot] = arrived[min(slot, CAP - 1)]
        for local in range(result.shape[0]):

            @pl.when(meta[OWNERS + slot] == meta[OFFSET] + local)
            def _():
                slots_ref[slot] = result[local]


def last_kernel(
    meta,
    cot_top,
    cot_2,
    cot_1,
    turn_field,
    turn_outer,
    turn_inner,
    turn_cot,
    turn_mat,
    cols,
    layer_row,
    down_t,
    down,
    up,
    slope,
    nhat,
    inv,
    hidden,
    acts,
    inner,
    outer,
    cot_ref,
    field_ref,
    field_inner_ref,
    field_outer_ref,
    keep_ref,
    near_ref,
    mate_ref,
    far_ref,
    out_ref,
    low_ref,
    bias_ref,
    gain_ref,
    rows_ref,
    packed_ref,
):
    count, chans, width = acts.shape
    units = slope.shape[0]
    odd = meta[ODD] == 1
    for section, cot in ((3, cot_top), (2, cot_2), (1, cot_1)):

        @pl.when(meta[SECTION] == section)
        def _():
            cot_ref[...] = cot[...]

    @pl.when(meta[SECTION] == 0)
    def _():
        conv_rows(meta, turn_field, turn_inner, turn_outer, turn_cot, turn_mat, cot_ref, rows_ref)

    cots = [cot_ref[row].astype(f32) for row in range(count)]
    mlp_backward(
        cots, meta, cols, down_t, up, slope, nhat, inv, out_ref, low_ref, field_ref, (bias_ref, gain_ref)
    )
    edges(odd, field_ref, field_inner_ref, field_outer_ref)
    gain = cols[:, KS * KS : KS * KS + 1]
    normed = (nhat[...] * gain).astype(bf16)
    turned = (((1,), (1,)), ((), ()))
    grad_up = lax.dot_general(normed, low_ref[...], turned, preferred_element_type=f32)
    packed_ref[:chans] = grad_up
    grad_down = lax.dot_general(out_ref[...], hidden[...], turned, preferred_element_type=f32)
    packed_ref[chans : 2 * chans] = grad_down
    product = grad_down * down[...].astype(f32)
    product = sum(product[:, first : first + 128] for first in range(0, units, 128))

    fill_rows(rows_ref, meta, acts, inner, outer)
    base = 2 * chans
    shifts = [(tap_col - MARGIN) % 128 for tap_col in range(KS)]
    own = lax.broadcasted_iota(jnp.int32, (BLOCK, 128), 0)
    diagonal = own == (lax.broadcasted_iota(jnp.int32, (BLOCK, 128), 1) & (BLOCK - 1))
    for block in range(chans // BLOCK):
        start = block * BLOCK
        windows = stacked(rows_ref, start, count)
        fields = [field_ref[row, start : start + BLOCK, :].astype(f32) for row in range(count)]
        rolled = jnp.concatenate(
            [
                jnp.concatenate(
                    [pltpu.roll(field, shift, 1) if shift else field for field in fields], axis=1
                )
                for shift in shifts
            ],
            axis=0,
        ).astype(bf16)
        crossed = lax.dot_general(rolled, windows, turned, preferred_element_type=f32)
        first = base + block // 6 * 8
        lanes = slice(block % 6 * 128, block % 6 * 128 + 128)
        for tap_col in range(KS):
            part = jnp.where(diagonal, crossed[tap_col * BLOCK : (tap_col + 1) * BLOCK], 0.0)
            packed_ref[first + tap_col : first + tap_col + 1, lanes] = jnp.sum(
                part, axis=0, keepdims=True
            )
        packed_ref[first + KS : first + PLACES, lanes] = jnp.zeros((1, 128), f32)
    bias_row = jnp.sum(jnp.transpose(bias_ref[...]), axis=0, keepdims=True)
    gain_row = jnp.sum(jnp.transpose(gain_ref[...]), axis=0, keepdims=True)
    scale_row = jnp.sum(jnp.transpose(product), axis=0, keepdims=True) / layer_row[...]
    packed_ref[base + 16 :] = jnp.zeros((packed_ref.shape[0] - base - 16, units), f32)
    packed_ref[base + 16 : base + 17] = bias_row
    packed_ref[base + 17 : base + 18, :chans] = gain_row
    packed_ref[base + 17 : base + 18, 256 : 256 + chans] = scale_row
    part_rows = keep_ref.shape[0]
    for place, target in ((KEEP, keep_ref), (NEAR, near_ref), (MATE, mate_ref), (FAR, far_ref)):
        start = pl.multiple_of(meta[place] * part_rows, 8)
        target[...] = packed_ref[pl.ds(start, part_rows), :].astype(bf16)


def finish_kernel(
    scale, meta, keep, near, mate, far, kernel_ref, gain_ref, up_ref, bias_ref, down_ref, scale_ref, packed_ref
):
    part_rows = keep.shape[0]
    for place, source in ((KEEP, keep), (NEAR, near), (MATE, mate), (FAR, far)):
        start = pl.multiple_of(meta[place] * part_rows, 8)
        packed_ref[pl.ds(start, part_rows), :] = source[...].astype(f32) * scale
    chans = up_ref.shape[1]
    base = 2 * chans
    up_ref[0] = packed_ref[:chans]
    down_ref[0] = packed_ref[chans:base]
    lane = lax.broadcasted_iota(jnp.int32, (PLACES, 128), 1) >> 4
    blocks = chans // BLOCK
    for tap_row in range(KS):
        halves = []
        for first in range(0, blocks, PLACES):
            half = jnp.zeros((PLACES, 128), f32)
            for block in range(first, min(first + PLACES, blocks)):
                rows = slice(base + block // 6 * 8, base + block // 6 * 8 + 8)
                part = packed_ref[rows, block % 6 * 128 : block % 6 * 128 + 128]
                shift = (block - first - tap_row) * BLOCK % 128
                if shift:
                    part = pltpu.roll(part, shift, 1)
                half = jnp.where(lane == block - first, part, half)
            halves.append(half)
        line = jnp.concatenate(halves, axis=1)
        for tap_col in range(KS):
            kernel_ref[tap_row * KS + tap_col] = line[tap_col : tap_col + 1, :chans]
    bias_ref[...] = packed_ref[base + 16 : base + 17]
    gain_ref[...] = packed_ref[base + 17 : base + 18, :chans]
    scale_ref[...] = packed_ref[base + 17 : base + 18, 256 : 256 + chans]


def added(*values):
    return sum(value.astype(f32) for value in values).astype(bf16)


def body(acts, cot_top, land, owners, dw_kernel, ln_gain, w_up, b_up, w_down, layer_scale):
    source = acts[0]
    count, chans, width = source.shape
    units = w_up.shape[2]
    cells = count * width
    tile_now = lax.axis_index("tile")
    section_now = lax.axis_index("section")
    scale = 1.0 / math.sqrt(lax.axis_size("tile") * cells)
    core, x, z = split_tile(tile_now)
    bit_x, bit_z = (x + 1) // 2 % 2, (z + 1) // 2 % 2
    bit = jnp.where(core == 0, bit_x, bit_z)
    mate_bit = jnp.where(core == 0, bit_z, bit_x)
    numbers = [
        section_now,
        core,
        2 * core + bit,
        2 * core + 1 - bit,
        2 * (1 - core) + mate_bit,
        2 * (1 - core) + 1 - mate_bit,
        tile_now * count,
        jnp.where((tile_now == 0) | (tile_now == TILES - 1), 0, 1),
    ]
    meta = jnp.concatenate([jnp.stack(numbers).astype(jnp.int32), land, owners])

    odd = core == 1
    head, tail = source[:MARGIN], source[count - MARGIN :]
    acts_inner, acts_outer = halo(jnp.where(odd, head, tail), jnp.where(odd, tail, head))
    up, down = w_up[0], w_down[0]
    swaps = [(section, section ^ 1) for section in range(SECTIONS)]
    taps_shape = shape((chans // BLOCK, KS * BLOCK, 256), bf16)
    weights_t = shape((units, chans), bf16)
    cols_shape = shape((chans, 64), f32)
    cols, forth, back, up_t, down_t, bias = call(
        prepare_kernel,
        (cols_shape, taps_shape, taps_shape, weights_t, weights_t, shape((units, 8), f32)),
        0,
        (dw_kernel[0], ln_gain, layer_scale, b_up, up, down),
        (pltpu.VMEM((64, chans), f32),),
        cost=(10**9, 10**7),
    )
    half = lax.ppermute(jnp.where(odd, down, up), "section", swaps)

    padded = pltpu.VMEM((count + PLACES - 1, chans, width), bf16)
    nhat_shape, inv_shape = shape((chans, cells), f32), shape((1, cells), f32)
    unit_shape = shape((units, cells), bf16)
    nhat, inv, hidden, slope, own_note = call(
        forward_kernel,
        (nhat_shape, inv_shape, unit_shape, unit_shape, shape((chans + BLOCK, units), bf16)),
        1,
        (meta, source, acts_inner, acts_outer, forth, cols, up_t, bias, b_up),
        (padded, pltpu.VMEM((chans, cells), f32), pltpu.VMEM((chans, cells), bf16)),
    )
    note = lax.ppermute(own_note, "section", swaps)

    rows_shape = shape((count, chans, width), bf16)
    edge_shape = shape((MARGIN, chans, width), bf16)
    outgrads = pltpu.VMEM((chans, cells), bf16)
    lowgrads = pltpu.VMEM((units, cells), bf16)

    def turn_field(plane, cot, params):
        field_cols, field_down_t, field_up, field_slope, field_nhat, field_inv = params
        return call(
            functools.partial(turn_kernel, plane),
            (rows_shape, edge_shape, edge_shape),
            1,
            (meta, cot, field_cols, field_down_t, field_up, field_slope, field_nhat, field_inv),
            (outgrads, lowgrads),
        )

    top = SECTIONS - 1
    field, inner, outer = turn_field(top, cot_top, (cols, down_t, up, slope, nhat, inv))
    half, field = lax.optimization_barrier((half, field))
    inner, outer = halo(inner, outer)
    other = moved(half, ("", ""), True)
    adopted = call(
        adopt_kernel,
        (nhat_shape, inv_shape, unit_shape, cols_shape, taps_shape, shape((chans, units), bf16))
        + (weights_t, weights_t, shape((units, 8), f32)),
        1,
        (meta, note, half, other),
        (pltpu.VMEM((chans, cells), bf16),),
        cost=(10**9, 10**7),
    )
    next_nhat, next_inv, next_slope, next_cols, next_back, next_up, next_down_t = adopted[:7]
    cot_2, field, inner, outer = call(
        functools.partial(middle_kernel, top),
        (rows_shape, rows_shape, edge_shape, edge_shape),
        1,
        (meta, field, outer, inner, cot_top, back, next_cols, next_down_t, next_up)
        + (next_slope, next_nhat, next_inv),
        (padded, outgrads, lowgrads),
    )
    own_2 = lax.ppermute(cot_2, "section", swaps)
    inner, outer = halo(inner, outer)
    cot_1 = call(
        functools.partial(conv_kernel, top),
        rows_shape,
        1,
        (meta, field, outer, inner, cot_2, next_back),
        (padded,),
    )
    cot_1 = lax.ppermute(cot_1, "section", [(0, top), (top, 0), (1, 2), (2, 1)])
    own_1 = lax.ppermute(cot_1, "section", swaps)

    adopted = (next_cols, next_down_t, next_up, next_slope, next_nhat, next_inv)
    field, inner, outer = turn_field(0, cot_1, adopted)
    inner, outer = halo(inner, outer)

    part = shape(((2 * chans + 32) // 4, units), bf16)
    cot_own, field, inner, outer, keep, near, mate, far = call(
        last_kernel,
        (rows_shape, rows_shape, edge_shape, edge_shape, part, part, part, part),
        1,
        (meta, cot_top, own_2, own_1, field, outer, inner, cot_1, next_back, cols, layer_scale, down_t, down, up, slope, nhat, inv, hidden)
        + (source, acts_inner, acts_outer),
        (
            outgrads,
            lowgrads,
            pltpu.VMEM((units, width), f32),
            pltpu.VMEM((chans, width), f32),
            padded,
            pltpu.VMEM((2 * chans + 32, units), f32),
        ),
    )
    far = moved(far, ("z0", "x0"), True)
    near = moved(near, ("x0", "z0"), False)
    mate = moved(mate, ("", ""), True)
    total = added(keep, near, mate, far)
    orders = (("x1", "x0"), ("z2", "z1"), ("z1", "z2"), ("z0", "x1"))
    total, inner = lax.optimization_barrier((total, inner))
    total = added(total, moved(total, orders[0], False))
    inner = within(inner)
    total, inner, outer = lax.optimization_barrier((total, inner, outer))
    total = added(total, moved(total, orders[1], False))
    outer = across(outer)
    total, outer = lax.optimization_barrier((total, outer))
    total = added(total, moved(total, orders[2], False))
    result, sent = call(
        last_conv_kernel,
        (rows_shape, shape((CAP, chans, width), bf16)),
        1,
        (meta, field, inner, outer, cot_own, back),
        (padded,),
    )
    total, result, sent = lax.optimization_barrier((total, result, sent))
    total = added(total, moved(total, orders[3], False))
    arrived = lax.ppermute(sent, "tile", [(tile, (tile + 1) % TILES) for tile in range(TILES)])
    total, arrived = lax.optimization_barrier((total, arrived))
    slotted = call(
        slots_kernel,
        shape((owners.shape[0], chans, width), bf16),
        1,
        (meta, result, arrived),
    )
    far = moved(total, ("x0", "z0"), True)
    near = moved(total, ("x0", "z0"), False)
    mate = moved(total, ("", ""), True)
    grads = call(
        functools.partial(finish_kernel, scale),
        (
            shape((KS * KS, 1, chans), f32),
            shape((1, chans), f32),
            shape((1, chans, units), f32),
            shape((1, units), f32),
            shape((1, chans, units), f32),
            shape((1, chans), f32),
        ),
        1,
        (meta, total, near, mate, far),
        (pltpu.VMEM((2 * chans + 32, units), f32),),
    )

    grad_kernel, grad_gain, grad_up, grad_bias, grad_down, grad_scale = grads
    return (
        slotted[None],
        jnp.transpose(grad_kernel, (1, 0, 2)),
        grad_gain,
        grad_up,
        grad_bias,
        grad_down,
        grad_scale,
    )


def solution(mesh):
    in_specs = (
        P("section", "tile", None, None),
        P("tile", None, None),
        P("tile"),
        P("tile"),
        P("section", None, None),
        P("section", None),
        P("section", None, None),
        P("section", None),
        P("section", None, None),
        P("section", None),
    )
    out_specs = (
        P("section", "tile", None, None),
        P("section", None, None),
        P("section", None),
        P("section", None, None),
        P("section", None),
        P("section", None, None),
        P("section", None),
    )
    return jax.shard_map(body, mesh=mesh, in_specs=in_specs, out_specs=out_specs, check_vma=False)
```

```python
import functools
import math

import jax
import jax.numpy as jnp
from jax import lax
from jax.experimental import pallas as pl
from jax.experimental.pallas import tpu as pltpu
from jax.sharding import PartitionSpec as P

KS = 7
CAP = 2
SECTIONS = 4
TILES = 64
MARGIN = 3
BLOCK = 16
UNROLL = 12

norm_eps = 1e-06
tanh_root = math.sqrt(2.0 / math.pi)
cubic_coef = 0.044715

f32 = jnp.float32
bf16 = jnp.bfloat16

SECTION, ODD, KEEP, NEAR, MATE, FAR, OFFSET, INSIDE, LAND = range(9)
PLACES = 8
OWNERS = LAND + 5


def split_tile(tile):
    return tile % 2, tile // 2 % 4, tile // 8


def flip_x0(x):
    return x ^ 1


def flip_x1(x):
    return 3 - x


def flip_z0(z):
    return z ^ 1


def flip_z1(z):
    return 3 - z if z < 4 else 11 - z


def flip_z2(z):
    return 7 - z


flips = {"x0": flip_x0, "x1": flip_x1, "z0": flip_z0, "z1": flip_z1, "z2": flip_z2}


def moved(value, dims, swap):
    pairs = []
    for tile in range(TILES):
        core, x, z = split_tile(tile)
        dim = dims[core]
        if dim in ("x0", "x1"):
            x = flips[dim](x)
        elif dim:
            z = flips[dim](z)
        core = 1 - core if swap else core
        pairs.append((tile, z * 8 + x * 2 + core))
    return lax.ppermute(value, "tile", pairs)


def within(value):
    return lax.ppermute(value, "tile", [(tile, tile ^ 1) for tile in range(TILES)])


def across(value):
    pairs = [(tile, (tile + 1 if tile % 2 else tile - 1) % TILES) for tile in range(TILES)]
    return lax.ppermute(value, "tile", pairs)


def halo(inner, outer):
    inner = within(inner)
    return inner, across(outer)


def call(body, out_shape, smem, operands, scratch=(), cost=(0, 0)):
    spec = [pl.BlockSpec(memory_space=pltpu.SMEM)] * smem
    spec += [pl.BlockSpec(memory_space=pltpu.VMEM)] * (len(operands) - smem)
    outs = jax.tree.map(lambda _: pl.BlockSpec(memory_space=pltpu.VMEM), out_shape)
    return pl.pallas_call(
        body,
        out_shape=out_shape,
        in_specs=spec,
        out_specs=outs,
        scratch_shapes=list(scratch),
        compiler_params=pltpu.CompilerParams(vmem_limit_bytes=32 * 1024 * 1024),
        cost_estimate=pl.CostEstimate(flops=cost[0], bytes_accessed=cost[1], transcendentals=0),
    )(*operands)


def shape(dims, dtype):
    return jax.ShapeDtypeStruct(dims, dtype)


def fill_rows(rows_ref, meta, own, inner, outer):
    count = own.shape[0]
    odd = meta[ODD] == 1
    far_rows = jnp.where(meta[INSIDE] == 1, outer[...], jnp.zeros_like(outer))
    near_rows = inner[...]
    rows_ref[MARGIN : MARGIN + count] = own[...]
    rows_ref[:MARGIN] = jnp.where(odd, near_rows, far_rows)
    rows_ref[MARGIN + count : 2 * MARGIN + count] = jnp.where(odd, far_rows, near_rows)
    rows_ref[2 * MARGIN + count :] = jnp.zeros((1,) + own.shape[1:], bf16)


def edges(odd, value_ref, inner_ref, outer_ref):
    count = value_ref.shape[0]
    head = value_ref[:MARGIN]
    tail = value_ref[count - MARGIN :]
    inner_ref[...] = jnp.where(odd, head, tail)
    outer_ref[...] = jnp.where(odd, tail, head)


def fill_taps(cols, targets):
    high = cols[...].astype(bf16)
    low = (cols[...] - high.astype(f32)).astype(bf16)
    chans, taps = cols.shape
    wide = KS * 128
    tap = lax.broadcasted_iota(jnp.int32, (taps, wide), 0)
    place = lax.broadcasted_iota(jnp.int32, (taps, wide), 1)
    tap_col, tap_row = place >> 7, (place >> 4) & (PLACES - 1)
    own = lax.broadcasted_iota(jnp.int32, (chans, wide), 0) & (BLOCK - 1)
    diagonal = own == (lax.broadcasted_iota(jnp.int32, (chans, wide), 1) & (BLOCK - 1))
    for target, row in zip(targets, (tap_row, KS - 1 - tap_row)):
        if target is None:
            continue
        hit = (tap == row * KS + tap_col) & (tap_row < KS)
        spread = jnp.where(hit, 1.0, 0.0).astype(bf16)
        for half, value in enumerate((high, low)):
            filled = jnp.dot(value, spread, preferred_element_type=f32)
            filled = jnp.where(diagonal, filled, 0.0).astype(bf16)
            for block in range(chans // BLOCK):
                for col in range(KS):
                    target[
                        block, col * BLOCK : (col + 1) * BLOCK, half * 128 : (half + 1) * 128
                    ] = filled[block * BLOCK : (block + 1) * BLOCK, col * 128 : (col + 1) * 128]


def prepare_kernel(
    kernel, gain, layer, bias, up, down, cols, forth_ref, back_ref, up_t_ref, down_t_ref, bias_ref, lines_ref
):
    lines_ref[...] = jnp.zeros_like(lines_ref)
    lines_ref[: KS * KS] = kernel[...]
    lines_ref[KS * KS : KS * KS + 1] = gain[...]
    lines_ref[KS * KS + 1 : KS * KS + 2] = layer[...]
    cols[...] = jnp.transpose(lines_ref[...])
    up_t_ref[...] = jnp.transpose(up[...].astype(f32)).astype(bf16)
    down_t_ref[...] = jnp.transpose(down[...].astype(f32)).astype(bf16)
    bias_ref[...] = jnp.transpose(jnp.broadcast_to(bias[...], (8, bias.shape[1])))
    fill_taps(cols, (forth_ref, back_ref))


def stacked(rows_ref, start, count):
    rows = [rows_ref[row, pl.ds(start, BLOCK), :] for row in range(count + PLACES - 1)]
    return jnp.concatenate(
        [jnp.concatenate(rows[place : place + count], axis=1) for place in range(PLACES)], axis=0
    )


def taps_sum(rows_ref, taps_mat, block, count, backward):
    windows = stacked(rows_ref, pl.multiple_of(block * BLOCK, BLOCK), count)
    parts = jnp.dot(
        taps_mat[block], jnp.concatenate([windows, windows], axis=0), preferred_element_type=f32
    )
    sums = []
    for row in range(count):
        total = None
        for tap_col in range(KS):
            shift = (tap_col - MARGIN if backward else MARGIN - tap_col) % 128
            part = parts[tap_col * BLOCK : (tap_col + 1) * BLOCK, row * 128 : (row + 1) * 128]
            if shift:
                part = pltpu.roll(part, shift, 1)
            total = part if total is None else total + part
        sums.append(total)
    return sums


def forward_kernel(
    meta, acts, inner, outer, taps_mat, cols, up_t, bias, bias_row, nhat_ref, inv_ref, hidden_ref, slope_ref, note_ref, rows_ref, field_ref, normed_ref
):
    count, chans, width = acts.shape
    fill_rows(rows_ref, meta, acts, inner, outer)

    def step(index, carry):
        start = pl.multiple_of(index * BLOCK, BLOCK)
        sums = taps_sum(rows_ref, taps_mat, index, count, False)
        for row in range(count):
            field_ref[pl.ds(start, BLOCK), row * width : (row + 1) * width] = sums[row]
        return carry

    lax.fori_loop(0, chans // BLOCK, step, 0, unroll=UNROLL)
    gain = cols[:, KS * KS : KS * KS + 1]
    for row in range(count):
        part = slice(row * width, (row + 1) * width)
        field = field_ref[:, part]
        center = field - jnp.mean(field, axis=0, keepdims=True)
        inverse = 1.0 / jnp.sqrt(jnp.mean(center * center, axis=0, keepdims=True) + norm_eps)
        nhat = center * inverse
        nhat_ref[:, part] = nhat
        inv_ref[:, part] = inverse
        normed_ref[:, part] = (nhat * gain).astype(bf16)
    cells = count * width
    note_ref[:chans, :cells] = nhat_ref[...].astype(bf16)
    high, low = two_parts(cols[...])
    note_ref[:chans, cells:] = jnp.concatenate([high, low], axis=1).astype(bf16)
    parts = two_parts(bias_row[...])
    padding = jnp.zeros((1, bias_row.shape[1] - cells), f32)
    parts += two_parts(jnp.concatenate([inv_ref[...], padding], axis=1))
    rest = jnp.zeros((BLOCK - len(parts), bias_row.shape[1]), f32)
    note_ref[chans:] = jnp.concatenate([*parts, rest]).astype(bf16)
    mlp_forward(normed_ref, up_t, bias, hidden_ref, slope_ref)


def two_parts(value):
    high = value.astype(bf16).astype(f32)
    return [high, value - high]


def mlp_forward(normed_ref, up_t, bias, hidden_ref, slope_ref):
    units = up_t.shape[0]
    chunk = 128
    for first in range(0, units, chunk):
        part = slice(first, first + chunk)
        preact = jnp.dot(up_t[part], normed_ref[...], preferred_element_type=f32) + bias[part, :1]
        square = preact * preact
        hyper = jnp.tanh(preact * (tanh_root + tanh_root * cubic_coef * square))
        half = 0.5 + 0.5 * hyper
        if hidden_ref is not None:
            hidden_ref[part] = (preact * half).astype(bf16)
        slope = half * (
            1.0 + preact * (1.0 - hyper) * (tanh_root + 3.0 * cubic_coef * tanh_root * square)
        )
        slope_ref[part] = slope.astype(bf16)


def adopt_kernel(
    meta, note, half, other, nhat_ref, inv_ref, slope_ref, cols_ref, back_ref, up_ref, down_t_ref, up_t_ref, bias_ref, normed_ref
):
    chans, cells = nhat_ref.shape
    units = slope_ref.shape[0]
    taps = cols_ref.shape[1]

    @pl.when((meta[SECTION] == SECTIONS - 1) | (meta[SECTION] == 0))
    def _():
        odd = meta[ODD] == 1
        up = jnp.where(odd, other[...], half[...])
        up_ref[...] = up
        up_t_ref[...] = jnp.transpose(up.astype(f32)).astype(bf16)
        down = jnp.where(odd, half[...], other[...])
        down_t_ref[...] = jnp.transpose(down.astype(f32)).astype(bf16)
        nhat = note[:chans, :cells].astype(f32)
        nhat_ref[...] = nhat
        pieces = note[:chans, cells:].astype(f32)
        cols_ref[...] = pieces[:, :taps] + pieces[:, taps:]
        lines = note[chans:].astype(f32)
        bias_row = lines[0:1] + lines[1:2]
        inv_ref[...] = (lines[2:3] + lines[3:4])[:, :cells]
        bias_ref[...] = jnp.transpose(jnp.broadcast_to(bias_row, (8, units)))
        fill_taps(cols_ref, (None, back_ref))
        normed_ref[...] = (nhat * cols_ref[:, KS * KS : KS * KS + 1]).astype(bf16)
        mlp_forward(normed_ref, up_t_ref, bias_ref, None, slope_ref)


def mlp_backward(cots, meta, cols, down_t, up, slope, nhat, inv, out_ref, low_ref, field_ref, sums=None):
    width = cots[0].shape[1]
    count = len(cots)
    gain = cols[:, KS * KS : KS * KS + 1]
    layer = cols[:, KS * KS + 1 : KS * KS + 2]
    for row in range(count):
        wet = meta[LAND + row].astype(f32)
        out_ref[:, row * width : (row + 1) * width] = (cots[row] * layer * wet).astype(bf16)
    units = down_t.shape[0]
    chunk = 128
    for first in range(0, units, chunk):
        part = slice(first, first + chunk)
        pregrad = jnp.dot(down_t[part], out_ref[...], preferred_element_type=f32)
        pregrad = pregrad * slope[part].astype(f32)
        low_ref[part] = pregrad.astype(bf16)
        if sums is not None:
            sums[0][part] = sum(
                pregrad[:, row * width : (row + 1) * width] for row in range(count)
            )
    featgrad = jnp.dot(up[...], low_ref[...], preferred_element_type=f32)
    gains = None
    for row in range(count):
        part = slice(row * width, (row + 1) * width)
        feat = featgrad[:, part]
        own = nhat[:, part]
        scaled = feat * gain
        mean = jnp.mean(scaled, axis=0, keepdims=True)
        cross = jnp.mean(scaled * own, axis=0, keepdims=True)
        field_ref[row] = (inv[:, part] * (scaled - mean - own * cross)).astype(bf16)
        if sums is not None:
            term = feat * own
            gains = term if gains is None else gains + term
    if sums is not None:
        sums[1][...] = gains


def turn_kernel(
    section, meta, cot, cols, down_t, up, slope, nhat, inv, field_ref, inner_ref, outer_ref, out_ref, low_ref
):
    @pl.when(meta[SECTION] == section)
    def _():
        cots = [cot[row].astype(f32) for row in range(cot.shape[0])]
        mlp_backward(cots, meta, cols, down_t, up, slope, nhat, inv, out_ref, low_ref, field_ref)
        edges(meta[ODD] == 1, field_ref, inner_ref, outer_ref)


def conv_rows(meta, field, inner, outer, cot, taps_mat, result_ref, rows_ref):
    count, chans, width = field.shape
    fill_rows(rows_ref, meta, field, inner, outer)

    def step(index, carry):
        start = pl.multiple_of(index * BLOCK, BLOCK)
        sums = taps_sum(rows_ref, taps_mat, index, count, True)
        for row in range(count):
            own = cot[row, pl.ds(start, BLOCK), :].astype(f32)
            result_ref[row, pl.ds(start, BLOCK), :] = (own + sums[row]).astype(bf16)
        return carry

    lax.fori_loop(0, chans // BLOCK, step, 0, unroll=UNROLL)


def conv_kernel(section, meta, field, outer, inner, cot, taps_mat, result_ref, rows_ref):
    @pl.when(meta[SECTION] == section)
    def _():
        conv_rows(meta, field, inner, outer, cot, taps_mat, result_ref, rows_ref)


def middle_kernel(
    plane,
    meta,
    field,
    outer,
    inner,
    cot,
    taps_mat,
    cols,
    down_t,
    up,
    slope,
    nhat,
    inv,
    result_ref,
    field_ref,
    inner_ref,
    outer_ref,
    rows_ref,
    out_ref,
    low_ref,
):
    @pl.when(meta[SECTION] == plane)
    def _():
        conv_rows(meta, field, inner, outer, cot, taps_mat, result_ref, rows_ref)
        cots = [result_ref[row].astype(f32) for row in range(result_ref.shape[0])]
        mlp_backward(cots, meta, cols, down_t, up, slope, nhat, inv, out_ref, low_ref, field_ref)
        edges(meta[ODD] == 1, field_ref, inner_ref, outer_ref)


def last_conv_kernel(meta, field, inner, outer, cot, taps_mat, result_ref, sent_ref, rows_ref):
    conv_rows(meta, field, inner, outer, cot, taps_mat, result_ref, rows_ref)
    sent_ref[...] = jnp.zeros_like(sent_ref)
    rank = jnp.int32(0)
    for local in range(result_ref.shape[0]):
        kept = jnp.bool_(False)
        for slot in range(OWNERS, meta.shape[0]):
            kept = kept | (meta[slot] == meta[OFFSET] + local)
        sent = (meta[LAND + local] == 1) & jnp.logical_not(kept)
        for place in range(CAP):

            @pl.when(sent & (rank == place))
            def _():
                sent_ref[place] = result_ref[local]

        rank = rank + sent.astype(jnp.int32)


def slots_kernel(meta, result, arrived, slots_ref):
    for slot in range(slots_ref.shape[0]):
        slots_ref[slot] = arrived[min(slot, CAP - 1)]
        for local in range(result.shape[0]):

            @pl.when(meta[OWNERS + slot] == meta[OFFSET] + local)
            def _():
                slots_ref[slot] = result[local]


def last_kernel(
    meta,
    cot_top,
    cot_2,
    cot_1,
    turn_field,
    turn_outer,
    turn_inner,
    turn_cot,
    turn_mat,
    cols,
    layer_row,
    down_t,
    down,
    up,
    slope,
    nhat,
    inv,
    hidden,
    acts,
    inner,
    outer,
    cot_ref,
    field_ref,
    field_inner_ref,
    field_outer_ref,
    keep_ref,
    near_ref,
    mate_ref,
    far_ref,
    out_ref,
    low_ref,
    bias_ref,
    gain_ref,
    rows_ref,
    packed_ref,
):
    count, chans, width = acts.shape
    units = slope.shape[0]
    odd = meta[ODD] == 1
    for section, cot in ((3, cot_top), (2, cot_2), (1, cot_1)):

        @pl.when(meta[SECTION] == section)
        def _():
            cot_ref[...] = cot[...]

    @pl.when(meta[SECTION] == 0)
    def _():
        conv_rows(meta, turn_field, turn_inner, turn_outer, turn_cot, turn_mat, cot_ref, rows_ref)

    cots = [cot_ref[row].astype(f32) for row in range(count)]
    mlp_backward(
        cots, meta, cols, down_t, up, slope, nhat, inv, out_ref, low_ref, field_ref, (bias_ref, gain_ref)
    )
    edges(odd, field_ref, field_inner_ref, field_outer_ref)
    gain = cols[:, KS * KS : KS * KS + 1]
    normed = (nhat[...] * gain).astype(bf16)
    turned = (((1,), (1,)), ((), ()))
    grad_up = lax.dot_general(normed, low_ref[...], turned, preferred_element_type=f32)
    packed_ref[:chans] = grad_up
    grad_down = lax.dot_general(out_ref[...], hidden[...], turned, preferred_element_type=f32)
    packed_ref[chans : 2 * chans] = grad_down
    product = grad_down * down[...].astype(f32)
    product = sum(product[:, first : first + 128] for first in range(0, units, 128))

    fill_rows(rows_ref, meta, acts, inner, outer)
    base = 2 * chans
    shifts = [(tap_col - MARGIN) % 128 for tap_col in range(KS)]
    own = lax.broadcasted_iota(jnp.int32, (BLOCK, 128), 0)
    diagonal = own == (lax.broadcasted_iota(jnp.int32, (BLOCK, 128), 1) & (BLOCK - 1))
    for block in range(chans // BLOCK):
        start = block * BLOCK
        windows = stacked(rows_ref, start, count)
        fields = [field_ref[row, start : start + BLOCK, :].astype(f32) for row in range(count)]
        rolled = jnp.concatenate(
            [
                jnp.concatenate(
                    [pltpu.roll(field, shift, 1) if shift else field for field in fields], axis=1
                )
                for shift in shifts
            ],
            axis=0,
        ).astype(bf16)
        crossed = lax.dot_general(rolled, windows, turned, preferred_element_type=f32)
        first = base + block // 6 * 8
        lanes = slice(block % 6 * 128, block % 6 * 128 + 128)
        for tap_col in range(KS):
            part = jnp.where(diagonal, crossed[tap_col * BLOCK : (tap_col + 1) * BLOCK], 0.0)
            packed_ref[first + tap_col : first + tap_col + 1, lanes] = jnp.sum(
                part, axis=0, keepdims=True
            )
        packed_ref[first + KS : first + PLACES, lanes] = jnp.zeros((1, 128), f32)
    bias_row = jnp.sum(jnp.transpose(bias_ref[...]), axis=0, keepdims=True)
    gain_row = jnp.sum(jnp.transpose(gain_ref[...]), axis=0, keepdims=True)
    scale_row = jnp.sum(jnp.transpose(product), axis=0, keepdims=True) / layer_row[...]
    packed_ref[base + 16 :] = jnp.zeros((packed_ref.shape[0] - base - 16, units), f32)
    packed_ref[base + 16 : base + 17] = bias_row
    packed_ref[base + 17 : base + 18, :chans] = gain_row
    packed_ref[base + 17 : base + 18, 256 : 256 + chans] = scale_row
    part_rows = keep_ref.shape[0]
    for place, target in ((KEEP, keep_ref), (NEAR, near_ref), (MATE, mate_ref), (FAR, far_ref)):
        start = pl.multiple_of(meta[place] * part_rows, 8)
        target[...] = packed_ref[pl.ds(start, part_rows), :].astype(bf16)


def finish_kernel(
    scale, meta, keep, near, mate, far, kernel_ref, gain_ref, up_ref, bias_ref, down_ref, scale_ref, packed_ref
):
    part_rows = keep.shape[0]
    for place, source in ((KEEP, keep), (NEAR, near), (MATE, mate), (FAR, far)):
        start = pl.multiple_of(meta[place] * part_rows, 8)
        packed_ref[pl.ds(start, part_rows), :] = source[...].astype(f32) * scale
    chans = up_ref.shape[1]
    base = 2 * chans
    up_ref[0] = packed_ref[:chans]
    down_ref[0] = packed_ref[chans:base]
    lane = lax.broadcasted_iota(jnp.int32, (PLACES, 128), 1) >> 4
    blocks = chans // BLOCK
    for tap_row in range(KS):
        halves = []
        for first in range(0, blocks, PLACES):
            half = jnp.zeros((PLACES, 128), f32)
            for block in range(first, min(first + PLACES, blocks)):
                rows = slice(base + block // 6 * 8, base + block // 6 * 8 + 8)
                part = packed_ref[rows, block % 6 * 128 : block % 6 * 128 + 128]
                shift = (block - first - tap_row) * BLOCK % 128
                if shift:
                    part = pltpu.roll(part, shift, 1)
                half = jnp.where(lane == block - first, part, half)
            halves.append(half)
        line = jnp.concatenate(halves, axis=1)
        for tap_col in range(KS):
            kernel_ref[tap_row * KS + tap_col] = line[tap_col : tap_col + 1, :chans]
    bias_ref[...] = packed_ref[base + 16 : base + 17]
    gain_ref[...] = packed_ref[base + 17 : base + 18, :chans]
    scale_ref[...] = packed_ref[base + 17 : base + 18, 256 : 256 + chans]


def added(*values):
    return sum(value.astype(f32) for value in values).astype(bf16)


def body(acts, cot_top, land, owners, dw_kernel, ln_gain, w_up, b_up, w_down, layer_scale):
    source = acts[0]
    count, chans, width = source.shape
    units = w_up.shape[2]
    cells = count * width
    tile_now = lax.axis_index("tile")
    section_now = lax.axis_index("section")
    scale = 1.0 / math.sqrt(lax.axis_size("tile") * cells)
    core, x, z = split_tile(tile_now)
    bit_x, bit_z = (x + 1) // 2 % 2, (z + 1) // 2 % 2
    bit = jnp.where(core == 0, bit_x, bit_z)
    mate_bit = jnp.where(core == 0, bit_z, bit_x)
    numbers = [
        section_now,
        core,
        2 * core + bit,
        2 * core + 1 - bit,
        2 * (1 - core) + mate_bit,
        2 * (1 - core) + 1 - mate_bit,
        tile_now * count,
        jnp.where((tile_now == 0) | (tile_now == TILES - 1), 0, 1),
    ]
    meta = jnp.concatenate([jnp.stack(numbers).astype(jnp.int32), land, owners])

    odd = core == 1
    head, tail = source[:MARGIN], source[count - MARGIN :]
    acts_inner, acts_outer = halo(jnp.where(odd, head, tail), jnp.where(odd, tail, head))
    up, down = w_up[0], w_down[0]
    swaps = [(section, section ^ 1) for section in range(SECTIONS)]
    taps_shape = shape((chans // BLOCK, KS * BLOCK, 256), bf16)
    weights_t = shape((units, chans), bf16)
    cols_shape = shape((chans, 64), f32)
    cols, forth, back, up_t, down_t, bias = call(
        prepare_kernel,
        (cols_shape, taps_shape, taps_shape, weights_t, weights_t, shape((units, 8), f32)),
        0,
        (dw_kernel[0], ln_gain, layer_scale, b_up, up, down),
        (pltpu.VMEM((64, chans), f32),),
        cost=(10**9, 10**7),
    )
    half = lax.ppermute(jnp.where(odd, down, up), "section", swaps)

    padded = pltpu.VMEM((count + PLACES - 1, chans, width), bf16)
    nhat_shape, inv_shape = shape((chans, cells), f32), shape((1, cells), f32)
    unit_shape = shape((units, cells), bf16)
    nhat, inv, hidden, slope, own_note = call(
        forward_kernel,
        (nhat_shape, inv_shape, unit_shape, unit_shape, shape((chans + BLOCK, units), bf16)),
        1,
        (meta, source, acts_inner, acts_outer, forth, cols, up_t, bias, b_up),
        (padded, pltpu.VMEM((chans, cells), f32), pltpu.VMEM((chans, cells), bf16)),
    )
    note = lax.ppermute(own_note, "section", swaps)

    rows_shape = shape((count, chans, width), bf16)
    edge_shape = shape((MARGIN, chans, width), bf16)
    outgrads = pltpu.VMEM((chans, cells), bf16)
    lowgrads = pltpu.VMEM((units, cells), bf16)

    def turn_field(plane, cot, params):
        field_cols, field_down_t, field_up, field_slope, field_nhat, field_inv = params
        return call(
            functools.partial(turn_kernel, plane),
            (rows_shape, edge_shape, edge_shape),
            1,
            (meta, cot, field_cols, field_down_t, field_up, field_slope, field_nhat, field_inv),
            (outgrads, lowgrads),
        )

    top = SECTIONS - 1
    field, inner, outer = turn_field(top, cot_top, (cols, down_t, up, slope, nhat, inv))
    half, field = lax.optimization_barrier((half, field))
    inner, outer = halo(inner, outer)
    other = moved(half, ("", ""), True)
    adopted = call(
        adopt_kernel,
        (nhat_shape, inv_shape, unit_shape, cols_shape, taps_shape, shape((chans, units), bf16))
        + (weights_t, weights_t, shape((units, 8), f32)),
        1,
        (meta, note, half, other),
        (pltpu.VMEM((chans, cells), bf16),),
        cost=(10**9, 10**7),
    )
    next_nhat, next_inv, next_slope, next_cols, next_back, next_up, next_down_t = adopted[:7]
    cot_2, field, inner, outer = call(
        functools.partial(middle_kernel, top),
        (rows_shape, rows_shape, edge_shape, edge_shape),
        1,
        (meta, field, outer, inner, cot_top, back, next_cols, next_down_t, next_up)
        + (next_slope, next_nhat, next_inv),
        (padded, outgrads, lowgrads),
    )
    own_2 = lax.ppermute(cot_2, "section", swaps)
    inner, outer = halo(inner, outer)
    cot_1 = call(
        functools.partial(conv_kernel, top),
        rows_shape,
        1,
        (meta, field, outer, inner, cot_2, next_back),
        (padded,),
    )
    cot_1 = lax.ppermute(cot_1, "section", [(0, top), (top, 0), (1, 2), (2, 1)])
    own_1 = lax.ppermute(cot_1, "section", swaps)

    adopted = (next_cols, next_down_t, next_up, next_slope, next_nhat, next_inv)
    field, inner, outer = turn_field(0, cot_1, adopted)
    inner, outer = halo(inner, outer)

    part = shape(((2 * chans + 32) // 4, units), bf16)
    cot_own, field, inner, outer, keep, near, mate, far = call(
        last_kernel,
        (rows_shape, rows_shape, edge_shape, edge_shape, part, part, part, part),
        1,
        (meta, cot_top, own_2, own_1, field, outer, inner, cot_1, next_back, cols, layer_scale, down_t, down, up, slope, nhat, inv, hidden)
        + (source, acts_inner, acts_outer),
        (
            outgrads,
            lowgrads,
            pltpu.VMEM((units, width), f32),
            pltpu.VMEM((chans, width), f32),
            padded,
            pltpu.VMEM((2 * chans + 32, units), f32),
        ),
    )
    far = moved(far, ("z0", "x0"), True)
    near = moved(near, ("x0", "z0"), False)
    mate = moved(mate, ("", ""), True)
    total = added(keep, near, mate, far)
    orders = (("x1", "z1"), ("z0", "z2"), ("z1", "x0"), ("z2", "x1"))
    total, outer = lax.optimization_barrier((total, outer))
    total = added(total, moved(total, orders[0], False))
    outer = across(outer)
    total, inner, outer = lax.optimization_barrier((total, inner, outer))
    total = added(total, moved(total, orders[1], False))
    inner = within(inner)
    total, inner = lax.optimization_barrier((total, inner))
    total = added(total, moved(total, orders[2], False))
    result, sent = call(
        last_conv_kernel,
        (rows_shape, shape((CAP, chans, width), bf16)),
        1,
        (meta, field, inner, outer, cot_own, back),
        (padded,),
    )
    total, result, sent = lax.optimization_barrier((total, result, sent))
    total = added(total, moved(total, orders[3], False))
    arrived = lax.ppermute(sent, "tile", [(tile, (tile + 1) % TILES) for tile in range(TILES)])
    total, arrived = lax.optimization_barrier((total, arrived))
    slotted = call(
        slots_kernel,
        shape((owners.shape[0], chans, width), bf16),
        1,
        (meta, result, arrived),
    )
    far = moved(total, ("x0", "z0"), True)
    near = moved(total, ("x0", "z0"), False)
    mate = moved(total, ("", ""), True)
    grads = call(
        functools.partial(finish_kernel, scale),
        (
            shape((KS * KS, 1, chans), f32),
            shape((1, chans), f32),
            shape((1, chans, units), f32),
            shape((1, units), f32),
            shape((1, chans, units), f32),
            shape((1, chans), f32),
        ),
        1,
        (meta, total, near, mate, far),
        (pltpu.VMEM((2 * chans + 32, units), f32),),
    )

    grad_kernel, grad_gain, grad_up, grad_bias, grad_down, grad_scale = grads
    return (
        slotted[None],
        jnp.transpose(grad_kernel, (1, 0, 2)),
        grad_gain,
        grad_up,
        grad_bias,
        grad_down,
        grad_scale,
    )


def solution(mesh):
    in_specs = (
        P("section", "tile", None, None),
        P("tile", None, None),
        P("tile"),
        P("tile"),
        P("section", None, None),
        P("section", None),
        P("section", None, None),
        P("section", None),
        P("section", None, None),
        P("section", None),
    )
    out_specs = (
        P("section", "tile", None, None),
        P("section", None, None),
        P("section", None),
        P("section", None, None),
        P("section", None),
        P("section", None, None),
        P("section", None),
    )
    return jax.shard_map(body, mesh=mesh, in_specs=in_specs, out_specs=out_specs, check_vma=False)
```

```python
import functools
import math

import jax
import jax.numpy as jnp
from jax import lax
from jax.experimental import pallas as pl
from jax.experimental.pallas import tpu as pltpu
from jax.sharding import PartitionSpec as P

KS = 7
CAP = 2
SECTIONS = 4
TILES = 64
MARGIN = 3
BLOCK = 16
UNROLL = 12

norm_eps = 1e-06
tanh_root = math.sqrt(2.0 / math.pi)
cubic_coef = 0.044715

f32 = jnp.float32
bf16 = jnp.bfloat16

SECTION, ODD, KEEP, NEAR, MATE, FAR, OFFSET, INSIDE, LAND = range(9)
PLACES = 8
OWNERS = LAND + 5


def split_tile(tile):
    return tile % 2, tile // 2 % 4, tile // 8


def flip_x0(x):
    return x ^ 1


def flip_x1(x):
    return 3 - x


def flip_z0(z):
    return z ^ 1


def flip_z1(z):
    return 3 - z if z < 4 else 11 - z


def flip_z2(z):
    return 7 - z


flips = {"x0": flip_x0, "x1": flip_x1, "z0": flip_z0, "z1": flip_z1, "z2": flip_z2}


def moved(value, dims, swap):
    pairs = []
    for tile in range(TILES):
        core, x, z = split_tile(tile)
        dim = dims[core]
        if dim in ("x0", "x1"):
            x = flips[dim](x)
        elif dim:
            z = flips[dim](z)
        core = 1 - core if swap else core
        pairs.append((tile, z * 8 + x * 2 + core))
    return lax.ppermute(value, "tile", pairs)


def within(value):
    return lax.ppermute(value, "tile", [(tile, tile ^ 1) for tile in range(TILES)])


def across(value):
    pairs = [(tile, (tile + 1 if tile % 2 else tile - 1) % TILES) for tile in range(TILES)]
    return lax.ppermute(value, "tile", pairs)


def halo(inner, outer):
    inner = within(inner)
    return inner, across(outer)


def call(body, out_shape, smem, operands, scratch=(), cost=(0, 0)):
    spec = [pl.BlockSpec(memory_space=pltpu.SMEM)] * smem
    spec += [pl.BlockSpec(memory_space=pltpu.VMEM)] * (len(operands) - smem)
    outs = jax.tree.map(lambda _: pl.BlockSpec(memory_space=pltpu.VMEM), out_shape)
    return pl.pallas_call(
        body,
        out_shape=out_shape,
        in_specs=spec,
        out_specs=outs,
        scratch_shapes=list(scratch),
        compiler_params=pltpu.CompilerParams(vmem_limit_bytes=32 * 1024 * 1024),
        cost_estimate=pl.CostEstimate(flops=cost[0], bytes_accessed=cost[1], transcendentals=0),
    )(*operands)


def shape(dims, dtype):
    return jax.ShapeDtypeStruct(dims, dtype)


def fill_rows(rows_ref, meta, own, inner, outer):
    count = own.shape[0]
    odd = meta[ODD] == 1
    far_rows = jnp.where(meta[INSIDE] == 1, outer[...], jnp.zeros_like(outer))
    near_rows = inner[...]
    rows_ref[MARGIN : MARGIN + count] = own[...]
    rows_ref[:MARGIN] = jnp.where(odd, near_rows, far_rows)
    rows_ref[MARGIN + count : 2 * MARGIN + count] = jnp.where(odd, far_rows, near_rows)
    rows_ref[2 * MARGIN + count :] = jnp.zeros((1,) + own.shape[1:], bf16)


def edges(odd, value_ref, inner_ref, outer_ref):
    count = value_ref.shape[0]
    head = value_ref[:MARGIN]
    tail = value_ref[count - MARGIN :]
    inner_ref[...] = jnp.where(odd, head, tail)
    outer_ref[...] = jnp.where(odd, tail, head)


def fill_taps(cols, targets):
    high = cols[...].astype(bf16)
    low = (cols[...] - high.astype(f32)).astype(bf16)
    chans, taps = cols.shape
    wide = KS * 128
    tap = lax.broadcasted_iota(jnp.int32, (taps, wide), 0)
    place = lax.broadcasted_iota(jnp.int32, (taps, wide), 1)
    tap_col, tap_row = place >> 7, (place >> 4) & (PLACES - 1)
    own = lax.broadcasted_iota(jnp.int32, (chans, wide), 0) & (BLOCK - 1)
    diagonal = own == (lax.broadcasted_iota(jnp.int32, (chans, wide), 1) & (BLOCK - 1))
    for target, row in zip(targets, (tap_row, KS - 1 - tap_row)):
        if target is None:
            continue
        hit = (tap == row * KS + tap_col) & (tap_row < KS)
        spread = jnp.where(hit, 1.0, 0.0).astype(bf16)
        for half, value in enumerate((high, low)):
            filled = jnp.dot(value, spread, preferred_element_type=f32)
            filled = jnp.where(diagonal, filled, 0.0).astype(bf16)
            for block in range(chans // BLOCK):
                for col in range(KS):
                    target[
                        block, col * BLOCK : (col + 1) * BLOCK, half * 128 : (half + 1) * 128
                    ] = filled[block * BLOCK : (block + 1) * BLOCK, col * 128 : (col + 1) * 128]


def prepare_kernel(
    kernel, gain, layer, bias, up, down, cols, forth_ref, back_ref, up_t_ref, down_t_ref, bias_ref, lines_ref
):
    lines_ref[...] = jnp.zeros_like(lines_ref)
    lines_ref[: KS * KS] = kernel[...]
    lines_ref[KS * KS : KS * KS + 1] = gain[...]
    lines_ref[KS * KS + 1 : KS * KS + 2] = layer[...]
    cols[...] = jnp.transpose(lines_ref[...])
    up_t_ref[...] = jnp.transpose(up[...].astype(f32)).astype(bf16)
    down_t_ref[...] = jnp.transpose(down[...].astype(f32)).astype(bf16)
    bias_ref[...] = jnp.transpose(jnp.broadcast_to(bias[...], (8, bias.shape[1])))
    fill_taps(cols, (forth_ref, back_ref))


def stacked(rows_ref, start, count):
    rows = [rows_ref[row, pl.ds(start, BLOCK), :] for row in range(count + PLACES - 1)]
    return jnp.concatenate(
        [jnp.concatenate(rows[place : place + count], axis=1) for place in range(PLACES)], axis=0
    )


def taps_sum(rows_ref, taps_mat, block, count, backward):
    windows = stacked(rows_ref, pl.multiple_of(block * BLOCK, BLOCK), count)
    parts = jnp.dot(
        taps_mat[block], jnp.concatenate([windows, windows], axis=0), preferred_element_type=f32
    )
    sums = []
    for row in range(count):
        total = None
        for tap_col in range(KS):
            shift = (tap_col - MARGIN if backward else MARGIN - tap_col) % 128
            part = parts[tap_col * BLOCK : (tap_col + 1) * BLOCK, row * 128 : (row + 1) * 128]
            if shift:
                part = pltpu.roll(part, shift, 1)
            total = part if total is None else total + part
        sums.append(total)
    return sums


def forward_kernel(
    meta, acts, inner, outer, taps_mat, cols, up_t, bias, bias_row, nhat_ref, inv_ref, hidden_ref, slope_ref, note_ref, rows_ref, field_ref, normed_ref
):
    count, chans, width = acts.shape
    fill_rows(rows_ref, meta, acts, inner, outer)

    def step(index, carry):
        start = pl.multiple_of(index * BLOCK, BLOCK)
        sums = taps_sum(rows_ref, taps_mat, index, count, False)
        for row in range(count):
            field_ref[pl.ds(start, BLOCK), row * width : (row + 1) * width] = sums[row]
        return carry

    lax.fori_loop(0, chans // BLOCK, step, 0, unroll=UNROLL)
    gain = cols[:, KS * KS : KS * KS + 1]
    for row in range(count):
        part = slice(row * width, (row + 1) * width)
        field = field_ref[:, part]
        center = field - jnp.mean(field, axis=0, keepdims=True)
        inverse = 1.0 / jnp.sqrt(jnp.mean(center * center, axis=0, keepdims=True) + norm_eps)
        nhat = center * inverse
        nhat_ref[:, part] = nhat
        inv_ref[:, part] = inverse
        normed_ref[:, part] = (nhat * gain).astype(bf16)
    cells = count * width
    note_ref[:chans, :cells] = nhat_ref[...].astype(bf16)
    high, low = two_parts(cols[...])
    note_ref[:chans, cells:] = jnp.concatenate([high, low], axis=1).astype(bf16)
    parts = two_parts(bias_row[...])
    padding = jnp.zeros((1, bias_row.shape[1] - cells), f32)
    parts += two_parts(jnp.concatenate([inv_ref[...], padding], axis=1))
    rest = jnp.zeros((BLOCK - len(parts), bias_row.shape[1]), f32)
    note_ref[chans:] = jnp.concatenate([*parts, rest]).astype(bf16)
    mlp_forward(normed_ref, up_t, bias, hidden_ref, slope_ref)


def two_parts(value):
    high = value.astype(bf16).astype(f32)
    return [high, value - high]


def mlp_forward(normed_ref, up_t, bias, hidden_ref, slope_ref):
    units = up_t.shape[0]
    chunk = 128
    for first in range(0, units, chunk):
        part = slice(first, first + chunk)
        preact = jnp.dot(up_t[part], normed_ref[...], preferred_element_type=f32) + bias[part, :1]
        square = preact * preact
        hyper = jnp.tanh(preact * (tanh_root + tanh_root * cubic_coef * square))
        half = 0.5 + 0.5 * hyper
        if hidden_ref is not None:
            hidden_ref[part] = (preact * half).astype(bf16)
        slope = half * (
            1.0 + preact * (1.0 - hyper) * (tanh_root + 3.0 * cubic_coef * tanh_root * square)
        )
        slope_ref[part] = slope.astype(bf16)


def adopt_kernel(
    meta, note, half, other, nhat_ref, inv_ref, slope_ref, cols_ref, back_ref, up_ref, down_t_ref, up_t_ref, bias_ref, normed_ref
):
    chans, cells = nhat_ref.shape
    units = slope_ref.shape[0]
    taps = cols_ref.shape[1]

    @pl.when((meta[SECTION] == SECTIONS - 1) | (meta[SECTION] == 0))
    def _():
        odd = meta[ODD] == 1
        up = jnp.where(odd, other[...], half[...])
        up_ref[...] = up
        up_t_ref[...] = jnp.transpose(up.astype(f32)).astype(bf16)
        down = jnp.where(odd, half[...], other[...])
        down_t_ref[...] = jnp.transpose(down.astype(f32)).astype(bf16)
        nhat = note[:chans, :cells].astype(f32)
        nhat_ref[...] = nhat
        pieces = note[:chans, cells:].astype(f32)
        cols_ref[...] = pieces[:, :taps] + pieces[:, taps:]
        lines = note[chans:].astype(f32)
        bias_row = lines[0:1] + lines[1:2]
        inv_ref[...] = (lines[2:3] + lines[3:4])[:, :cells]
        bias_ref[...] = jnp.transpose(jnp.broadcast_to(bias_row, (8, units)))
        fill_taps(cols_ref, (None, back_ref))
        normed_ref[...] = (nhat * cols_ref[:, KS * KS : KS * KS + 1]).astype(bf16)
        mlp_forward(normed_ref, up_t_ref, bias_ref, None, slope_ref)


def mlp_backward(cots, meta, cols, down_t, up, slope, nhat, inv, out_ref, low_ref, field_ref, sums=None):
    width = cots[0].shape[1]
    count = len(cots)
    gain = cols[:, KS * KS : KS * KS + 1]
    layer = cols[:, KS * KS + 1 : KS * KS + 2]
    for row in range(count):
        wet = meta[LAND + row].astype(f32)
        out_ref[:, row * width : (row + 1) * width] = (cots[row] * layer * wet).astype(bf16)
    units = down_t.shape[0]
    chunk = 128
    for first in range(0, units, chunk):
        part = slice(first, first + chunk)
        pregrad = jnp.dot(down_t[part], out_ref[...], preferred_element_type=f32)
        pregrad = pregrad * slope[part].astype(f32)
        low_ref[part] = pregrad.astype(bf16)
        if sums is not None:
            sums[0][part] = sum(
                pregrad[:, row * width : (row + 1) * width] for row in range(count)
            )
    featgrad = jnp.dot(up[...], low_ref[...], preferred_element_type=f32)
    gains = None
    for row in range(count):
        part = slice(row * width, (row + 1) * width)
        feat = featgrad[:, part]
        own = nhat[:, part]
        scaled = feat * gain
        mean = jnp.mean(scaled, axis=0, keepdims=True)
        cross = jnp.mean(scaled * own, axis=0, keepdims=True)
        field_ref[row] = (inv[:, part] * (scaled - mean - own * cross)).astype(bf16)
        if sums is not None:
            term = feat * own
            gains = term if gains is None else gains + term
    if sums is not None:
        sums[1][...] = gains


def turn_kernel(
    section, meta, cot, cols, down_t, up, slope, nhat, inv, field_ref, inner_ref, outer_ref, out_ref, low_ref
):
    @pl.when(meta[SECTION] == section)
    def _():
        cots = [cot[row].astype(f32) for row in range(cot.shape[0])]
        mlp_backward(cots, meta, cols, down_t, up, slope, nhat, inv, out_ref, low_ref, field_ref)
        edges(meta[ODD] == 1, field_ref, inner_ref, outer_ref)


def conv_rows(meta, field, inner, outer, cot, taps_mat, result_ref, rows_ref):
    count, chans, width = field.shape
    fill_rows(rows_ref, meta, field, inner, outer)

    def step(index, carry):
        start = pl.multiple_of(index * BLOCK, BLOCK)
        sums = taps_sum(rows_ref, taps_mat, index, count, True)
        for row in range(count):
            own = cot[row, pl.ds(start, BLOCK), :].astype(f32)
            result_ref[row, pl.ds(start, BLOCK), :] = (own + sums[row]).astype(bf16)
        return carry

    lax.fori_loop(0, chans // BLOCK, step, 0, unroll=UNROLL)


def conv_kernel(section, meta, field, outer, inner, cot, taps_mat, result_ref, rows_ref):
    @pl.when(meta[SECTION] == section)
    def _():
        conv_rows(meta, field, inner, outer, cot, taps_mat, result_ref, rows_ref)


def middle_kernel(
    plane,
    meta,
    field,
    outer,
    inner,
    cot,
    taps_mat,
    cols,
    down_t,
    up,
    slope,
    nhat,
    inv,
    result_ref,
    field_ref,
    inner_ref,
    outer_ref,
    rows_ref,
    out_ref,
    low_ref,
):
    @pl.when(meta[SECTION] == plane)
    def _():
        conv_rows(meta, field, inner, outer, cot, taps_mat, result_ref, rows_ref)
        cots = [result_ref[row].astype(f32) for row in range(result_ref.shape[0])]
        mlp_backward(cots, meta, cols, down_t, up, slope, nhat, inv, out_ref, low_ref, field_ref)
        edges(meta[ODD] == 1, field_ref, inner_ref, outer_ref)


def last_conv_kernel(meta, field, inner, outer, cot, taps_mat, result_ref, sent_ref, rows_ref):
    conv_rows(meta, field, inner, outer, cot, taps_mat, result_ref, rows_ref)
    sent_ref[...] = jnp.zeros_like(sent_ref)
    rank = jnp.int32(0)
    for local in range(result_ref.shape[0]):
        kept = jnp.bool_(False)
        for slot in range(OWNERS, meta.shape[0]):
            kept = kept | (meta[slot] == meta[OFFSET] + local)
        sent = (meta[LAND + local] == 1) & jnp.logical_not(kept)
        for place in range(CAP):

            @pl.when(sent & (rank == place))
            def _():
                sent_ref[place] = result_ref[local]

        rank = rank + sent.astype(jnp.int32)


def slots_kernel(meta, result, arrived, slots_ref):
    for slot in range(slots_ref.shape[0]):
        slots_ref[slot] = arrived[min(slot, CAP - 1)]
        for local in range(result.shape[0]):

            @pl.when(meta[OWNERS + slot] == meta[OFFSET] + local)
            def _():
                slots_ref[slot] = result[local]


def last_kernel(
    meta,
    cot_top,
    cot_2,
    cot_1,
    turn_field,
    turn_outer,
    turn_inner,
    turn_cot,
    turn_mat,
    cols,
    layer_row,
    down_t,
    down,
    up,
    slope,
    nhat,
    inv,
    hidden,
    acts,
    inner,
    outer,
    cot_ref,
    field_ref,
    field_inner_ref,
    field_outer_ref,
    keep_ref,
    near_ref,
    mate_ref,
    far_ref,
    out_ref,
    low_ref,
    bias_ref,
    gain_ref,
    rows_ref,
    packed_ref,
):
    count, chans, width = acts.shape
    units = slope.shape[0]
    odd = meta[ODD] == 1
    for section, cot in ((3, cot_top), (2, cot_2), (1, cot_1)):

        @pl.when(meta[SECTION] == section)
        def _():
            cot_ref[...] = cot[...]

    @pl.when(meta[SECTION] == 0)
    def _():
        conv_rows(meta, turn_field, turn_inner, turn_outer, turn_cot, turn_mat, cot_ref, rows_ref)

    cots = [cot_ref[row].astype(f32) for row in range(count)]
    mlp_backward(
        cots, meta, cols, down_t, up, slope, nhat, inv, out_ref, low_ref, field_ref, (bias_ref, gain_ref)
    )
    edges(odd, field_ref, field_inner_ref, field_outer_ref)
    gain = cols[:, KS * KS : KS * KS + 1]
    normed = (nhat[...] * gain).astype(bf16)
    turned = (((1,), (1,)), ((), ()))
    grad_up = lax.dot_general(normed, low_ref[...], turned, preferred_element_type=f32)
    packed_ref[:chans] = grad_up
    grad_down = lax.dot_general(out_ref[...], hidden[...], turned, preferred_element_type=f32)
    packed_ref[chans : 2 * chans] = grad_down
    product = grad_down * down[...].astype(f32)
    product = sum(product[:, first : first + 128] for first in range(0, units, 128))

    fill_rows(rows_ref, meta, acts, inner, outer)
    base = 2 * chans
    shifts = [(tap_col - MARGIN) % 128 for tap_col in range(KS)]
    own = lax.broadcasted_iota(jnp.int32, (BLOCK, 128), 0)
    diagonal = own == (lax.broadcasted_iota(jnp.int32, (BLOCK, 128), 1) & (BLOCK - 1))
    for block in range(chans // BLOCK):
        start = block * BLOCK
        windows = stacked(rows_ref, start, count)
        fields = [field_ref[row, start : start + BLOCK, :].astype(f32) for row in range(count)]
        rolled = jnp.concatenate(
            [
                jnp.concatenate(
                    [pltpu.roll(field, shift, 1) if shift else field for field in fields], axis=1
                )
                for shift in shifts
            ],
            axis=0,
        ).astype(bf16)
        crossed = lax.dot_general(rolled, windows, turned, preferred_element_type=f32)
        first = base + block // 6 * 8
        lanes = slice(block % 6 * 128, block % 6 * 128 + 128)
        for tap_col in range(KS):
            part = jnp.where(diagonal, crossed[tap_col * BLOCK : (tap_col + 1) * BLOCK], 0.0)
            packed_ref[first + tap_col : first + tap_col + 1, lanes] = jnp.sum(
                part, axis=0, keepdims=True
            )
        packed_ref[first + KS : first + PLACES, lanes] = jnp.zeros((1, 128), f32)
    bias_row = jnp.sum(jnp.transpose(bias_ref[...]), axis=0, keepdims=True)
    gain_row = jnp.sum(jnp.transpose(gain_ref[...]), axis=0, keepdims=True)
    scale_row = jnp.sum(jnp.transpose(product), axis=0, keepdims=True) / layer_row[...]
    packed_ref[base + 16 :] = jnp.zeros((packed_ref.shape[0] - base - 16, units), f32)
    packed_ref[base + 16 : base + 17] = bias_row
    packed_ref[base + 17 : base + 18, :chans] = gain_row
    packed_ref[base + 17 : base + 18, 256 : 256 + chans] = scale_row
    part_rows = keep_ref.shape[0]
    for place, target in ((KEEP, keep_ref), (NEAR, near_ref), (MATE, mate_ref), (FAR, far_ref)):
        start = pl.multiple_of(meta[place] * part_rows, 8)
        target[...] = packed_ref[pl.ds(start, part_rows), :].astype(bf16)


def finish_kernel(
    scale, meta, keep, near, mate, far, kernel_ref, gain_ref, up_ref, bias_ref, down_ref, scale_ref, packed_ref
):
    part_rows = keep.shape[0]
    for place, source in ((KEEP, keep), (NEAR, near), (MATE, mate), (FAR, far)):
        start = pl.multiple_of(meta[place] * part_rows, 8)
        packed_ref[pl.ds(start, part_rows), :] = source[...].astype(f32) * scale
    chans = up_ref.shape[1]
    base = 2 * chans
    up_ref[0] = packed_ref[:chans]
    down_ref[0] = packed_ref[chans:base]
    lane = lax.broadcasted_iota(jnp.int32, (PLACES, 128), 1) >> 4
    blocks = chans // BLOCK
    for tap_row in range(KS):
        halves = []
        for first in range(0, blocks, PLACES):
            half = jnp.zeros((PLACES, 128), f32)
            for block in range(first, min(first + PLACES, blocks)):
                rows = slice(base + block // 6 * 8, base + block // 6 * 8 + 8)
                part = packed_ref[rows, block % 6 * 128 : block % 6 * 128 + 128]
                shift = (block - first - tap_row) * BLOCK % 128
                if shift:
                    part = pltpu.roll(part, shift, 1)
                half = jnp.where(lane == block - first, part, half)
            halves.append(half)
        line = jnp.concatenate(halves, axis=1)
        for tap_col in range(KS):
            kernel_ref[tap_row * KS + tap_col] = line[tap_col : tap_col + 1, :chans]
    bias_ref[...] = packed_ref[base + 16 : base + 17]
    gain_ref[...] = packed_ref[base + 17 : base + 18, :chans]
    scale_ref[...] = packed_ref[base + 17 : base + 18, 256 : 256 + chans]


def added(*values):
    return sum(value.astype(f32) for value in values).astype(bf16)


def body(acts, cot_top, land, owners, dw_kernel, ln_gain, w_up, b_up, w_down, layer_scale):
    source = acts[0]
    count, chans, width = source.shape
    units = w_up.shape[2]
    cells = count * width
    tile_now = lax.axis_index("tile")
    section_now = lax.axis_index("section")
    scale = 1.0 / math.sqrt(lax.axis_size("tile") * cells)
    core, x, z = split_tile(tile_now)
    bit_x, bit_z = (x + 1) // 2 % 2, (z + 1) // 2 % 2
    bit = jnp.where(core == 0, bit_x, bit_z)
    mate_bit = jnp.where(core == 0, bit_z, bit_x)
    numbers = [
        section_now,
        core,
        2 * core + bit,
        2 * core + 1 - bit,
        2 * (1 - core) + mate_bit,
        2 * (1 - core) + 1 - mate_bit,
        tile_now * count,
        jnp.where((tile_now == 0) | (tile_now == TILES - 1), 0, 1),
    ]
    meta = jnp.concatenate([jnp.stack(numbers).astype(jnp.int32), land, owners])

    odd = core == 1
    head, tail = source[:MARGIN], source[count - MARGIN :]
    acts_inner, acts_outer = halo(jnp.where(odd, head, tail), jnp.where(odd, tail, head))
    up, down = w_up[0], w_down[0]
    swaps = [(section, section ^ 1) for section in range(SECTIONS)]
    taps_shape = shape((chans // BLOCK, KS * BLOCK, 256), bf16)
    weights_t = shape((units, chans), bf16)
    cols_shape = shape((chans, 64), f32)
    cols, forth, back, up_t, down_t, bias = call(
        prepare_kernel,
        (cols_shape, taps_shape, taps_shape, weights_t, weights_t, shape((units, 8), f32)),
        0,
        (dw_kernel[0], ln_gain, layer_scale, b_up, up, down),
        (pltpu.VMEM((64, chans), f32),),
        cost=(10**9, 10**7),
    )
    half = lax.ppermute(jnp.where(odd, down, up), "section", swaps)

    padded = pltpu.VMEM((count + PLACES - 1, chans, width), bf16)
    nhat_shape, inv_shape = shape((chans, cells), f32), shape((1, cells), f32)
    unit_shape = shape((units, cells), bf16)
    nhat, inv, hidden, slope, own_note = call(
        forward_kernel,
        (nhat_shape, inv_shape, unit_shape, unit_shape, shape((chans + BLOCK, units), bf16)),
        1,
        (meta, source, acts_inner, acts_outer, forth, cols, up_t, bias, b_up),
        (padded, pltpu.VMEM((chans, cells), f32), pltpu.VMEM((chans, cells), bf16)),
        cost=(3 * 10**9, 12 * 10**6),
    )
    note = lax.ppermute(own_note, "section", swaps)

    rows_shape = shape((count, chans, width), bf16)
    edge_shape = shape((MARGIN, chans, width), bf16)
    outgrads = pltpu.VMEM((chans, cells), bf16)
    lowgrads = pltpu.VMEM((units, cells), bf16)

    def turn_field(plane, cot, params):
        field_cols, field_down_t, field_up, field_slope, field_nhat, field_inv = params
        return call(
            functools.partial(turn_kernel, plane),
            (rows_shape, edge_shape, edge_shape),
            1,
            (meta, cot, field_cols, field_down_t, field_up, field_slope, field_nhat, field_inv),
            (outgrads, lowgrads),
            cost=(10**9, 6 * 10**6),
        )

    top = SECTIONS - 1
    field, inner, outer = turn_field(top, cot_top, (cols, down_t, up, slope, nhat, inv))
    half, field = lax.optimization_barrier((half, field))
    inner, outer = halo(inner, outer)
    other = moved(half, ("", ""), True)
    adopted = call(
        adopt_kernel,
        (nhat_shape, inv_shape, unit_shape, cols_shape, taps_shape, shape((chans, units), bf16))
        + (weights_t, weights_t, shape((units, 8), f32)),
        1,
        (meta, note, half, other),
        (pltpu.VMEM((chans, cells), bf16),),
        cost=(10**9, 10**7),
    )
    next_nhat, next_inv, next_slope, next_cols, next_back, next_up, next_down_t = adopted[:7]
    cot_2, field, inner, outer = call(
        functools.partial(middle_kernel, top),
        (rows_shape, rows_shape, edge_shape, edge_shape),
        1,
        (meta, field, outer, inner, cot_top, back, next_cols, next_down_t, next_up)
        + (next_slope, next_nhat, next_inv),
        (padded, outgrads, lowgrads),
    )
    own_2 = lax.ppermute(cot_2, "section", swaps)
    inner, outer = halo(inner, outer)
    cot_1 = call(
        functools.partial(conv_kernel, top),
        rows_shape,
        1,
        (meta, field, outer, inner, cot_2, next_back),
        (padded,),
    )
    cot_1 = lax.ppermute(cot_1, "section", [(0, top), (top, 0), (1, 2), (2, 1)])
    own_1 = lax.ppermute(cot_1, "section", swaps)

    adopted = (next_cols, next_down_t, next_up, next_slope, next_nhat, next_inv)
    field, inner, outer = turn_field(0, cot_1, adopted)
    inner, outer = halo(inner, outer)

    part = shape(((2 * chans + 32) // 4, units), bf16)
    cot_own, field, inner, outer, keep, near, mate, far = call(
        last_kernel,
        (rows_shape, rows_shape, edge_shape, edge_shape, part, part, part, part),
        1,
        (meta, cot_top, own_2, own_1, field, outer, inner, cot_1, next_back, cols, layer_scale, down_t, down, up, slope, nhat, inv, hidden)
        + (source, acts_inner, acts_outer),
        (
            outgrads,
            lowgrads,
            pltpu.VMEM((units, width), f32),
            pltpu.VMEM((chans, width), f32),
            padded,
            pltpu.VMEM((2 * chans + 32, units), f32),
        ),
    )
    far = moved(far, ("z0", "x0"), True)
    near = moved(near, ("x0", "z0"), False)
    mate = moved(mate, ("", ""), True)
    total = added(keep, near, mate, far)
    orders = (("x1", "z1"), ("z0", "z2"), ("z1", "x0"), ("z2", "x1"))
    total, outer = lax.optimization_barrier((total, outer))
    total = added(total, moved(total, orders[0], False))
    outer = across(outer)
    total, inner, outer = lax.optimization_barrier((total, inner, outer))
    total = added(total, moved(total, orders[1], False))
    inner = within(inner)
    total, inner = lax.optimization_barrier((total, inner))
    total = added(total, moved(total, orders[2], False))
    result, sent = call(
        last_conv_kernel,
        (rows_shape, shape((CAP, chans, width), bf16)),
        1,
        (meta, field, inner, outer, cot_own, back),
        (padded,),
    )
    total, result, sent = lax.optimization_barrier((total, result, sent))
    total = added(total, moved(total, orders[3], False))
    arrived = lax.ppermute(sent, "tile", [(tile, (tile + 1) % TILES) for tile in range(TILES)])
    total, arrived = lax.optimization_barrier((total, arrived))
    slotted = call(
        slots_kernel,
        shape((owners.shape[0], chans, width), bf16),
        1,
        (meta, result, arrived),
    )
    far = moved(total, ("x0", "z0"), True)
    near = moved(total, ("x0", "z0"), False)
    mate = moved(total, ("", ""), True)
    grads = call(
        functools.partial(finish_kernel, scale),
        (
            shape((KS * KS, 1, chans), f32),
            shape((1, chans), f32),
            shape((1, chans, units), f32),
            shape((1, units), f32),
            shape((1, chans, units), f32),
            shape((1, chans), f32),
        ),
        1,
        (meta, total, near, mate, far),
        (pltpu.VMEM((2 * chans + 32, units), f32),),
    )

    grad_kernel, grad_gain, grad_up, grad_bias, grad_down, grad_scale = grads
    return (
        slotted[None],
        jnp.transpose(grad_kernel, (1, 0, 2)),
        grad_gain,
        grad_up,
        grad_bias,
        grad_down,
        grad_scale,
    )


def solution(mesh):
    in_specs = (
        P("section", "tile", None, None),
        P("tile", None, None),
        P("tile"),
        P("tile"),
        P("section", None, None),
        P("section", None),
        P("section", None, None),
        P("section", None),
        P("section", None, None),
        P("section", None),
    )
    out_specs = (
        P("section", "tile", None, None),
        P("section", None, None),
        P("section", None),
        P("section", None, None),
        P("section", None),
        P("section", None, None),
        P("section", None),
    )
    return jax.shard_map(body, mesh=mesh, in_specs=in_specs, out_specs=out_specs, check_vma=False)
```

```python
import functools
import math

import jax
import jax.numpy as jnp
from jax import lax
from jax.experimental import pallas as pl
from jax.experimental.pallas import tpu as pltpu
from jax.sharding import PartitionSpec as P

KS = 7
CAP = 2
SECTIONS = 4
TILES = 64
MARGIN = 3
BLOCK = 16
UNROLL = 12

norm_eps = 1e-06
tanh_root = math.sqrt(2.0 / math.pi)
cubic_coef = 0.044715

f32 = jnp.float32
bf16 = jnp.bfloat16

SECTION, ODD, KEEP, NEAR, MATE, FAR, OFFSET, INSIDE, LAND = range(9)
PLACES = 8
OWNERS = LAND + 5


def split_tile(tile):
    return tile % 2, tile // 2 % 4, tile // 8


def flip_x0(x):
    return x ^ 1


def flip_x1(x):
    return 3 - x


def flip_z0(z):
    return z ^ 1


def flip_z1(z):
    return 3 - z if z < 4 else 11 - z


def flip_z2(z):
    return 7 - z


flips = {"x0": flip_x0, "x1": flip_x1, "z0": flip_z0, "z1": flip_z1, "z2": flip_z2}


def moved(value, dims, swap):
    pairs = []
    for tile in range(TILES):
        core, x, z = split_tile(tile)
        dim = dims[core]
        if dim in ("x0", "x1"):
            x = flips[dim](x)
        elif dim:
            z = flips[dim](z)
        core = 1 - core if swap else core
        pairs.append((tile, z * 8 + x * 2 + core))
    return lax.ppermute(value, "tile", pairs)


def within(value):
    return lax.ppermute(value, "tile", [(tile, tile ^ 1) for tile in range(TILES)])


def across(value):
    pairs = [(tile, (tile + 1 if tile % 2 else tile - 1) % TILES) for tile in range(TILES)]
    return lax.ppermute(value, "tile", pairs)


def halo(inner, outer):
    inner = within(inner)
    return inner, across(outer)


def call(body, out_shape, smem, operands, scratch=(), cost=(0, 0)):
    spec = [pl.BlockSpec(memory_space=pltpu.SMEM)] * smem
    spec += [pl.BlockSpec(memory_space=pltpu.VMEM)] * (len(operands) - smem)
    outs = jax.tree.map(lambda _: pl.BlockSpec(memory_space=pltpu.VMEM), out_shape)
    return pl.pallas_call(
        body,
        out_shape=out_shape,
        in_specs=spec,
        out_specs=outs,
        scratch_shapes=list(scratch),
        compiler_params=pltpu.CompilerParams(vmem_limit_bytes=32 * 1024 * 1024),
        cost_estimate=pl.CostEstimate(flops=cost[0], bytes_accessed=cost[1], transcendentals=0),
    )(*operands)


def shape(dims, dtype):
    return jax.ShapeDtypeStruct(dims, dtype)


def fill_rows(rows_ref, meta, own, inner, outer):
    count = own.shape[0]
    odd = meta[ODD] == 1
    far_rows = jnp.where(meta[INSIDE] == 1, outer[...], jnp.zeros_like(outer))
    near_rows = inner[...]
    rows_ref[MARGIN : MARGIN + count] = own[...]
    rows_ref[:MARGIN] = jnp.where(odd, near_rows, far_rows)
    rows_ref[MARGIN + count : 2 * MARGIN + count] = jnp.where(odd, far_rows, near_rows)
    rows_ref[2 * MARGIN + count :] = jnp.zeros((1,) + own.shape[1:], bf16)


def edges(odd, value_ref, inner_ref, outer_ref):
    count = value_ref.shape[0]
    head = value_ref[:MARGIN]
    tail = value_ref[count - MARGIN :]
    inner_ref[...] = jnp.where(odd, head, tail)
    outer_ref[...] = jnp.where(odd, tail, head)


def fill_taps(cols, targets):
    high = cols[...].astype(bf16)
    low = (cols[...] - high.astype(f32)).astype(bf16)
    chans, taps = cols.shape
    wide = KS * 128
    tap = lax.broadcasted_iota(jnp.int32, (taps, wide), 0)
    place = lax.broadcasted_iota(jnp.int32, (taps, wide), 1)
    tap_col, tap_row = place >> 7, (place >> 4) & (PLACES - 1)
    own = lax.broadcasted_iota(jnp.int32, (chans, wide), 0) & (BLOCK - 1)
    diagonal = own == (lax.broadcasted_iota(jnp.int32, (chans, wide), 1) & (BLOCK - 1))
    for target, row in zip(targets, (tap_row, KS - 1 - tap_row)):
        if target is None:
            continue
        hit = (tap == row * KS + tap_col) & (tap_row < KS)
        spread = jnp.where(hit, 1.0, 0.0).astype(bf16)
        for half, value in enumerate((high, low)):
            filled = jnp.dot(value, spread, preferred_element_type=f32)
            filled = jnp.where(diagonal, filled, 0.0).astype(bf16)
            for block in range(chans // BLOCK):
                for col in range(KS):
                    target[
                        block, col * BLOCK : (col + 1) * BLOCK, half * 128 : (half + 1) * 128
                    ] = filled[block * BLOCK : (block + 1) * BLOCK, col * 128 : (col + 1) * 128]


def prepare_kernel(
    kernel, gain, layer, bias, up, down, cols, forth_ref, back_ref, up_t_ref, down_t_ref, bias_ref, lines_ref
):
    lines_ref[...] = jnp.zeros_like(lines_ref)
    lines_ref[: KS * KS] = kernel[...]
    lines_ref[KS * KS : KS * KS + 1] = gain[...]
    lines_ref[KS * KS + 1 : KS * KS + 2] = layer[...]
    cols[...] = jnp.transpose(lines_ref[...])
    up_t_ref[...] = jnp.transpose(up[...].astype(f32)).astype(bf16)
    down_t_ref[...] = jnp.transpose(down[...].astype(f32)).astype(bf16)
    bias_ref[...] = jnp.transpose(jnp.broadcast_to(bias[...], (8, bias.shape[1])))
    fill_taps(cols, (forth_ref, back_ref))


def stacked(rows_ref, start, count):
    rows = [rows_ref[row, pl.ds(start, BLOCK), :] for row in range(count + PLACES - 1)]
    return jnp.concatenate(
        [jnp.concatenate(rows[place : place + count], axis=1) for place in range(PLACES)], axis=0
    )


def taps_sum(rows_ref, taps_mat, block, count, backward):
    windows = stacked(rows_ref, pl.multiple_of(block * BLOCK, BLOCK), count)
    parts = jnp.dot(
        taps_mat[block], jnp.concatenate([windows, windows], axis=0), preferred_element_type=f32
    )
    sums = []
    for row in range(count):
        total = None
        for tap_col in range(KS):
            shift = (tap_col - MARGIN if backward else MARGIN - tap_col) % 128
            part = parts[tap_col * BLOCK : (tap_col + 1) * BLOCK, row * 128 : (row + 1) * 128]
            if shift:
                part = pltpu.roll(part, shift, 1)
            total = part if total is None else total + part
        sums.append(total)
    return sums


def forward_kernel(
    meta, acts, inner, outer, taps_mat, cols, up_t, bias, bias_row, nhat_ref, inv_ref, hidden_ref, slope_ref, note_ref, rows_ref, field_ref, normed_ref
):
    count, chans, width = acts.shape
    fill_rows(rows_ref, meta, acts, inner, outer)

    def step(index, carry):
        start = pl.multiple_of(index * BLOCK, BLOCK)
        sums = taps_sum(rows_ref, taps_mat, index, count, False)
        for row in range(count):
            field_ref[pl.ds(start, BLOCK), row * width : (row + 1) * width] = sums[row]
        return carry

    lax.fori_loop(0, chans // BLOCK, step, 0, unroll=UNROLL)
    gain = cols[:, KS * KS : KS * KS + 1]
    for row in range(count):
        part = slice(row * width, (row + 1) * width)
        field = field_ref[:, part]
        center = field - jnp.mean(field, axis=0, keepdims=True)
        inverse = 1.0 / jnp.sqrt(jnp.mean(center * center, axis=0, keepdims=True) + norm_eps)
        nhat = center * inverse
        nhat_ref[:, part] = nhat
        inv_ref[:, part] = inverse
        normed_ref[:, part] = (nhat * gain).astype(bf16)
    cells = count * width
    note_ref[:chans, :cells] = nhat_ref[...].astype(bf16)
    high, low = two_parts(cols[...])
    note_ref[:chans, cells:] = jnp.concatenate([high, low], axis=1).astype(bf16)
    parts = two_parts(bias_row[...])
    padding = jnp.zeros((1, bias_row.shape[1] - cells), f32)
    parts += two_parts(jnp.concatenate([inv_ref[...], padding], axis=1))
    rest = jnp.zeros((BLOCK - len(parts), bias_row.shape[1]), f32)
    note_ref[chans:] = jnp.concatenate([*parts, rest]).astype(bf16)
    mlp_forward(normed_ref, up_t, bias, hidden_ref, slope_ref)


def two_parts(value):
    high = value.astype(bf16).astype(f32)
    return [high, value - high]


def mlp_forward(normed_ref, up_t, bias, hidden_ref, slope_ref):
    units = up_t.shape[0]
    chunk = 128
    for first in range(0, units, chunk):
        part = slice(first, first + chunk)
        preact = jnp.dot(up_t[part], normed_ref[...], preferred_element_type=f32) + bias[part, :1]
        square = preact * preact
        hyper = jnp.tanh(preact * (tanh_root + tanh_root * cubic_coef * square))
        half = 0.5 + 0.5 * hyper
        if hidden_ref is not None:
            hidden_ref[part] = (preact * half).astype(bf16)
        slope = half * (
            1.0 + preact * (1.0 - hyper) * (tanh_root + 3.0 * cubic_coef * tanh_root * square)
        )
        slope_ref[part] = slope.astype(bf16)


def adopt_kernel(
    meta, note, half, other, nhat_ref, inv_ref, slope_ref, cols_ref, back_ref, up_ref, down_t_ref, up_t_ref, bias_ref, normed_ref
):
    chans, cells = nhat_ref.shape
    units = slope_ref.shape[0]
    taps = cols_ref.shape[1]

    @pl.when((meta[SECTION] == SECTIONS - 1) | (meta[SECTION] == 0))
    def _():
        odd = meta[ODD] == 1
        up = jnp.where(odd, other[...], half[...])
        up_ref[...] = up
        up_t_ref[...] = jnp.transpose(up.astype(f32)).astype(bf16)
        down = jnp.where(odd, half[...], other[...])
        down_t_ref[...] = jnp.transpose(down.astype(f32)).astype(bf16)
        nhat = note[:chans, :cells].astype(f32)
        nhat_ref[...] = nhat
        pieces = note[:chans, cells:].astype(f32)
        cols_ref[...] = pieces[:, :taps] + pieces[:, taps:]
        lines = note[chans:].astype(f32)
        bias_row = lines[0:1] + lines[1:2]
        inv_ref[...] = (lines[2:3] + lines[3:4])[:, :cells]
        bias_ref[...] = jnp.transpose(jnp.broadcast_to(bias_row, (8, units)))
        fill_taps(cols_ref, (None, back_ref))
        normed_ref[...] = (nhat * cols_ref[:, KS * KS : KS * KS + 1]).astype(bf16)
        mlp_forward(normed_ref, up_t_ref, bias_ref, None, slope_ref)


def mlp_backward(cots, meta, cols, down_t, up, slope, nhat, inv, out_ref, low_ref, field_ref, sums=None):
    width = cots[0].shape[1]
    count = len(cots)
    gain = cols[:, KS * KS : KS * KS + 1]
    layer = cols[:, KS * KS + 1 : KS * KS + 2]
    for row in range(count):
        wet = meta[LAND + row].astype(f32)
        out_ref[:, row * width : (row + 1) * width] = (cots[row] * layer * wet).astype(bf16)
    units = down_t.shape[0]
    chunk = 128
    for first in range(0, units, chunk):
        part = slice(first, first + chunk)
        pregrad = jnp.dot(down_t[part], out_ref[...], preferred_element_type=f32)
        pregrad = pregrad * slope[part].astype(f32)
        low_ref[part] = pregrad.astype(bf16)
        if sums is not None:
            sums[0][part] = sum(
                pregrad[:, row * width : (row + 1) * width] for row in range(count)
            )
    featgrad = jnp.dot(up[...], low_ref[...], preferred_element_type=f32)
    gains = None
    for row in range(count):
        part = slice(row * width, (row + 1) * width)
        feat = featgrad[:, part]
        own = nhat[:, part]
        scaled = feat * gain
        mean = jnp.mean(scaled, axis=0, keepdims=True)
        cross = jnp.mean(scaled * own, axis=0, keepdims=True)
        field_ref[row] = (inv[:, part] * (scaled - mean - own * cross)).astype(bf16)
        if sums is not None:
            term = feat * own
            gains = term if gains is None else gains + term
    if sums is not None:
        sums[1][...] = gains


def turn_kernel(
    section, meta, cot, cols, down_t, up, slope, nhat, inv, field_ref, inner_ref, outer_ref, out_ref, low_ref
):
    @pl.when(meta[SECTION] == section)
    def _():
        cots = [cot[row].astype(f32) for row in range(cot.shape[0])]
        mlp_backward(cots, meta, cols, down_t, up, slope, nhat, inv, out_ref, low_ref, field_ref)
        edges(meta[ODD] == 1, field_ref, inner_ref, outer_ref)


def conv_rows(meta, field, inner, outer, cot, taps_mat, result_ref, rows_ref):
    count, chans, width = field.shape
    fill_rows(rows_ref, meta, field, inner, outer)

    def step(index, carry):
        start = pl.multiple_of(index * BLOCK, BLOCK)
        sums = taps_sum(rows_ref, taps_mat, index, count, True)
        for row in range(count):
            own = cot[row, pl.ds(start, BLOCK), :].astype(f32)
            result_ref[row, pl.ds(start, BLOCK), :] = (own + sums[row]).astype(bf16)
        return carry

    lax.fori_loop(0, chans // BLOCK, step, 0, unroll=UNROLL)


def conv_kernel(section, meta, field, outer, inner, cot, taps_mat, result_ref, rows_ref):
    @pl.when(meta[SECTION] == section)
    def _():
        conv_rows(meta, field, inner, outer, cot, taps_mat, result_ref, rows_ref)


def middle_kernel(
    plane,
    meta,
    field,
    outer,
    inner,
    cot,
    taps_mat,
    cols,
    down_t,
    up,
    slope,
    nhat,
    inv,
    result_ref,
    field_ref,
    inner_ref,
    outer_ref,
    rows_ref,
    out_ref,
    low_ref,
):
    @pl.when(meta[SECTION] == plane)
    def _():
        conv_rows(meta, field, inner, outer, cot, taps_mat, result_ref, rows_ref)
        cots = [result_ref[row].astype(f32) for row in range(result_ref.shape[0])]
        mlp_backward(cots, meta, cols, down_t, up, slope, nhat, inv, out_ref, low_ref, field_ref)
        edges(meta[ODD] == 1, field_ref, inner_ref, outer_ref)


def last_conv_kernel(meta, field, inner, outer, cot, taps_mat, result_ref, sent_ref, rows_ref):
    conv_rows(meta, field, inner, outer, cot, taps_mat, result_ref, rows_ref)
    sent_ref[...] = jnp.zeros_like(sent_ref)
    rank = jnp.int32(0)
    for local in range(result_ref.shape[0]):
        kept = jnp.bool_(False)
        for slot in range(OWNERS, meta.shape[0]):
            kept = kept | (meta[slot] == meta[OFFSET] + local)
        sent = (meta[LAND + local] == 1) & jnp.logical_not(kept)
        for place in range(CAP):

            @pl.when(sent & (rank == place))
            def _():
                sent_ref[place] = result_ref[local]

        rank = rank + sent.astype(jnp.int32)


def slots_kernel(meta, result, arrived, slots_ref):
    for slot in range(slots_ref.shape[0]):
        slots_ref[slot] = arrived[min(slot, CAP - 1)]
        for local in range(result.shape[0]):

            @pl.when(meta[OWNERS + slot] == meta[OFFSET] + local)
            def _():
                slots_ref[slot] = result[local]


def last_kernel(
    meta,
    cot_top,
    cot_2,
    cot_1,
    turn_field,
    turn_outer,
    turn_inner,
    turn_cot,
    turn_mat,
    cols,
    layer_row,
    down_t,
    down,
    up,
    slope,
    nhat,
    inv,
    hidden,
    acts,
    inner,
    outer,
    cot_ref,
    field_ref,
    field_inner_ref,
    field_outer_ref,
    keep_ref,
    near_ref,
    mate_ref,
    far_ref,
    out_ref,
    low_ref,
    bias_ref,
    gain_ref,
    rows_ref,
    packed_ref,
):
    count, chans, width = acts.shape
    units = slope.shape[0]
    odd = meta[ODD] == 1
    for section, cot in ((3, cot_top), (2, cot_2), (1, cot_1)):

        @pl.when(meta[SECTION] == section)
        def _():
            cot_ref[...] = cot[...]

    @pl.when(meta[SECTION] == 0)
    def _():
        conv_rows(meta, turn_field, turn_inner, turn_outer, turn_cot, turn_mat, cot_ref, rows_ref)

    cots = [cot_ref[row].astype(f32) for row in range(count)]
    mlp_backward(
        cots, meta, cols, down_t, up, slope, nhat, inv, out_ref, low_ref, field_ref, (bias_ref, gain_ref)
    )
    edges(odd, field_ref, field_inner_ref, field_outer_ref)
    gain = cols[:, KS * KS : KS * KS + 1]
    normed = (nhat[...] * gain).astype(bf16)
    turned = (((1,), (1,)), ((), ()))
    grad_up = lax.dot_general(normed, low_ref[...], turned, preferred_element_type=f32)
    packed_ref[:chans] = grad_up
    grad_down = lax.dot_general(out_ref[...], hidden[...], turned, preferred_element_type=f32)
    packed_ref[chans : 2 * chans] = grad_down
    product = grad_down * down[...].astype(f32)
    product = sum(product[:, first : first + 128] for first in range(0, units, 128))

    fill_rows(rows_ref, meta, acts, inner, outer)
    base = 2 * chans
    shifts = [(tap_col - MARGIN) % 128 for tap_col in range(KS)]
    own = lax.broadcasted_iota(jnp.int32, (BLOCK, 128), 0)
    diagonal = own == (lax.broadcasted_iota(jnp.int32, (BLOCK, 128), 1) & (BLOCK - 1))
    for block in range(chans // BLOCK):
        start = block * BLOCK
        windows = stacked(rows_ref, start, count)
        fields = [field_ref[row, start : start + BLOCK, :].astype(f32) for row in range(count)]
        rolled = jnp.concatenate(
            [
                jnp.concatenate(
                    [pltpu.roll(field, shift, 1) if shift else field for field in fields], axis=1
                )
                for shift in shifts
            ],
            axis=0,
        ).astype(bf16)
        crossed = lax.dot_general(rolled, windows, turned, preferred_element_type=f32)
        first = base + block // 6 * 8
        lanes = slice(block % 6 * 128, block % 6 * 128 + 128)
        for tap_col in range(KS):
            part = jnp.where(diagonal, crossed[tap_col * BLOCK : (tap_col + 1) * BLOCK], 0.0)
            packed_ref[first + tap_col : first + tap_col + 1, lanes] = jnp.sum(
                part, axis=0, keepdims=True
            )
        packed_ref[first + KS : first + PLACES, lanes] = jnp.zeros((1, 128), f32)
    bias_row = jnp.sum(jnp.transpose(bias_ref[...]), axis=0, keepdims=True)
    gain_row = jnp.sum(jnp.transpose(gain_ref[...]), axis=0, keepdims=True)
    scale_row = jnp.sum(jnp.transpose(product), axis=0, keepdims=True) / layer_row[...]
    packed_ref[base + 16 :] = jnp.zeros((packed_ref.shape[0] - base - 16, units), f32)
    packed_ref[base + 16 : base + 17] = bias_row
    packed_ref[base + 17 : base + 18, :chans] = gain_row
    packed_ref[base + 17 : base + 18, 256 : 256 + chans] = scale_row
    part_rows = keep_ref.shape[0]
    for place, target in ((KEEP, keep_ref), (NEAR, near_ref), (MATE, mate_ref), (FAR, far_ref)):
        start = pl.multiple_of(meta[place] * part_rows, 8)
        target[...] = packed_ref[pl.ds(start, part_rows), :].astype(bf16)


def finish_kernel(
    scale, meta, keep, near, mate, far, kernel_ref, gain_ref, up_ref, bias_ref, down_ref, scale_ref, packed_ref
):
    part_rows = keep.shape[0]
    for place, source in ((KEEP, keep), (NEAR, near), (MATE, mate), (FAR, far)):
        start = pl.multiple_of(meta[place] * part_rows, 8)
        packed_ref[pl.ds(start, part_rows), :] = source[...].astype(f32) * scale
    chans = up_ref.shape[1]
    base = 2 * chans
    up_ref[0] = packed_ref[:chans]
    down_ref[0] = packed_ref[chans:base]
    lane = lax.broadcasted_iota(jnp.int32, (PLACES, 128), 1) >> 4
    blocks = chans // BLOCK
    for tap_row in range(KS):
        halves = []
        for first in range(0, blocks, PLACES):
            half = jnp.zeros((PLACES, 128), f32)
            for block in range(first, min(first + PLACES, blocks)):
                rows = slice(base + block // 6 * 8, base + block // 6 * 8 + 8)
                part = packed_ref[rows, block % 6 * 128 : block % 6 * 128 + 128]
                shift = (block - first - tap_row) * BLOCK % 128
                if shift:
                    part = pltpu.roll(part, shift, 1)
                half = jnp.where(lane == block - first, part, half)
            halves.append(half)
        line = jnp.concatenate(halves, axis=1)
        for tap_col in range(KS):
            kernel_ref[tap_row * KS + tap_col] = line[tap_col : tap_col + 1, :chans]
    bias_ref[...] = packed_ref[base + 16 : base + 17]
    gain_ref[...] = packed_ref[base + 17 : base + 18, :chans]
    scale_ref[...] = packed_ref[base + 17 : base + 18, 256 : 256 + chans]


def added(*values):
    return sum(value.astype(f32) for value in values).astype(bf16)


def body(acts, cot_top, land, owners, dw_kernel, ln_gain, w_up, b_up, w_down, layer_scale):
    source = acts[0]
    count, chans, width = source.shape
    units = w_up.shape[2]
    cells = count * width
    tile_now = lax.axis_index("tile")
    section_now = lax.axis_index("section")
    scale = 1.0 / math.sqrt(lax.axis_size("tile") * cells)
    core, x, z = split_tile(tile_now)
    bit_x, bit_z = (x + 1) // 2 % 2, (z + 1) // 2 % 2
    bit = jnp.where(core == 0, bit_x, bit_z)
    mate_bit = jnp.where(core == 0, bit_z, bit_x)
    numbers = [
        section_now,
        core,
        2 * core + bit,
        2 * core + 1 - bit,
        2 * (1 - core) + mate_bit,
        2 * (1 - core) + 1 - mate_bit,
        tile_now * count,
        jnp.where((tile_now == 0) | (tile_now == TILES - 1), 0, 1),
    ]
    meta = jnp.concatenate([jnp.stack(numbers).astype(jnp.int32), land, owners])

    odd = core == 1
    head, tail = source[:MARGIN], source[count - MARGIN :]
    acts_inner, acts_outer = halo(jnp.where(odd, head, tail), jnp.where(odd, tail, head))
    up, down = w_up[0], w_down[0]
    swaps = [(section, section ^ 1) for section in range(SECTIONS)]
    taps_shape = shape((chans // BLOCK, KS * BLOCK, 256), bf16)
    weights_t = shape((units, chans), bf16)
    cols_shape = shape((chans, 64), f32)
    cols, forth, back, up_t, down_t, bias = call(
        prepare_kernel,
        (cols_shape, taps_shape, taps_shape, weights_t, weights_t, shape((units, 8), f32)),
        0,
        (dw_kernel[0], ln_gain, layer_scale, b_up, up, down),
        (pltpu.VMEM((64, chans), f32),),
        cost=(10**9, 10**7),
    )
    half = lax.ppermute(jnp.where(odd, down, up), "section", swaps)

    padded = pltpu.VMEM((count + PLACES - 1, chans, width), bf16)
    nhat_shape, inv_shape = shape((chans, cells), f32), shape((1, cells), f32)
    unit_shape = shape((units, cells), bf16)
    nhat, inv, hidden, slope, own_note = call(
        forward_kernel,
        (nhat_shape, inv_shape, unit_shape, unit_shape, shape((chans + BLOCK, units), bf16)),
        1,
        (meta, source, acts_inner, acts_outer, forth, cols, up_t, bias, b_up),
        (padded, pltpu.VMEM((chans, cells), f32), pltpu.VMEM((chans, cells), bf16)),
        cost=(3 * 10**9, 12 * 10**6),
    )
    note = lax.ppermute(own_note, "section", swaps)

    rows_shape = shape((count, chans, width), bf16)
    edge_shape = shape((MARGIN, chans, width), bf16)
    outgrads = pltpu.VMEM((chans, cells), bf16)
    lowgrads = pltpu.VMEM((units, cells), bf16)

    def turn_field(plane, cot, params):
        field_cols, field_down_t, field_up, field_slope, field_nhat, field_inv = params
        return call(
            functools.partial(turn_kernel, plane),
            (rows_shape, edge_shape, edge_shape),
            1,
            (meta, cot, field_cols, field_down_t, field_up, field_slope, field_nhat, field_inv),
            (outgrads, lowgrads),
            cost=(10**9, 6 * 10**6),
        )

    top = SECTIONS - 1
    field, inner, outer = turn_field(top, cot_top, (cols, down_t, up, slope, nhat, inv))
    half, field = lax.optimization_barrier((half, field))
    inner, outer = halo(inner, outer)
    other = moved(half, ("", ""), True)
    adopted = call(
        adopt_kernel,
        (nhat_shape, inv_shape, unit_shape, cols_shape, taps_shape, shape((chans, units), bf16))
        + (weights_t, weights_t, shape((units, 8), f32)),
        1,
        (meta, note, half, other),
        (pltpu.VMEM((chans, cells), bf16),),
        cost=(10**9, 10**7),
    )
    next_nhat, next_inv, next_slope, next_cols, next_back, next_up, next_down_t = adopted[:7]
    cot_2, field, inner, outer = call(
        functools.partial(middle_kernel, top),
        (rows_shape, rows_shape, edge_shape, edge_shape),
        1,
        (meta, field, outer, inner, cot_top, back, next_cols, next_down_t, next_up)
        + (next_slope, next_nhat, next_inv),
        (padded, outgrads, lowgrads),
    )
    own_2 = lax.ppermute(cot_2, "section", swaps)
    inner, outer = halo(inner, outer)
    cot_1 = call(
        functools.partial(conv_kernel, top),
        rows_shape,
        1,
        (meta, field, outer, inner, cot_2, next_back),
        (padded,),
    )
    cot_1 = lax.ppermute(cot_1, "section", [(0, top), (top, 0), (1, 2), (2, 1)])
    own_1 = lax.ppermute(cot_1, "section", swaps)

    adopted = (next_cols, next_down_t, next_up, next_slope, next_nhat, next_inv)
    field, inner, outer = turn_field(0, cot_1, adopted)
    inner, outer = halo(inner, outer)

    part = shape(((2 * chans + 32) // 4, units), bf16)
    cot_own, field, inner, outer, keep, near, mate, far = call(
        last_kernel,
        (rows_shape, rows_shape, edge_shape, edge_shape, part, part, part, part),
        1,
        (meta, cot_top, own_2, own_1, field, outer, inner, cot_1, next_back, cols, layer_scale, down_t, down, up, slope, nhat, inv, hidden)
        + (source, acts_inner, acts_outer),
        (
            outgrads,
            lowgrads,
            pltpu.VMEM((units, width), f32),
            pltpu.VMEM((chans, width), f32),
            padded,
            pltpu.VMEM((2 * chans + 32, units), f32),
        ),
    )
    far = moved(far, ("z0", "x0"), True)
    near = moved(near, ("x0", "z0"), False)
    mate = moved(mate, ("", ""), True)
    total = added(keep, near, mate, far)
    orders = (("x1", "z1"), ("z0", "z2"), ("z1", "x0"), ("z2", "x1"))
    total, outer = lax.optimization_barrier((total, outer))
    total = added(total, moved(total, orders[0], False))
    outer = across(outer)
    total, inner, outer = lax.optimization_barrier((total, inner, outer))
    total = added(total, moved(total, orders[1], False))
    inner = within(inner)
    total, inner = lax.optimization_barrier((total, inner))
    total = added(total, moved(total, orders[2], False))
    result, sent = call(
        last_conv_kernel,
        (rows_shape, shape((CAP, chans, width), bf16)),
        1,
        (meta, field, inner, outer, cot_own, back),
        (padded,),
    )
    total, result, sent = lax.optimization_barrier((total, result, sent))
    total = added(total, moved(total, orders[3], False))
    arrived = lax.ppermute(sent, "tile", [(tile, (tile + 1) % TILES) for tile in range(TILES)])
    slotted = call(
        slots_kernel,
        shape((owners.shape[0], chans, width), bf16),
        1,
        (meta, result, arrived),
    )
    far = moved(total, ("x0", "z0"), True)
    near = moved(total, ("x0", "z0"), False)
    mate = moved(total, ("", ""), True)
    grads = call(
        functools.partial(finish_kernel, scale),
        (
            shape((KS * KS, 1, chans), f32),
            shape((1, chans), f32),
            shape((1, chans, units), f32),
            shape((1, units), f32),
            shape((1, chans, units), f32),
            shape((1, chans), f32),
        ),
        1,
        (meta, total, near, mate, far),
        (pltpu.VMEM((2 * chans + 32, units), f32),),
    )

    grad_kernel, grad_gain, grad_up, grad_bias, grad_down, grad_scale = grads
    return (
        slotted[None],
        jnp.transpose(grad_kernel, (1, 0, 2)),
        grad_gain,
        grad_up,
        grad_bias,
        grad_down,
        grad_scale,
    )


def solution(mesh):
    in_specs = (
        P("section", "tile", None, None),
        P("tile", None, None),
        P("tile"),
        P("tile"),
        P("section", None, None),
        P("section", None),
        P("section", None, None),
        P("section", None),
        P("section", None, None),
        P("section", None),
    )
    out_specs = (
        P("section", "tile", None, None),
        P("section", None, None),
        P("section", None),
        P("section", None, None),
        P("section", None),
        P("section", None, None),
        P("section", None),
    )
    return jax.shard_map(body, mesh=mesh, in_specs=in_specs, out_specs=out_specs, check_vma=False)
```
